32 devices in a mesh: dp: 8 (over z, x), fsdp: 4 (over y, core).
Axes of the slice: x: 2, y: 2, z: 4, core: 2. Of those that a mesh axis runs over, the one named last changes fastest.
Arguments:
- tokens: bfloat16 [16384, 1024], P(('dp', 'fsdp')), may hold values from -6 to 6
- cotangent: bfloat16 [16384, 1024], P(('dp', 'fsdp')), may hold values from -6 to 6
- prot_lens: int32 [32, 8], P(('dp', 'fsdp')), may hold values from 0 to 512, as said below
- clus_start: int32 [32, 8], P(('dp', 'fsdp')), may hold values 0 or 1
- norm_gain: bfloat16 [1024], P('fsdp'), may hold values from 0.5 to 1.5
- in_w: bfloat16 [1024, 4096], P('fsdp'), may hold values from -0.1875 to 0.1875
- conv_w: bfloat16 [4, 2048], P(None, 'fsdp'), may hold values from -3 to 3
- conv_b: bfloat16 [2048], P('fsdp'), may hold values from -3 to 3
- xproj_w: bfloat16 [2048, 96], P('fsdp'), may hold values from -0.125 to 0.125
- dtproj_w: bfloat16 [64, 2048], P(None, 'fsdp'), may hold values from -0.75 to 0.75
- dt_bias: bfloat16 [2048], P('fsdp'), may hold values from -6.875 to -2.296875
- a_log: bfloat16 [16, 2048], P(None, 'fsdp'), may hold values from 0 to 2.765625
- d_skip: bfloat16 [2048], P('fsdp'), may hold values from 0.5 to 1.5
- out_w: bfloat16 [2048, 1024], P('fsdp'), may hold values from -0.25 to 0.25
Outputs:
- mixed: bfloat16 [16384, 1024], P(('dp', 'fsdp'))
- token_grad: float32 [16384, 1024], P(('dp', 'fsdp'))
- gain_grad: float32 [1024], P('fsdp')
- in_grad: float32 [1024, 4096], P('fsdp')
- conv_grad: float32 [4, 2048], P(None, 'fsdp')
- conv_bias_grad: float32 [2048], P('fsdp')
- xproj_grad: float32 [2048, 96], P('fsdp')
- dtproj_grad: float32 [64, 2048], P(None, 'fsdp')
- dt_bias_grad: float32 [2048], P('fsdp')
- a_log_grad: float32 [16, 2048], P(None, 'fsdp')
- skip_grad: float32 [2048], P('fsdp')
- out_grad: float32 [2048, 1024], P('fsdp')
The draws below stay inside these ranges and needn't reach their ends.
Inputs may be any that keep to these rules, and one draw needn't show every extreme that they name: `prot_lens`: each row lists the lengths of the proteins in one buffer, in order, then zeros; a protein has 50 to 512 residues, a row sums to at most 512, and some buffer holds a single protein of 512 residues. `clus_start`: row r marks which protein slots of buffer r begin a new cluster; a cluster runs on over the following proteins of the buffer until the next mark.
All inputs are finite; a program needn't handle non-finite values. No bound on the sum of `clus_start` on one device may be relied on, other than what follows from the above.
Results may differ from the reference program's by a relative error of at most 0.011.
Values may be sent and summed in bfloat16 or wider, within the bound.
A program may use at most 320 MiB of HBM per device.

```python
import jax
import jax.numpy as jnp
from jax import lax

D = 1024
DI = 2048
NST = 16
DCONV = 4
RANK = 64
CAP = 512
SLOTS = 8
MINLEN = 50
QLEN = 16
BUFFERS = 32
TOKENS = 16384


def draw_prot_lens(key, part):
    key = jax.random.fold_in(key, 11)
    first_key, second_key = jax.random.split(key)
    raw = jax.random.randint(first_key, (BUFFERS, SLOTS), 0, 1024)
    cubed = raw * raw // 1024 * raw // 1024
    lengths = MINLEN + (CAP - MINLEN) * cubed // 1021
    chosen = jax.random.randint(second_key, (), 0, BUFFERS)
    row_index = jnp.arange(BUFFERS, dtype=jnp.int32)[:, None]
    col_index = jnp.arange(SLOTS, dtype=jnp.int32)[None, :]
    lengths = jnp.where((row_index == chosen) & (col_index == 0), CAP, lengths)
    running = jnp.cumsum(lengths, axis=1)
    return jnp.where(running <= CAP, lengths, 0).astype(jnp.int32)


def touch_ends(entries, own_key, low, top_value):
    spot = [jax.random.randint(jax.random.fold_in(own_key, axis), (), 0, length) for axis, length in enumerate(entries.shape)]
    widest = entries.shape.index(max(entries.shape))
    beside = spot[:widest] + [(spot[widest] + 1) % entries.shape[widest]] + spot[widest + 1:]
    return entries.at[tuple(spot)].set(low).at[tuple(beside)].set(top_value)


def block_levels(rng, extent, cuts, low, top_value):
    level = 1.0
    for dim, parts in cuts:
        heights = jax.random.uniform(jax.random.fold_in(jax.random.fold_in(rng, 6), dim), (parts,), jnp.float32, low / len(cuts), top_value / len(cuts))
        level = level * jnp.repeat(jnp.exp(heights), extent[dim] // parts).reshape((-1,) + (1,) * (len(extent) - 1 - dim))
    return level


def bell_draw(stream_key, dims, deviation, reach, cuts=(), held_as=jnp.bfloat16):
    loudness = block_levels(stream_key, dims, cuts, -0.22, 0.18) if cuts else 1.0
    array = jax.random.normal(stream_key, dims, jnp.float32) * deviation * loudness
    return jnp.minimum(jnp.maximum(array, -reach), reach).astype(held_as)


def setup_inputs(seed: int = 0) -> dict:
    arg_keys = jax.random.split(jax.random.key(seed), 15)
    tokens = bell_draw(arg_keys[0], (TOKENS, D), 1.0, 6.0, ((0, 32),))
    cotangent = bell_draw(arg_keys[1], (TOKENS, D), 1.0, 6.0, ((0, 32),))
    prot_lens = draw_prot_lens(jax.random.fold_in(arg_keys[14], 71), 0)
    clus_start = touch_ends((jax.random.randint(arg_keys[3], (BUFFERS, SLOTS), 0, 3) < 1).astype(jnp.int32), jax.random.fold_in(arg_keys[3], 1), 0, 1)
    norm_gain = jnp.clip(1.0 + 0.1 * jax.random.normal(arg_keys[4], (D,), jnp.float32), 0.5, 1.5).astype(jnp.bfloat16)
    in_w = bell_draw(arg_keys[5], (D, 2 * DI), D ** -0.5, 0.1875, ((0, 4),))
    conv_w = bell_draw(arg_keys[6], (DCONV, DI), DCONV ** -0.5, 3.0, ((1, 4),))
    conv_b = bell_draw(arg_keys[7], (DI,), 0.5, 3.0, ((0, 4),))
    xproj_w = bell_draw(arg_keys[8], (DI, RANK + 2 * NST), DI ** -0.5, 0.125, ((0, 4),))
    dtproj_w = bell_draw(arg_keys[9], (RANK, DI), RANK ** -0.5, 0.75, ((1, 4),))
    dt_bias = jnp.clip(-6.875 + 4.578125 * jax.random.uniform(arg_keys[10], (DI,), jnp.float32) ** block_levels(arg_keys[10], (DI,), ((0, 4),), -0.2, 0.2), -6.875, -2.296875).astype(jnp.bfloat16)
    a_log = jnp.clip(2.765625 * jax.random.uniform(arg_keys[11], (NST, DI), jnp.float32) ** block_levels(arg_keys[11], (NST, DI), ((1, 4),), -0.2, 0.2), 0.0, 2.765625).astype(jnp.bfloat16)
    d_skip = jnp.clip(0.5 + 1.0 * jax.random.uniform(arg_keys[12], (DI,), jnp.float32) ** block_levels(arg_keys[12], (DI,), ((0, 4),), -0.2, 0.2), 0.5, 1.5).astype(jnp.bfloat16)
    out_w = bell_draw(arg_keys[13], (DI, D), (DI // 4) ** -0.5, 0.25, ((0, 4),))
    return dict(tokens=tokens, cotangent=cotangent, prot_lens=prot_lens, clus_start=clus_start, norm_gain=norm_gain, in_w=in_w, conv_w=conv_w, conv_b=conv_b, xproj_w=xproj_w, dtproj_w=dtproj_w, dt_bias=dt_bias, a_log=a_log, d_skip=d_skip, out_w=out_w)


@jax.custom_vjp
def low(v):
    return lax.optimization_barrier(v.astype(jnp.bfloat16)).astype(jnp.float32)

@jax.custom_vjp
def low_back(v):
    return v

def low_keep(v):
    return (low(v), None)

def low_pass(kept, grad):
    return (grad,)

def back_keep(v):
    return (v, None)

def back_low(kept, grad):
    return (low(grad),)
low.defvjp(low_keep, low_pass)
low_back.defvjp(back_keep, back_low)
EPSILON = 1e-05

def matmul_high(left, right):
    return jnp.dot(left, right, precision=lax.Precision.HIGHEST, preferred_element_type=jnp.float32)

def shifted_down(values, offset):
    padding = jnp.zeros((offset,) + values.shape[1:], values.dtype)
    return jnp.concatenate([padding, values[:-offset]], axis=0)

def protein_masks(lens_row, start_row):
    protein_ends = jnp.cumsum(lens_row).astype(jnp.int32)
    protein_begins = (protein_ends - lens_row).astype(jnp.int32)
    flagged = (start_row > 0) & (lens_row > 0)
    position = jnp.arange(CAP, dtype=jnp.int32)
    cluster = lax.optimization_barrier(jnp.sum(((position[:, None] >= protein_begins[None, :]) & flagged[None, :]).astype(jnp.int32), axis=1)).astype(jnp.int32)
    live_mask = (position < protein_ends[-1]).astype(jnp.float32)
    same_masks = []
    for offset in range(1, DCONV):
        matching = (position >= offset) & (cluster == shifted_down(cluster, offset))
        same_masks.append(matching.astype(jnp.float32))
    return (live_mask, same_masks)

def selective_scan(step_size, inputs, b_proj, c_proj, keep_mask, decay_rate):
    blocks = CAP // QLEN

    def run_block(hidden_state, block_inputs):

        def advance(inner_state, token_inputs):
            step_tok, input_tok, b_tok, c_tok, keep_tok = token_inputs
            decay_now = keep_tok * jnp.exp(decay_rate * step_tok[None, :])
            inner_state = decay_now * inner_state + b_tok[:, None] * (step_tok * input_tok)[None, :]
            return (inner_state, lax.optimization_barrier(jnp.sum(c_tok[:, None] * inner_state, axis=0)))
        return lax.scan(advance, hidden_state, block_inputs)
    shaped = tuple((member.reshape((blocks, QLEN) + member.shape[1:]) for member in (step_size, inputs, b_proj, c_proj, keep_mask)))
    initial = jnp.zeros((NST, DI), jnp.float32)
    _, outputs = lax.scan(jax.checkpoint(run_block), initial, shaped)
    return outputs.reshape(CAP, DI)

def layer_block(weights, x_rows, lens_row, start_row):
    gain, in_proj, conv_taps, conv_bias, x_proj, dt_proj, dt_shift, a_logs, skip_coef, out_proj = weights
    live_mask, same_masks = protein_masks(lens_row, start_row)
    mean_sq = lax.optimization_barrier(jnp.mean(x_rows * x_rows, axis=1, keepdims=True))
    x_hat = x_rows * lax.rsqrt(mean_sq + EPSILON)
    normed = low(x_hat * gain)
    projected = low_back(matmul_high(normed, in_proj))
    inner_part = projected[:, :DI]
    gate_part = projected[:, DI:]
    conv_pre = conv_bias + conv_taps[DCONV - 1] * inner_part
    for offset in range(1, DCONV):
        conv_pre = conv_pre + conv_taps[DCONV - 1 - offset] * shifted_down(inner_part, offset) * same_masks[offset - 1][:, None]
    activated = low(jax.nn.silu(conv_pre))
    dbc_rows = low_back(matmul_high(activated, x_proj))
    step_rank = low(dbc_rows[:, :RANK])
    b_proj = dbc_rows[:, RANK:RANK + NST]
    c_proj = dbc_rows[:, RANK + NST:]
    step_pre = low_back(matmul_high(step_rank, dt_proj) + dt_shift)
    step_size = jax.nn.softplus(step_pre)
    decay_rate = -jnp.exp(a_logs)
    scanned = selective_scan(step_size, activated, b_proj, c_proj, same_masks[0], decay_rate)
    y_rows = scanned + skip_coef * activated
    gated = low(y_rows * jax.nn.silu(gate_part))
    branch = low_back(matmul_high(gated, out_proj))
    return x_rows + live_mask[:, None] * branch

def reference(tokens, cotangent, prot_lens, clus_start, norm_gain, in_w, conv_w, conv_b, xproj_w, dtproj_w, dt_bias, a_log, d_skip, out_w):
    weights = tuple((member.astype(jnp.float32) for member in (norm_gain, in_w, conv_w, conv_b, xproj_w, dtproj_w, dt_bias, a_log, d_skip, out_w)))
    x_buffers = tokens.astype(jnp.float32).reshape(BUFFERS, CAP, D)
    cot_buffers = cotangent.astype(jnp.float32).reshape(BUFFERS, CAP, D)

    def forward(weight_set, x_all):

        def one_buffer(carried, buffer_inputs):
            x_rows, lens_row, start_row = buffer_inputs
            return (carried, jax.checkpoint(layer_block)(weight_set, x_rows, lens_row, start_row))
        _, outputs = lax.scan(one_buffer, jnp.zeros((), jnp.float32), (x_all, prot_lens, clus_start))
        return outputs
    outputs, pullback = jax.vjp(forward, weights, x_buffers)
    weight_grads, x_grads = pullback(cot_buffers)
    mixed = outputs.reshape(TOKENS, D).astype(jnp.bfloat16)
    token_grad = x_grads.reshape(TOKENS, D)
    return (mixed, token_grad, weight_grads[0], weight_grads[1], weight_grads[2], weight_grads[3], weight_grads[4], weight_grads[5], weight_grads[6], weight_grads[7], weight_grads[8], weight_grads[9])
```

```python
import functools

import jax
import jax.numpy as jnp
from jax import lax
from jax.experimental import pallas as pl
from jax.experimental.pallas import tpu as pltpu
from jax.sharding import PartitionSpec as P

QLEN = 16
LANES = 128
NEVER = 1e30
LOG2E = 1.4426950408889634


EPSILON = 1e-05


def shifted_down(values, offset):
    padding = jnp.zeros((offset,) + values.shape[1:], values.dtype)
    return jnp.concatenate([padding, values[:-offset]], axis=0)


def shifted_up(values, offset):
    padding = jnp.zeros((offset,) + values.shape[1:], values.dtype)
    return jnp.concatenate([values[offset:], padding], axis=0)


def protein_masks(lens_row, start_row, length, taps):
    protein_ends = jnp.cumsum(lens_row)
    protein_begins = protein_ends - lens_row
    flagged = (start_row > 0) & (lens_row > 0)
    position = jnp.arange(length, dtype=jnp.int32)
    cluster = jnp.sum(
        ((position[:, None] >= protein_begins[None, :]) & flagged[None, :]).astype(jnp.int32),
        axis=1,
    )
    live_mask = (position < protein_ends[-1]).astype(jnp.float32)
    same_masks = []
    for offset in range(1, taps):
        matching = (position >= offset) & (cluster == shifted_down(cluster, offset))
        same_masks.append(matching.astype(jnp.float32))
    return (live_mask, same_masks)


def rows_product(left, right):
    return lax.dot_general(
        left, right, (((0,), (0,)), ((), ())), preferred_element_type=jnp.float32
    )


def transposed_product(left, weight):
    return lax.dot_general(
        left, weight, (((1,), (1,)), ((), ())), preferred_element_type=jnp.float32
    )


def step_selectors(states):
    rows = QLEN * states
    by_token = (
        lax.broadcasted_iota(jnp.int32, (QLEN, rows), 1) // states
        == lax.broadcasted_iota(jnp.int32, (QLEN, rows), 0)
    ).astype(jnp.bfloat16)
    by_state = (
        lax.broadcasted_iota(jnp.int32, (states, rows), 1) % states
        == lax.broadcasted_iota(jnp.int32, (states, rows), 0)
    ).astype(jnp.bfloat16)
    diagonal = lax.broadcasted_iota(jnp.int32, (rows, QLEN), 0) // states == (
        lax.broadcasted_iota(jnp.int32, (rows, QLEN), 1)
    )
    return by_token, by_state, diagonal


def forward_kernel(group, dt_ref, feed_ref, b_ref, cblk_ref, rate_ref, y_ref, h_ref, state):
    blocks, _, width = dt_ref.shape
    states = rate_ref.shape[0]

    @pl.when(pl.program_id(0) == 0)
    def _():
        state[...] = jnp.zeros_like(state)

    def block(j, carried):
        r0 = pl.multiple_of(j * QLEN, QLEN)
        h0 = pl.multiple_of(j * QLEN * states, QLEN * states)
        for c0 in range(0, width, group * LANES):
            columns = [slice(c, c + LANES) for c in range(c0, c0 + group * LANES, LANES)]
            held = [state[:, s] for s in columns]
            rates = [rate_ref[:, s] for s in columns]
            for t in range(QLEN):
                b_t = b_ref[pl.ds(h0 + t * states, states), :]
                for k, s in enumerate(columns):
                    decay = jnp.exp2(dt_ref[j, t : t + 1, s] * rates[k])
                    held[k] = decay * held[k] + b_t * feed_ref[j, t : t + 1, s]
                    h_ref[pl.ds(h0 + t * states, states), s] = held[k].astype(h_ref.dtype)
            for k, s in enumerate(columns):
                state[:, s] = held[k]
            s = slice(c0, c0 + group * LANES)
            y_ref[pl.ds(r0, QLEN), s] = jnp.dot(
                cblk_ref[pl.ds(r0, QLEN), :],
                h_ref[pl.ds(h0, QLEN * states), s],
                preferred_element_type=jnp.float32,
            )
        return carried

    lax.fori_loop(0, blocks, block, 0)


def backward_kernel(
    group,
    dt_ref,
    feed_ref,
    dy_ref,
    c_ref,
    bblk_ref,
    h_ref,
    before_ref,
    rate2_ref,
    rate_ref,
    e_ref,
    lrate_ref,
    ldt_ref,
    db_ref,
    dc_ref,
    message,
    g_s,
    lrate_s,
    ldt_s,
    before_s,
):
    blocks, _, width = dt_ref.shape
    states = rate_ref.shape[0]
    rows = QLEN * states
    by_token, by_state, diagonal = step_selectors(states)

    @pl.when(pl.program_id(0) == 0)
    def _():
        message[...] = jnp.zeros_like(message)
        ldt_ref[...] = jnp.zeros_like(ldt_ref)

    def block(step, carried):
        j = blocks - 1 - step
        r0 = pl.multiple_of(j * QLEN, QLEN)
        h0 = pl.multiple_of(j * rows, rows)

        @pl.when(j == 0)
        def _():
            before_s[...] = before_ref[...]

        @pl.when(j > 0)
        def _():
            before_s[...] = h_ref[pl.ds(pl.multiple_of(jnp.maximum(h0 - states, 0), states), states), :]

        d_b = jnp.zeros((rows, QLEN), jnp.float32)
        d_c = jnp.zeros((rows, QLEN), jnp.float32)
        for c0 in range(0, width, group * LANES):
            columns = [slice(c, c + LANES) for c in range(c0, c0 + group * LANES, LANES)]
            held = [message[:, s] for s in columns]
            rates2 = [rate2_ref[:, s] for s in columns]
            rates = [rate_ref[:, s] for s in columns]
            for t in reversed(range(QLEN)):
                c_t = c_ref[pl.ds(h0 + t * states, states), :]
                at = slice(t * states, (t + 1) * states)
                for k, s in enumerate(columns):
                    g = c_t * dy_ref[j, t : t + 1, s] + held[k]
                    g_s[at, s] = g.astype(g_s.dtype)
                    dt = dt_ref[j, t : t + 1, s]
                    held[k] = jnp.exp2(dt * rates2[k]) * g
                    before = before_s[:, s] if t == 0 else h_ref[pl.ds(h0 + (t - 1) * states, states), s]
                    l = held[k].astype(jnp.bfloat16) * before
                    lrate_s[at, s] = l * rates[k]
                    ldt_s[at, s] = l * jnp.broadcast_to(dt, (states, LANES)).astype(jnp.bfloat16)
            for k, s in enumerate(columns):
                message[:, s] = held[k]
            s = slice(c0, c0 + group * LANES)
            e_ref[pl.ds(r0, QLEN), s] = jnp.dot(
                bblk_ref[pl.ds(r0, QLEN), :], g_s[:, s], preferred_element_type=jnp.float32
            )
            lrate_ref[pl.ds(r0, QLEN), s] = jnp.dot(
                by_token, lrate_s[:, s], preferred_element_type=jnp.float32
            )
            ldt_ref[:, s] += jnp.dot(by_state, ldt_s[:, s], preferred_element_type=jnp.float32)
            d_b += transposed_product(g_s[:, s], feed_ref[j, :, s].astype(jnp.bfloat16))
            d_c += transposed_product(
                h_ref[pl.ds(h0, rows), s], dy_ref[j, :, s].astype(jnp.bfloat16)
            )
        for total, out_ref in ((d_b, db_ref), (d_c, dc_ref)):
            out_ref[j] = jnp.dot(
                by_state,
                jnp.where(diagonal, total, 0.0).astype(jnp.bfloat16),
                preferred_element_type=jnp.float32,
            )
        return carried

    lax.fori_loop(0, blocks, block, 0)


def in_blocks(values):
    return values.reshape((values.shape[0] // QLEN, QLEN) + values.shape[1:])


def over_lanes(values):
    tokens, states = values.shape
    spread = jnp.broadcast_to(values[:, :, None], (tokens, states, LANES))
    return spread.reshape(tokens * states, LANES)


def block_diagonal(values):
    tokens, states = values.shape
    own = jnp.arange(tokens)[:, None] % QLEN == jnp.arange(QLEN * states)[None, :] // states
    return jnp.where(own, jnp.tile(values, (1, QLEN)), 0.0).astype(jnp.bfloat16)


def scan_forward(step_long, feed, b_proj, c_proj, decay_rate, blocks=4, group=4):
    tokens, width = feed.shape
    states = decay_rate.shape[0]
    rows = blocks * QLEN
    wide = pl.BlockSpec((blocks, QLEN, width), lambda i: (i, 0, 0))
    return pl.pallas_call(
        functools.partial(forward_kernel, group),
        grid=(tokens // rows,),
        in_specs=[
            wide,
            wide,
            pl.BlockSpec((rows * states, LANES), lambda i: (i, 0)),
            pl.BlockSpec((rows, QLEN * states), lambda i: (i, 0)),
            pl.BlockSpec((states, width), lambda i: (0, 0)),
        ],
        out_specs=[
            pl.BlockSpec((rows, width), lambda i: (i, 0)),
            pl.BlockSpec((rows * states, width), lambda i: (i, 0)),
        ],
        out_shape=[
            jax.ShapeDtypeStruct((tokens, width), jnp.float32),
            jax.ShapeDtypeStruct((tokens * states, width), jnp.bfloat16),
        ],
        scratch_shapes=[pltpu.VMEM((states, width), jnp.float32)],
        compiler_params=pltpu.CompilerParams(vmem_limit_bytes=48 << 20),
        name="scan_forward",
    )(in_blocks(step_long), in_blocks(feed), over_lanes(b_proj), block_diagonal(c_proj), decay_rate * LOG2E)


def scan_backward(step_long, feed, b_proj, c_proj, d_y, states_kept, decay_rate, blocks=4, group=2):
    tokens, width = feed.shape
    states = decay_rate.shape[0]
    rows = blocks * QLEN
    steps = tokens // rows
    wide = pl.BlockSpec((blocks, QLEN, width), lambda i: (steps - 1 - i, 0, 0))
    flat = lambda i: (steps - 1 - i, 0)
    small = pl.BlockSpec((blocks, states, QLEN), lambda i: (steps - 1 - i, 0, 0))
    whole = pl.BlockSpec((states, width), lambda i: (0, 0))
    small_shape = jax.ShapeDtypeStruct((tokens // QLEN, states, QLEN), jnp.float32)
    held = pltpu.VMEM((QLEN * states, width), jnp.bfloat16)
    e, lrate, ldt, d_b, d_c = pl.pallas_call(
        functools.partial(backward_kernel, group),
        grid=(steps,),
        in_specs=[
            wide,
            wide,
            wide,
            pl.BlockSpec((rows * states, LANES), flat),
            pl.BlockSpec((rows, QLEN * states), flat),
            pl.BlockSpec((rows * states, width), flat),
            pl.BlockSpec((states, width), lambda i: (jnp.maximum((steps - 1 - i) * rows - 1, 0), 0)),
            whole,
            whole,
        ],
        out_specs=[
            pl.BlockSpec((rows, width), flat),
            pl.BlockSpec((rows, width), flat),
            whole,
            small,
            small,
        ],
        out_shape=[
            jax.ShapeDtypeStruct((tokens, width), jnp.float32),
            jax.ShapeDtypeStruct((tokens, width), jnp.float32),
            jax.ShapeDtypeStruct((states, width), jnp.float32),
            small_shape,
            small_shape,
        ],
        scratch_shapes=[
            pltpu.VMEM((states, width), jnp.float32),
            held,
            held,
            held,
            pltpu.VMEM((states, width), jnp.bfloat16),
        ],
        compiler_params=pltpu.CompilerParams(vmem_limit_bytes=56 << 20),
        name="scan_backward",
    )(
        in_blocks(step_long),
        in_blocks(feed),
        in_blocks(d_y),
        over_lanes(c_proj),
        block_diagonal(b_proj),
        states_kept,
        states_kept,
        decay_rate * LOG2E,
        decay_rate.astype(jnp.bfloat16),
    )
    by_token = lambda v: jnp.swapaxes(v, 1, 2).reshape(tokens, states)
    return e, lrate, ldt, by_token(d_b), by_token(d_c)


MESH = pl.DeviceIdType.MESH
GROUP = 8


def own_bits():
    d, f = lax.axis_index("dp"), lax.axis_index("fsdp")
    inside = lax.rem(d, GROUP)
    return {
        "pair": f // 2,
        "core": lax.rem(f, 2),
        "high": inside // 4,
        "low": lax.rem(inside // 2, 2),
        "bit": lax.rem(inside, 2),
    }


def across(own, dim):
    d, f = lax.axis_index("dp"), lax.axis_index("fsdp")
    step = {"pair": 2, "core": 1, "high": 4, "low": 2, "bit": 1}[dim]
    flip = step * (1 - 2 * own[dim])
    return (d, f + flip) if dim in ("pair", "core") else (d + flip, f)


def greet(own, dims):
    barrier = pltpu.get_barrier_semaphore()
    for dim in dims:
        pl.semaphore_signal(barrier, inc=1, device_id=across(own, dim), device_id_type=MESH)
    pl.semaphore_wait(barrier, len(dims))


class Link:
    def __init__(self, own):
        self.own = own
        self.sent = []

    def copy(self, src, dst, sems, dim):
        return pltpu.make_async_remote_copy(
            src_ref=src,
            dst_ref=dst,
            send_sem=sems[0],
            recv_sem=sems[1],
            device_id=across(self.own, dim),
            device_id_type=MESH,
        )

    def send(self, src, dst, sems, dim):
        self.copy(src, dst, sems, dim).start()
        self.sent.append((src, dst, sems, dim))

    def receive(self, ref, sems, dim):
        self.copy(ref, ref, sems, dim).wait_recv()

    def finish(self):
        for entry in self.sent:
            self.copy(*entry).wait_send()


def gather_kernel(*refs):
    count = (len(refs) - 4) // 3
    shards, outs, stage = refs[:count], refs[count : 2 * count], refs[2 * count : 3 * count]
    load_sem, core_sem, hop_sem, whole_sem = refs[3 * count :]
    own = own_bits()
    greet(own, ("core", "pair", "bit", "low"))
    link = Link(own)
    mine = 2 * own["pair"] + own["core"]
    theirs = 2 * (1 - own["pair"]) + own["core"]
    sibling = 2 * own["pair"] + 1 - own["core"]
    beyond = 2 * (1 - own["pair"]) + 1 - own["core"]

    def eighth(a, bit, low, half):
        rows = shards[a].shape[0] // 8
        start = (2 * (bit + 2 * low) + (half or 0)) * rows
        return pl.ds(pl.multiple_of(start, rows), rows * (1 if half is not None else 2))

    here, far = own["bit"], 1 - own["bit"]
    near, off = own["low"], 1 - own["low"]
    for half in range(2):
        for a in range(count):
            rows = eighth(a, here, near, half)
            sems = (hop_sem.at[0, a, 0, half], hop_sem.at[1, a, 0, half])
            link.send(shards[a].at[rows], outs[a].at[mine, rows], sems, "pair")
    loads = [pltpu.make_async_copy(shards[a], stage[a], load_sem.at[a]) for a in range(count)]
    for a in range(count):
        loads[a].start()
        sems = (whole_sem.at[0, a], whole_sem.at[1, a])
        link.send(shards[a], outs[a].at[mine], sems, "core")

    def arrive(a, kind, half, rows, dim):
        ref = outs[a].at[theirs, rows]
        link.receive(ref, (hop_sem.at[0, a, kind, half], hop_sem.at[1, a, kind, half]), dim)
        link.send(ref, ref, (core_sem.at[0, a, kind, half], core_sem.at[1, a, kind, half]), "core")
        return ref

    def pass_on(ref, a, kind, half, dim):
        link.send(ref, ref, (hop_sem.at[0, a, kind, half], hop_sem.at[1, a, kind, half]), dim)

    for half in range(2):
        for a in range(count):
            ref = arrive(a, 0, half, eighth(a, here, near, half), "pair")
            pass_on(ref, a, 1, half, "bit")
            pass_on(ref, a, 2, half, "low")
    for a in range(count):
        loads[a].wait()
    stores = [pltpu.make_async_copy(stage[a], outs[a].at[mine], load_sem.at[a]) for a in range(count)]
    for copy in stores:
        copy.start()
    for half in range(2):
        for a in range(count):
            ref = arrive(a, 1, half, eighth(a, far, near, half), "bit")
            if half == 0:
                pass_on(ref, a, 3, 0, "low")
            ref = arrive(a, 2, half, eighth(a, here, off, half), "low")
            if half == 1:
                pass_on(ref, a, 3, 1, "bit")
    for a in range(count):
        arrive(a, 3, 0, eighth(a, far, off, 0), "low")
        arrive(a, 3, 1, eighth(a, far, off, 1), "bit")
    for a in range(count):
        link.receive(outs[a].at[sibling], (whole_sem.at[0, a], whole_sem.at[1, a]), "core")
        for kind, bit, low in ((0, here, near), (1, far, near), (2, here, off), (3, far, off)):
            for half in range(2):
                ref = outs[a].at[beyond, eighth(a, bit, low, half)]
                link.receive(ref, (core_sem.at[0, a, kind, half], core_sem.at[1, a, kind, half]), "core")
    for copy in stores:
        copy.wait()
    link.finish()


def gather_weights(shards, collective_id):
    count = len(shards)
    dma = pltpu.SemaphoreType.DMA
    return pl.pallas_call(
        gather_kernel,
        out_shape=[jax.ShapeDtypeStruct((4,) + s.shape, s.dtype) for s in shards],
        in_specs=[pl.BlockSpec(memory_space=pl.ANY)] * count,
        out_specs=[pl.BlockSpec(memory_space=pl.ANY)] * count,
        scratch_shapes=[pltpu.VMEM(s.shape, s.dtype) for s in shards]
        + [dma((count,)), dma((2, count, 4, 2)), dma((2, count, 4, 2)), dma((2, count))],
        compiler_params=pltpu.CompilerParams(
            collective_id=collective_id, has_side_effects=True, vmem_limit_bytes=32 << 20
        ),
        name="gather_weights",
    )(*shards)


DIMS = ("pair", "high", "low", "bit")
HALVE = (("pair", "bit", "low", "high"), ("bit", "low", "pair", "high"), ("low", "pair", "bit", "high"))
SPREAD = (("high", "bit", "low"), ("high", "low", "bit"), ("high", "bit", "low"))
EVERY = slice(None)


def each_block(free, body):
    if not free:
        body(())
        return

    def step(i, carried):
        body(tuple(lax.rem(i // 2 ** (free - 1 - n), 2) for n in range(free)))
        return carried

    lax.fori_loop(0, 2**free, step, 0)


def cut_parts(shape):
    axis, tile = (1, 128) if shape[1] >= 512 else (0, 16)
    tiles = shape[axis] // tile
    sizes = [(tiles + 2 - k) // 3 * tile for k in range(3)]
    return [(axis, sum(sizes[:k]), sizes[k]) for k in range(3)]


class Reduction:
    def __init__(self, grads, outs, scratch):
        count = len(grads)
        self.grads, self.outs = grads, outs
        self.accs, self.cores, self.fulls = (scratch[i * count : (i + 1) * count] for i in range(3))
        rest = scratch[3 * count :]
        self.arrived = [[[rest[(s * count + a) * 3 + k] for k in range(3)] for a in range(count)] for s in range(4)]
        self.load_sem, self.core_sem, self.half_sem, self.full_sem, self.out_sem = rest[12 * count :]
        self.parts = [cut_parts(g.shape[4:]) for g in grads]
        self.jobs = [(k, a) for k in range(3) for a in range(count)]
        self.own = own_bits()
        self.link = Link(self.own)
        self.stages = [self.begin, self.join, *(functools.partial(self.halved, s) for s in range(4))]
        self.stages += [*(functools.partial(self.spread, s) for s in range(3)), self.end]

    def part(self, k, a):
        axis, start, size = self.parts[a][k]
        return (pl.ds(start, size), EVERY) if axis == 0 else (EVERY, pl.ds(start, size))

    def region(self, chosen, dims, k, a):
        return tuple(chosen.get(d, EVERY) for d in dims) + self.part(k, a)

    def loading(self, k, a, y):
        at = self.region({"pair": y}, DIMS, k, a)
        kept = (2 * y + self.own["core"],) + at[1:]
        return pltpu.make_async_copy(self.grads[a].at[kept], self.accs[a].at[at], self.load_sem.at[a, k, y])

    def begin(self):
        greet(self.own, ("core", "pair", "bit", "low", "high"))
        for k, a in self.jobs:
            for y in range(2):
                at = self.region({"pair": y}, DIMS, k, a)
                given = (2 * y + 1 - self.own["core"],) + at[1:]
                sems = (self.core_sem.at[0, a, k, y], self.core_sem.at[1, a, k, y])
                self.link.send(self.grads[a].at[given], self.cores[a].at[at], sems, "core")
                self.loading(k, a, y).start()

    def halve(self, k, a, step):
        dim = HALVE[k][step]
        chosen = {d: self.own[d] for d in HALVE[k][:step]}
        chosen[dim] = 1 - self.own[dim]
        sems = (self.half_sem.at[0, a, k, step], self.half_sem.at[1, a, k, step])
        self.link.send(self.accs[a].at[self.region(chosen, DIMS, k, a)], self.arrived[step][a][k], sems, dim)

    def join(self):
        for k, a in self.jobs:
            for y in range(2):
                self.loading(k, a, y).wait()
                sems = (self.core_sem.at[0, a, k, y], self.core_sem.at[1, a, k, y])
                self.link.receive(self.cores[a].at[self.region({"pair": y}, DIMS, k, a)], sems, "core")

            def add(lead):
                at = lead + self.part(k, a)
                self.accs[a][at] = self.accs[a][at] + self.cores[a][at]

            each_block(4, add)
            self.halve(k, a, 0)

    def halved(self, step):
        for k, a in self.jobs:
            sems = (self.half_sem.at[0, a, k, step], self.half_sem.at[1, a, k, step])
            self.link.receive(self.arrived[step][a][k], sems, HALVE[k][step])
            chosen = {d: self.own[d] for d in HALVE[k][: step + 1]}
            free = [d for d in DIMS if d not in chosen]

            def add(lead):
                at = tuple(chosen[d] if d in chosen else lead[free.index(d)] for d in DIMS) + self.part(k, a)
                total = self.accs[a][at] + self.arrived[step][a][k][lead + (EVERY, EVERY)]
                if step < 3:
                    self.accs[a][at] = total
                else:
                    self.fulls[a][at[1:]] = total

            each_block(len(free), add)
            if step < 3:
                self.halve(k, a, step + 1)
            else:
                self.pass_on(k, a, 0)

    def pass_on(self, k, a, step):
        chosen = {d: self.own[d] for d in SPREAD[k][step:]}
        here = self.fulls[a].at[self.region(chosen, DIMS[1:], k, a)]
        self.link.send(here, here, (self.full_sem.at[0, a, k, step], self.full_sem.at[1, a, k, step]), SPREAD[k][step])

    def spread(self, step):
        for k, a in self.jobs:
            chosen = {d: self.own[d] for d in SPREAD[k][step:]}
            dim = SPREAD[k][step]
            chosen[dim] = 1 - self.own[dim]
            there = self.fulls[a].at[self.region(chosen, DIMS[1:], k, a)]
            self.link.receive(there, (self.full_sem.at[0, a, k, step], self.full_sem.at[1, a, k, step]), dim)
            if step < 2:
                self.pass_on(k, a, step + 1)

    def end(self):
        stores = [
            pltpu.make_async_copy(self.fulls[a], self.outs[a], self.out_sem.at[a]) for a in range(len(self.outs))
        ]
        for copy in stores:
            copy.start()
        for copy in stores:
            copy.wait()
        self.link.finish()

    @staticmethod
    def scratch(grads):
        count = len(grads)
        dma = pltpu.SemaphoreType.DMA
        low = jnp.bfloat16
        shapes = [pltpu.VMEM((2, 2, 2, 2) + g.shape[4:], low) for g in grads] * 2
        shapes += [pltpu.VMEM((2, 2, 2) + g.shape[4:], low) for g in grads]
        for step in range(4):
            for g in grads:
                for axis, _, size in cut_parts(g.shape[4:]):
                    block = (size, g.shape[5]) if axis == 0 else (g.shape[4], size)
                    shapes.append(pltpu.VMEM((2,) * (3 - step) + block, low))
        return shapes + [
            dma((count, 3, 2)),
            dma((2, count, 3, 2)),
            dma((2, count, 3, 4)),
            dma((2, count, 3, 3)),
            dma((count,)),
        ]


def reduce_kernel(count, *refs):
    for stage in Reduction(refs[:count], refs[count : 2 * count], refs[2 * count :]).stages:
        stage()


def reduce_gradients(grads, collective_id):
    count = len(grads)
    return pl.pallas_call(
        functools.partial(reduce_kernel, count),
        out_shape=[jax.ShapeDtypeStruct(g.shape[1:], g.dtype) for g in grads],
        in_specs=[pl.BlockSpec(memory_space=pl.ANY)] * count,
        out_specs=[pl.BlockSpec(memory_space=pl.ANY)] * count,
        scratch_shapes=Reduction.scratch(grads),
        compiler_params=pltpu.CompilerParams(
            collective_id=collective_id, has_side_effects=True, vmem_limit_bytes=56 << 20
        ),
        name="reduce_gradients",
    )(*grads)


def add_groups(sums):
    groups = lax.axis_size("dp") // GROUP
    if groups == 1:
        return sums
    alike = [[g * GROUP + i for g in range(groups)] for i in range(GROUP)]
    return lax.psum(sums, "dp", axis_index_groups=alike)


def body(
    tokens,
    cotangent,
    prot_lens,
    clus_start,
    norm_gain,
    in_w,
    conv_w,
    conv_b,
    xproj_w,
    dtproj_w,
    dt_bias,
    a_log,
    d_skip,
    out_w,
):
    rank_width, owned = dtproj_w.shape
    state_width = a_log.shape[0]
    taps = conv_w.shape[0]
    width_by_channel = (
        (dtproj_w, rank_width),
        (a_log, state_width),
        (xproj_w.T, xproj_w.shape[1]),
        (conv_w, taps),
        (conv_b[None], 1),
        (dt_bias[None], 1),
        (d_skip[None], 1),
        (jnp.pad(norm_gain, (0, owned - norm_gain.shape[0]))[None], 1),
    )
    packed = jnp.concatenate([v for v, _ in width_by_channel], axis=0)
    packed = jnp.pad(packed, ((0, -packed.shape[0] % 128), (0, 0)))
    in_full, out_full, packed = gather_weights((in_w, out_w, packed), 1)
    in_full = in_full.reshape(-1, in_full.shape[2])
    out_full = out_full.reshape(-1, out_full.shape[2])
    gain_full = packed[:, sum(n for _, n in width_by_channel) - 1, : norm_gain.shape[0]].reshape(-1)
    by_channel = jnp.swapaxes(packed, 0, 1).reshape(packed.shape[1], -1)
    unpacked = []
    for _, n in width_by_channel[:-1]:
        unpacked.append(by_channel[:n])
        by_channel = by_channel[n:]
    dtproj_full, alog_full, xproj_full, conv_full, convb_full, dtb_full, skip_full = unpacked
    xproj_full = xproj_full.T
    convb_full, dtb_full, skip_full = convb_full[0], dtb_full[0], skip_full[0]
    length = tokens.shape[0]
    inner_width = in_full.shape[1] // 2
    live_mask, same_masks = protein_masks(prot_lens[0], clus_start[0], length, taps)
    keep_mask = same_masks[0]
    x_float = tokens.astype(jnp.float32)
    inv_rms = lax.rsqrt(jnp.mean(x_float * x_float, axis=1, keepdims=True) + EPSILON)
    x_hat = x_float * inv_rms
    normed = (x_hat * gain_full.astype(jnp.float32)).astype(jnp.bfloat16)
    projected = jnp.dot(normed, in_full, preferred_element_type=jnp.float32)
    inner_part = projected[:, :inner_width]
    gate_part = projected[:, inner_width:]
    tap_weights = conv_full.astype(jnp.float32)
    shifted_parts = [
        shifted_down(inner_part, offset) * same_masks[offset - 1][:, None]
        for offset in range(1, taps)
    ]
    conv_pre = convb_full.astype(jnp.float32) + tap_weights[taps - 1] * inner_part
    for offset in range(1, taps):
        conv_pre = conv_pre + tap_weights[taps - 1 - offset] * shifted_parts[offset - 1]
    act_low = jax.nn.silu(conv_pre).astype(jnp.bfloat16)
    act_float = act_low.astype(jnp.float32)
    dbc_rows = jnp.dot(act_low, xproj_full, preferred_element_type=jnp.float32)
    step_rank = dbc_rows[:, :rank_width].astype(jnp.bfloat16)
    b_proj = dbc_rows[:, rank_width : rank_width + state_width]
    c_proj = dbc_rows[:, rank_width + state_width :]
    step_pre = jnp.dot(
        step_rank, dtproj_full, preferred_element_type=jnp.float32
    ) + dtb_full.astype(jnp.float32)
    step_size = jax.nn.softplus(step_pre)
    decay_rate = -jnp.exp(alog_full.astype(jnp.float32))
    feed = step_size * act_float
    step_long = jnp.where(keep_mask[:, None] > 0, step_size, NEVER)
    scanned, states_kept = scan_forward(step_long, feed, b_proj, c_proj, decay_rate)
    skip_float = skip_full.astype(jnp.float32)
    y_rows = scanned + skip_float * act_float
    gate_sig = jax.nn.sigmoid(gate_part)
    gate_silu = gate_part * gate_sig
    gated_low = (y_rows * gate_silu).astype(jnp.bfloat16)
    branch = jnp.dot(gated_low, out_full, preferred_element_type=jnp.float32)
    mixed = (x_float + live_mask[:, None] * branch).astype(jnp.bfloat16)
    back_taps = tap_weights
    cot_float = cotangent.astype(jnp.float32)
    d_branch = (live_mask[:, None] * cot_float).astype(jnp.bfloat16)
    out_local = rows_product(gated_low, d_branch)
    d_gated = transposed_product(d_branch, out_full)
    d_y = d_gated * gate_silu
    d_gate = d_gated * y_rows * gate_sig * (1.0 + gate_part * (1.0 - gate_sig))
    skip_local = jnp.sum(d_y * act_float, axis=0)
    grad_feed, grad_step, rate_sum, grad_b, grad_c = scan_backward(
        step_long, feed, b_proj, c_proj, d_y, states_kept, decay_rate
    )
    alog_local = rate_sum * decay_rate
    d_step = grad_feed * act_float + grad_step
    d_act = d_y * skip_full.astype(jnp.float32) + grad_feed * step_size
    d_step_pre = (d_step * jax.nn.sigmoid(step_pre)).astype(jnp.bfloat16)
    dtb_local = jnp.sum(d_step_pre.astype(jnp.float32), axis=0)
    dtproj_local = rows_product(d_step_pre, step_rank)
    d_rank = transposed_product(d_step_pre, dtproj_full)
    d_dbc = jnp.concatenate([d_rank, grad_b, grad_c], axis=1).astype(jnp.bfloat16)
    xproj_local = rows_product(act_low, d_dbc)
    d_act = d_act + transposed_product(d_dbc, xproj_full)
    pre_sig = jax.nn.sigmoid(conv_pre)
    d_pre = d_act * pre_sig * (1.0 + conv_pre * (1.0 - pre_sig))
    convb_local = jnp.sum(d_pre, axis=0)
    tap_rows = [
        jnp.sum(d_pre * shifted_parts[taps - 2 - index], axis=0) for index in range(taps - 1)
    ]
    tap_rows.append(jnp.sum(d_pre * inner_part, axis=0))
    conv_local = jnp.stack(tap_rows, axis=0)
    d_inner = back_taps[taps - 1] * d_pre
    for offset in range(1, taps):
        d_inner = d_inner + back_taps[taps - 1 - offset] * shifted_up(
            d_pre * same_masks[offset - 1][:, None], offset
        )
    d_proj = jnp.concatenate([d_inner, d_gate], axis=1).astype(jnp.bfloat16)
    in_local = rows_product(normed, d_proj)
    d_normed = transposed_product(d_proj, in_full)
    gain_local = jnp.sum(d_normed * x_hat, axis=0)
    d_hat = d_normed * gain_full.astype(jnp.float32)
    token_grad = cot_float + inv_rms * (
        d_hat - x_hat * jnp.mean(d_hat * x_hat, axis=1, keepdims=True)
    )
    gain_rows = jnp.pad(gain_local.reshape(4, -1), ((0, 0), (0, owned - norm_gain.shape[0]))).reshape(-1, 1)
    by_channel = (
        xproj_local,
        dtproj_local,
        alog_local.T,
        conv_local.T,
        convb_local[:, None],
        dtb_local[:, None],
        skip_local[:, None],
        gain_rows,
    )
    small_local = jnp.concatenate([v.astype(jnp.bfloat16) for v in by_channel], axis=1)
    small_local = jnp.pad(small_local, ((0, 0), (0, -small_local.shape[1] % 128)))
    in_pieces = lambda v: v.astype(jnp.bfloat16).reshape((4, 2, 2, 2, v.shape[0] // 32, v.shape[1]))
    sums = reduce_gradients([in_pieces(v) for v in (in_local, out_local, small_local)], 2)
    in_grad, out_grad, small = (v.reshape(-1, v.shape[-1]).astype(jnp.float32) for v in sums)
    rest = add_groups((in_grad, out_grad, small))
    in_grad, out_grad, small = rest
    columns = []
    for v in by_channel:
        columns.append(small[:, : v.shape[1]])
        small = small[:, v.shape[1] :]
    xproj_grad, dtproj_grad, alog_grad, conv_grad, convb_grad, dtb_grad, skip_grad, gain_grad = columns
    dtproj_grad, alog_grad, conv_grad = dtproj_grad.T, alog_grad.T, conv_grad.T
    convb_grad, dtb_grad, skip_grad = convb_grad[:, 0], dtb_grad[:, 0], skip_grad[:, 0]
    gain_grad = gain_grad[: norm_gain.shape[0], 0]
    return (
        mixed,
        token_grad,
        gain_grad,
        in_grad,
        conv_grad,
        convb_grad,
        xproj_grad,
        dtproj_grad,
        dtb_grad,
        alog_grad,
        skip_grad,
        out_grad,
    )


def solution(mesh):
    in_specs = (
        P(("dp", "fsdp"), None),
        P(("dp", "fsdp"), None),
        P(("dp", "fsdp"), None),
        P(("dp", "fsdp"), None),
        P("fsdp"),
        P("fsdp", None),
        P(None, "fsdp"),
        P("fsdp"),
        P("fsdp", None),
        P(None, "fsdp"),
        P("fsdp"),
        P(None, "fsdp"),
        P("fsdp"),
        P("fsdp", None),
    )
    out_specs = (
        P(("dp", "fsdp"), None),
        P(("dp", "fsdp"), None),
        P("fsdp"),
        P("fsdp", None),
        P(None, "fsdp"),
        P("fsdp"),
        P("fsdp", None),
        P(None, "fsdp"),
        P("fsdp"),
        P(None, "fsdp"),
        P("fsdp"),
        P("fsdp", None),
    )
    return jax.shard_map(body, mesh=mesh, in_specs=in_specs, out_specs=out_specs, check_vma=False)
```

```python
import functools

import jax
import jax.numpy as jnp
from jax import lax
from jax.experimental import pallas as pl
from jax.experimental.pallas import tpu as pltpu
from jax.sharding import PartitionSpec as P

QLEN = 16
LANES = 128
NEVER = 1e30
LOG2E = 1.4426950408889634
FORWARD_STEPS = (0, 2, 3, 4, 5, 6)
BACKWARD_STEPS = (0, 3, 7, 10, 12, 14, 15)


EPSILON = 1e-05


def shifted_down(values, offset):
    padding = jnp.zeros((offset,) + values.shape[1:], values.dtype)
    return jnp.concatenate([padding, values[:-offset]], axis=0)


def shifted_up(values, offset):
    padding = jnp.zeros((offset,) + values.shape[1:], values.dtype)
    return jnp.concatenate([values[offset:], padding], axis=0)


def protein_masks(lens_row, start_row, length, taps):
    protein_ends = jnp.cumsum(lens_row)
    protein_begins = protein_ends - lens_row
    flagged = (start_row > 0) & (lens_row > 0)
    position = jnp.arange(length, dtype=jnp.int32)
    cluster = jnp.sum(
        ((position[:, None] >= protein_begins[None, :]) & flagged[None, :]).astype(jnp.int32),
        axis=1,
    )
    live_mask = (position < protein_ends[-1]).astype(jnp.float32)
    same_masks = []
    for offset in range(1, taps):
        matching = (position >= offset) & (cluster == shifted_down(cluster, offset))
        same_masks.append(matching.astype(jnp.float32))
    return (live_mask, same_masks)


def rows_product(left, right):
    return lax.dot_general(
        left, right, (((0,), (0,)), ((), ())), preferred_element_type=jnp.float32
    )


def transposed_product(left, weight):
    return lax.dot_general(
        left, weight, (((1,), (1,)), ((), ())), preferred_element_type=jnp.float32
    )


MESH = pl.DeviceIdType.MESH
GROUP = 8


def own_bits():
    d, f = lax.axis_index("dp"), lax.axis_index("fsdp")
    inside = lax.rem(d, GROUP)
    return {
        "pair": f // 2,
        "core": lax.rem(f, 2),
        "high": inside // 4,
        "low": lax.rem(inside // 2, 2),
        "bit": lax.rem(inside, 2),
    }


def across(own, dim):
    d, f = lax.axis_index("dp"), lax.axis_index("fsdp")
    step = {"pair": 2, "core": 1, "high": 4, "low": 2, "bit": 1}[dim]
    flip = step * (1 - 2 * own[dim])
    return (d, f + flip) if dim in ("pair", "core") else (d + flip, f)


def greet(own, dims):
    barrier = pltpu.get_barrier_semaphore()
    for dim in dims:
        pl.semaphore_signal(barrier, inc=1, device_id=across(own, dim), device_id_type=MESH)
    pl.semaphore_wait(barrier, len(dims))


class Link:
    def __init__(self, own):
        self.own = own
        self.sent = []

    def copy(self, src, dst, sems, dim):
        return pltpu.make_async_remote_copy(
            src_ref=src,
            dst_ref=dst,
            send_sem=sems[0],
            recv_sem=sems[1],
            device_id=across(self.own, dim),
            device_id_type=MESH,
        )

    def send(self, described):
        self.copy(*described()).start()
        self.sent.append(described)

    def receive(self, ref, sems, dim):
        self.copy(ref, ref, sems, dim).wait_recv()

    def finish(self):
        for described in self.sent:
            self.copy(*described()).wait_send()


class Gather:
    def __init__(self, shards, outs, scratch):
        self.shards, self.outs = shards, outs
        self.count = len(shards)
        self.stage = scratch[: self.count]
        self.load_sem, self.core_sem, self.hop_sem, self.whole_sem = scratch[self.count :]
        self.own = own_bits()
        self.link = Link(self.own)
        pair, core = self.own["pair"], self.own["core"]
        self.mine = 2 * pair + core
        self.theirs = 2 * (1 - pair) + core
        self.sibling = 2 * pair + 1 - core
        self.beyond = 2 * (1 - pair) + 1 - core
        bit, low = self.own["bit"], self.own["low"]
        self.kinds = ((bit, low), (1 - bit, low), (bit, 1 - low), (1 - bit, 1 - low))
        self.stages = [self.begin, *(functools.partial(self.from_pair, half) for half in range(2))]
        self.stages += [*(functools.partial(self.from_near, half) for half in range(2)), self.from_far, self.end]

    def eighth(self, a, kind, half):
        rows = self.shards[a].shape[0] // 8
        bit, low = self.kinds[kind]
        return pl.ds(pl.multiple_of((2 * (bit + 2 * low) + half) * rows, rows), rows)

    def hop(self, a, kind, half):
        return self.hop_sem.at[0, a, kind, half], self.hop_sem.at[1, a, kind, half]

    def to_core(self, a, kind, half):
        return self.core_sem.at[0, a, kind, half], self.core_sem.at[1, a, kind, half]

    def whole(self, a):
        return self.whole_sem.at[0, a], self.whole_sem.at[1, a]

    def load(self, a):
        return pltpu.make_async_copy(self.shards[a], self.stage[a], self.load_sem.at[a])

    def store(self, a):
        return pltpu.make_async_copy(self.stage[a], self.outs[a].at[self.mine], self.load_sem.at[a])

    def begin(self):
        greet(self.own, ("core", "pair", "bit", "low"))
        for half in range(2):
            for a in range(self.count):
                self.link.send(functools.partial(self.to_pair, a, half))
        for a in range(self.count):
            self.load(a).start()
            self.link.send(functools.partial(self.own_to_core, a))

    def to_pair(self, a, half):
        rows = self.eighth(a, 0, half)
        return self.shards[a].at[rows], self.outs[a].at[self.mine, rows], self.hop(a, 0, half), "pair"

    def own_to_core(self, a):
        return self.shards[a], self.outs[a].at[self.mine], self.whole(a), "core"

    def came(self, a, kind, half):
        return self.outs[a].at[self.theirs, self.eighth(a, kind, half)]

    def onward(self, a, kind, half, new_kind, dim):
        ref = self.came(a, kind, half)
        return ref, ref, self.to_core(a, kind, half) if dim == "core" else self.hop(a, new_kind, half), dim

    def pass_on(self, a, kind, half, new_kind, dim):
        self.link.send(functools.partial(self.onward, a, kind, half, new_kind, dim))

    def arrive(self, a, kind, half, dim):
        self.link.receive(self.came(a, kind, half), self.hop(a, kind, half), dim)
        self.pass_on(a, kind, half, kind, "core")

    def from_pair(self, half):
        for a in range(self.count):
            self.arrive(a, 0, half, "pair")
            self.pass_on(a, 0, half, 1, "bit")
            self.pass_on(a, 0, half, 2, "low")
        if half == 1:
            for a in range(self.count):
                self.load(a).wait()
                self.store(a).start()

    def from_near(self, half):
        for a in range(self.count):
            self.arrive(a, 1, half, "bit")
            if half == 0:
                self.pass_on(a, 1, 0, 3, "low")
            self.arrive(a, 2, half, "low")
            if half == 1:
                self.pass_on(a, 2, 1, 3, "bit")

    def from_far(self):
        for a in range(self.count):
            self.arrive(a, 3, 0, "low")
            self.arrive(a, 3, 1, "bit")

    def end(self):
        for a in range(self.count):
            self.link.receive(self.outs[a].at[self.sibling], self.whole(a), "core")
            for kind in range(4):
                for half in range(2):
                    ref = self.outs[a].at[self.beyond, self.eighth(a, kind, half)]
                    self.link.receive(ref, self.to_core(a, kind, half), "core")
            self.store(a).wait()
        self.link.finish()

    @staticmethod
    def scratch(shards):
        count = len(shards)
        dma = pltpu.SemaphoreType.DMA
        staged = [pltpu.VMEM(s.shape, s.dtype) for s in shards]
        return staged + [dma((count,)), dma((2, count, 4, 2)), dma((2, count, 4, 2)), dma((2, count))]


def gather_kernel(count, *refs):
    for stage in Gather(refs[:count], refs[count : 2 * count], refs[2 * count :]).stages:
        stage()


def gathered_shape(shard):
    return jax.ShapeDtypeStruct((4,) + shard.shape, shard.dtype)


def gather_weights(shards, collective_id):
    count = len(shards)
    return pl.pallas_call(
        functools.partial(gather_kernel, count),
        out_shape=[gathered_shape(s) for s in shards],
        in_specs=[pl.BlockSpec(memory_space=pl.ANY)] * count,
        out_specs=[pl.BlockSpec(memory_space=pl.ANY)] * count,
        scratch_shapes=Gather.scratch(shards),
        compiler_params=pltpu.CompilerParams(
            collective_id=collective_id, has_side_effects=True, vmem_limit_bytes=32 << 20
        ),
        name="gather_weights",
    )(*shards)


def run_stages(stages, at_steps):
    for step in sorted(set(at_steps)):

        @pl.when(pl.program_id(0) == step)
        def _():
            for stage, at in zip(stages, at_steps):
                if at == step:
                    stage()


DIMS = ("pair", "high", "low", "bit")
HALVE = (("pair", "bit", "low", "high"), ("bit", "low", "pair", "high"), ("low", "pair", "bit", "high"))
SPREAD = (("high", "bit", "low"), ("high", "low", "bit"), ("high", "bit", "low"))
EVERY = slice(None)


def each_block(free, body):
    if not free:
        body(())
        return

    def step(i, carried):
        body(tuple(lax.rem(i // 2 ** (free - 1 - n), 2) for n in range(free)))
        return carried

    lax.fori_loop(0, 2**free, step, 0)


def cut_parts(shape):
    axis, tile = (1, 128) if shape[1] >= 512 else (0, 16)
    tiles = shape[axis] // tile
    sizes = [(tiles + 2 - k) // 3 * tile for k in range(3)]
    return [(axis, sum(sizes[:k]), sizes[k]) for k in range(3)]


class Reduction:
    def __init__(self, grads, outs, scratch):
        count = len(grads)
        self.grads, self.outs = grads, outs
        self.accs, self.cores, self.fulls = (scratch[i * count : (i + 1) * count] for i in range(3))
        rest = scratch[3 * count :]
        self.arrived = [[[rest[(s * count + a) * 3 + k] for k in range(3)] for a in range(count)] for s in range(4)]
        self.load_sem, self.core_sem, self.half_sem, self.full_sem, self.out_sem = rest[12 * count :]
        self.parts = [cut_parts(g.shape[4:]) for g in grads]
        self.jobs = [(k, a) for k in range(3) for a in range(count)]
        self.own = own_bits()
        self.link = Link(self.own)
        self.stages = [self.begin, self.join, *(functools.partial(self.halved, s) for s in range(4))]
        self.stages += [*(functools.partial(self.spread, s) for s in range(3)), self.end]

    def part(self, k, a):
        axis, start, size = self.parts[a][k]
        return (pl.ds(start, size), EVERY) if axis == 0 else (EVERY, pl.ds(start, size))

    def region(self, chosen, dims, k, a):
        return tuple(chosen.get(d, EVERY) for d in dims) + self.part(k, a)

    def loading(self, k, a, y):
        at = self.region({"pair": y}, DIMS, k, a)
        kept = (2 * y + self.own["core"],) + at[1:]
        return pltpu.make_async_copy(self.grads[a].at[kept], self.accs[a].at[at], self.load_sem.at[a, k, y])

    def begin(self):
        greet(self.own, ("core", "pair", "bit", "low", "high"))
        for k, a in self.jobs:
            for y in range(2):
                self.link.send(functools.partial(self.given, k, a, y))
                self.loading(k, a, y).start()

    def given(self, k, a, y):
        at = self.region({"pair": y}, DIMS, k, a)
        other = (2 * y + 1 - self.own["core"],) + at[1:]
        sems = (self.core_sem.at[0, a, k, y], self.core_sem.at[1, a, k, y])
        return self.grads[a].at[other], self.cores[a].at[at], sems, "core"

    def half(self, k, a, step):
        dim = HALVE[k][step]
        chosen = {d: self.own[d] for d in HALVE[k][:step]}
        chosen[dim] = 1 - self.own[dim]
        sems = (self.half_sem.at[0, a, k, step], self.half_sem.at[1, a, k, step])
        return self.accs[a].at[self.region(chosen, DIMS, k, a)], self.arrived[step][a][k], sems, dim

    def halve(self, k, a, step):
        self.link.send(functools.partial(self.half, k, a, step))

    def join(self):
        for k, a in self.jobs:
            for y in range(2):
                self.loading(k, a, y).wait()
                sems = (self.core_sem.at[0, a, k, y], self.core_sem.at[1, a, k, y])
                self.link.receive(self.cores[a].at[self.region({"pair": y}, DIMS, k, a)], sems, "core")

            def add(lead):
                at = lead + self.part(k, a)
                self.accs[a][at] = self.accs[a][at] + self.cores[a][at]

            each_block(4, add)
            self.halve(k, a, 0)

    def halved(self, step):
        for k, a in self.jobs:
            sems = (self.half_sem.at[0, a, k, step], self.half_sem.at[1, a, k, step])
            self.link.receive(self.arrived[step][a][k], sems, HALVE[k][step])
            chosen = {d: self.own[d] for d in HALVE[k][: step + 1]}
            free = [d for d in DIMS if d not in chosen]

            def add(lead):
                at = tuple(chosen[d] if d in chosen else lead[free.index(d)] for d in DIMS) + self.part(k, a)
                total = self.accs[a][at] + self.arrived[step][a][k][lead + (EVERY, EVERY)]
                if step < 3:
                    self.accs[a][at] = total
                else:
                    self.fulls[a][at[1:]] = total

            each_block(len(free), add)
            if step < 3:
                self.halve(k, a, step + 1)
            else:
                self.pass_on(k, a, 0)

    def held(self, k, a, step):
        chosen = {d: self.own[d] for d in SPREAD[k][step:]}
        here = self.fulls[a].at[self.region(chosen, DIMS[1:], k, a)]
        return here, here, (self.full_sem.at[0, a, k, step], self.full_sem.at[1, a, k, step]), SPREAD[k][step]

    def pass_on(self, k, a, step):
        self.link.send(functools.partial(self.held, k, a, step))

    def spread(self, step):
        for k, a in self.jobs:
            chosen = {d: self.own[d] for d in SPREAD[k][step:]}
            dim = SPREAD[k][step]
            chosen[dim] = 1 - self.own[dim]
            there = self.fulls[a].at[self.region(chosen, DIMS[1:], k, a)]
            self.link.receive(there, (self.full_sem.at[0, a, k, step], self.full_sem.at[1, a, k, step]), dim)
            if step < 2:
                self.pass_on(k, a, step + 1)

    def end(self):
        stores = [
            pltpu.make_async_copy(self.fulls[a], self.outs[a], self.out_sem.at[a]) for a in range(len(self.outs))
        ]
        for copy in stores:
            copy.start()
        for copy in stores:
            copy.wait()
        self.link.finish()

    @staticmethod
    def scratch(grads):
        count = len(grads)
        dma = pltpu.SemaphoreType.DMA
        low = jnp.bfloat16
        shapes = [pltpu.VMEM((2, 2, 2, 2) + g.shape[4:], low) for g in grads] * 2
        shapes += [pltpu.VMEM((2, 2, 2) + g.shape[4:], low) for g in grads]
        for step in range(4):
            for g in grads:
                for axis, _, size in cut_parts(g.shape[4:]):
                    block = (size, g.shape[5]) if axis == 0 else (g.shape[4], size)
                    shapes.append(pltpu.VMEM((2,) * (3 - step) + block, low))
        return shapes + [
            dma((count, 3, 2)),
            dma((2, count, 3, 2)),
            dma((2, count, 3, 4)),
            dma((2, count, 3, 3)),
            dma((count,)),
        ]


def reduce_kernel(count, *refs):
    for stage in Reduction(refs[:count], refs[count : 2 * count], refs[2 * count :]).stages:
        stage()


def reduce_gradients(grads, collective_id):
    count = len(grads)
    return pl.pallas_call(
        functools.partial(reduce_kernel, count),
        out_shape=[jax.ShapeDtypeStruct(g.shape[1:], g.dtype) for g in grads],
        in_specs=[pl.BlockSpec(memory_space=pl.ANY)] * count,
        out_specs=[pl.BlockSpec(memory_space=pl.ANY)] * count,
        scratch_shapes=Reduction.scratch(grads),
        compiler_params=pltpu.CompilerParams(
            collective_id=collective_id, has_side_effects=True, vmem_limit_bytes=56 << 20
        ),
        name="reduce_gradients",
    )(*grads)


def step_selectors(states):
    rows = QLEN * states
    by_token = (
        lax.broadcasted_iota(jnp.int32, (QLEN, rows), 1) // states
        == lax.broadcasted_iota(jnp.int32, (QLEN, rows), 0)
    ).astype(jnp.bfloat16)
    by_state = (
        lax.broadcasted_iota(jnp.int32, (states, rows), 1) % states
        == lax.broadcasted_iota(jnp.int32, (states, rows), 0)
    ).astype(jnp.bfloat16)
    diagonal = lax.broadcasted_iota(jnp.int32, (rows, QLEN), 0) // states == (
        lax.broadcasted_iota(jnp.int32, (rows, QLEN), 1)
    )
    return by_token, by_state, diagonal


def forward_kernel(group, count, dt_ref, feed_ref, b_ref, cblk_ref, rate_ref, *refs):
    shards, (y_ref, h_ref), outs = refs[:count], refs[count : count + 2], refs[count + 2 : 2 * count + 2]
    state, scratch = refs[2 * count + 2], refs[2 * count + 3 :]
    blocks, _, width = dt_ref.shape
    states = rate_ref.shape[0]
    gather = Gather(shards, outs, scratch)
    run_stages(gather.stages[:-1], FORWARD_STEPS)

    @pl.when(pl.program_id(0) == 0)
    def _():
        state[...] = jnp.zeros_like(state)

    def block(j, carried):
        r0 = pl.multiple_of(j * QLEN, QLEN)
        h0 = pl.multiple_of(j * QLEN * states, QLEN * states)
        for c0 in range(0, width, group * LANES):
            columns = [slice(c, c + LANES) for c in range(c0, c0 + group * LANES, LANES)]
            held = [state[:, s] for s in columns]
            rates = [rate_ref[:, s] for s in columns]
            for t in range(QLEN):
                b_t = b_ref[pl.ds(h0 + t * states, states), :]
                for k, s in enumerate(columns):
                    decay = jnp.exp2(dt_ref[j, t : t + 1, s] * rates[k])
                    held[k] = decay * held[k] + b_t * feed_ref[j, t : t + 1, s]
                    h_ref[pl.ds(h0 + t * states, states), s] = held[k].astype(h_ref.dtype)
            for k, s in enumerate(columns):
                state[:, s] = held[k]
            s = slice(c0, c0 + group * LANES)
            y_ref[pl.ds(r0, QLEN), s] = jnp.dot(
                cblk_ref[pl.ds(r0, QLEN), :],
                h_ref[pl.ds(h0, QLEN * states), s],
                preferred_element_type=jnp.float32,
            )
        return carried

    lax.fori_loop(0, blocks, block, 0)
    run_stages(gather.stages[-1:], (pl.num_programs(0) - 1,))


def backward_kernel(
    group,
    count,
    dt_ref,
    feed_ref,
    dy_ref,
    c_ref,
    bblk_ref,
    h_ref,
    before_ref,
    rate2_ref,
    rate_ref,
    *refs,
):
    grads, (e_ref, lrate_ref, ldt_ref, db_ref, dc_ref) = refs[:count], refs[count : count + 5]
    outs = refs[count + 5 : 2 * count + 5]
    message, g_s, lrate_s, ldt_s, before_s = refs[2 * count + 5 : 2 * count + 10]
    blocks, _, width = dt_ref.shape
    states = rate_ref.shape[0]
    reduction = Reduction(grads, outs, refs[2 * count + 10 :])
    early = len(BACKWARD_STEPS)
    run_stages(reduction.stages[:early], BACKWARD_STEPS)
    rows = QLEN * states
    by_token, by_state, diagonal = step_selectors(states)

    @pl.when(pl.program_id(0) == 0)
    def _():
        message[...] = jnp.zeros_like(message)
        ldt_ref[...] = jnp.zeros_like(ldt_ref)

    def block(step, carried):
        j = blocks - 1 - step
        r0 = pl.multiple_of(j * QLEN, QLEN)
        h0 = pl.multiple_of(j * rows, rows)

        @pl.when(j == 0)
        def _():
            before_s[...] = before_ref[...]

        @pl.when(j > 0)
        def _():
            before_s[...] = h_ref[pl.ds(pl.multiple_of(jnp.maximum(h0 - states, 0), states), states), :]

        d_b = jnp.zeros((rows, QLEN), jnp.float32)
        d_c = jnp.zeros((rows, QLEN), jnp.float32)
        for c0 in range(0, width, group * LANES):
            columns = [slice(c, c + LANES) for c in range(c0, c0 + group * LANES, LANES)]
            held = [message[:, s] for s in columns]
            rates2 = [rate2_ref[:, s] for s in columns]
            rates = [rate_ref[:, s] for s in columns]
            for t in reversed(range(QLEN)):
                c_t = c_ref[pl.ds(h0 + t * states, states), :]
                at = slice(t * states, (t + 1) * states)
                for k, s in enumerate(columns):
                    g = c_t * dy_ref[j, t : t + 1, s] + held[k]
                    g_s[at, s] = g.astype(g_s.dtype)
                    dt = dt_ref[j, t : t + 1, s]
                    held[k] = jnp.exp2(dt * rates2[k]) * g
                    before = before_s[:, s] if t == 0 else h_ref[pl.ds(h0 + (t - 1) * states, states), s]
                    l = held[k].astype(jnp.bfloat16) * before
                    lrate_s[at, s] = l * rates[k]
                    ldt_s[at, s] = l * jnp.broadcast_to(dt, (states, LANES)).astype(jnp.bfloat16)
            for k, s in enumerate(columns):
                message[:, s] = held[k]
            s = slice(c0, c0 + group * LANES)
            e_ref[pl.ds(r0, QLEN), s] = jnp.dot(
                bblk_ref[pl.ds(r0, QLEN), :], g_s[:, s], preferred_element_type=jnp.float32
            )
            lrate_ref[pl.ds(r0, QLEN), s] = jnp.dot(
                by_token, lrate_s[:, s], preferred_element_type=jnp.float32
            )
            ldt_ref[:, s] += jnp.dot(by_state, ldt_s[:, s], preferred_element_type=jnp.float32)
            d_b += transposed_product(g_s[:, s], feed_ref[j, :, s].astype(jnp.bfloat16))
            d_c += transposed_product(
                h_ref[pl.ds(h0, rows), s], dy_ref[j, :, s].astype(jnp.bfloat16)
            )
        for total, out_ref in ((d_b, db_ref), (d_c, dc_ref)):
            out_ref[j] = jnp.dot(
                by_state,
                jnp.where(diagonal, total, 0.0).astype(jnp.bfloat16),
                preferred_element_type=jnp.float32,
            )
        return carried

    lax.fori_loop(0, blocks, block, 0)
    late = reduction.stages[early:]
    run_stages(late, (pl.num_programs(0) - 1,) * len(late))


def in_blocks(values):
    return values.reshape((values.shape[0] // QLEN, QLEN) + values.shape[1:])


def over_lanes(values):
    tokens, states = values.shape
    spread = jnp.broadcast_to(values[:, :, None], (tokens, states, LANES))
    return spread.reshape(tokens * states, LANES)


def block_diagonal(values):
    tokens, states = values.shape
    own = jnp.arange(tokens)[:, None] % QLEN == jnp.arange(QLEN * states)[None, :] // states
    return jnp.where(own, jnp.tile(values, (1, QLEN)), 0.0).astype(jnp.bfloat16)


def scan_forward(step_long, feed, b_proj, c_proj, decay_rate, shards, collective_id, blocks=4, group=4):
    count = len(shards)
    anywhere = [pl.BlockSpec(memory_space=pl.ANY)] * count
    tokens, width = feed.shape
    states = decay_rate.shape[0]
    rows = blocks * QLEN
    wide = pl.BlockSpec((blocks, QLEN, width), lambda i: (i, 0, 0))
    y, h, *gathered = pl.pallas_call(
        functools.partial(forward_kernel, group, count),
        grid=(tokens // rows,),
        in_specs=[
            wide,
            wide,
            pl.BlockSpec((rows * states, LANES), lambda i: (i, 0)),
            pl.BlockSpec((rows, QLEN * states), lambda i: (i, 0)),
            pl.BlockSpec((states, width), lambda i: (0, 0)),
            *anywhere,
        ],
        out_specs=[
            pl.BlockSpec((rows, width), lambda i: (i, 0)),
            pl.BlockSpec((rows * states, width), lambda i: (i, 0)),
            *anywhere,
        ],
        out_shape=[
            jax.ShapeDtypeStruct((tokens, width), jnp.float32),
            jax.ShapeDtypeStruct((tokens * states, width), jnp.bfloat16),
            *(gathered_shape(s) for s in shards),
        ],
        scratch_shapes=[pltpu.VMEM((states, width), jnp.float32), *Gather.scratch(shards)],
        compiler_params=pltpu.CompilerParams(
            collective_id=collective_id, has_side_effects=True, vmem_limit_bytes=48 << 20
        ),
        name="scan_forward",
    )(
        in_blocks(step_long),
        in_blocks(feed),
        over_lanes(b_proj),
        block_diagonal(c_proj),
        decay_rate * LOG2E,
        *shards,
    )
    return y, h, gathered


def scan_backward(
    step_long, feed, b_proj, c_proj, d_y, states_kept, decay_rate, grads, collective_id, blocks=2, group=2
):
    count = len(grads)
    anywhere = [pl.BlockSpec(memory_space=pl.ANY)] * count
    tokens, width = feed.shape
    states = decay_rate.shape[0]
    rows = blocks * QLEN
    steps = tokens // rows
    wide = pl.BlockSpec((blocks, QLEN, width), lambda i: (steps - 1 - i, 0, 0))
    flat = lambda i: (steps - 1 - i, 0)
    small = pl.BlockSpec((blocks, states, QLEN), lambda i: (steps - 1 - i, 0, 0))
    whole = pl.BlockSpec((states, width), lambda i: (0, 0))
    small_shape = jax.ShapeDtypeStruct((tokens // QLEN, states, QLEN), jnp.float32)
    held = pltpu.VMEM((QLEN * states, width), jnp.bfloat16)
    e, lrate, ldt, d_b, d_c, *sums = pl.pallas_call(
        functools.partial(backward_kernel, group, count),
        grid=(steps,),
        in_specs=[
            wide,
            wide,
            wide,
            pl.BlockSpec((rows * states, LANES), flat),
            pl.BlockSpec((rows, QLEN * states), flat),
            pl.BlockSpec((rows * states, width), flat),
            pl.BlockSpec((states, width), lambda i: (jnp.maximum((steps - 1 - i) * rows - 1, 0), 0)),
            whole,
            whole,
            *anywhere,
        ],
        out_specs=[
            pl.BlockSpec((rows, width), flat),
            pl.BlockSpec((rows, width), flat),
            whole,
            small,
            small,
            *anywhere,
        ],
        out_shape=[
            jax.ShapeDtypeStruct((tokens, width), jnp.float32),
            jax.ShapeDtypeStruct((tokens, width), jnp.float32),
            jax.ShapeDtypeStruct((states, width), jnp.float32),
            small_shape,
            small_shape,
            *(jax.ShapeDtypeStruct(g.shape[1:], g.dtype) for g in grads),
        ],
        scratch_shapes=[
            pltpu.VMEM((states, width), jnp.float32),
            held,
            held,
            held,
            pltpu.VMEM((states, width), jnp.bfloat16),
            *Reduction.scratch(grads),
        ],
        compiler_params=pltpu.CompilerParams(
            collective_id=collective_id, has_side_effects=True, vmem_limit_bytes=56 << 20
        ),
        name="scan_backward",
    )(
        in_blocks(step_long),
        in_blocks(feed),
        in_blocks(d_y),
        over_lanes(c_proj),
        block_diagonal(b_proj),
        states_kept,
        states_kept,
        decay_rate * LOG2E,
        decay_rate.astype(jnp.bfloat16),
        *grads,
    )
    by_token = lambda v: jnp.swapaxes(v, 1, 2).reshape(tokens, states)
    return e, lrate, ldt, by_token(d_b), by_token(d_c), sums


def add_groups(sums):
    groups = lax.axis_size("dp") // GROUP
    if groups == 1:
        return sums
    alike = [[g * GROUP + i for g in range(groups)] for i in range(GROUP)]
    return lax.psum(sums, "dp", axis_index_groups=alike)


def body(
    tokens,
    cotangent,
    prot_lens,
    clus_start,
    norm_gain,
    in_w,
    conv_w,
    conv_b,
    xproj_w,
    dtproj_w,
    dt_bias,
    a_log,
    d_skip,
    out_w,
):
    rank_width, owned = dtproj_w.shape
    state_width = a_log.shape[0]
    taps = conv_w.shape[0]
    width_by_channel = (
        (dtproj_w, rank_width),
        (a_log, state_width),
        (xproj_w.T, xproj_w.shape[1]),
        (conv_w, taps),
        (conv_b[None], 1),
        (dt_bias[None], 1),
        (d_skip[None], 1),
        (jnp.pad(norm_gain, (0, owned - norm_gain.shape[0]))[None], 1),
    )
    packed = jnp.concatenate([v for v, _ in width_by_channel], axis=0)
    packed = jnp.pad(packed, ((0, -packed.shape[0] % 128), (0, 0)))
    inner_width = in_w.shape[1] // 2
    inner_w, packed = gather_weights((in_w[:, :inner_width], packed), 1)
    inner_w = inner_w.reshape(-1, inner_width)
    gain_full = packed[:, sum(n for _, n in width_by_channel) - 1, : norm_gain.shape[0]].reshape(-1)
    by_channel = jnp.swapaxes(packed, 0, 1).reshape(packed.shape[1], -1)
    unpacked = []
    for _, n in width_by_channel[:-1]:
        unpacked.append(by_channel[:n])
        by_channel = by_channel[n:]
    dtproj_full, alog_full, xproj_full, conv_full, convb_full, dtb_full, skip_full = unpacked
    xproj_full = xproj_full.T
    convb_full, dtb_full, skip_full = convb_full[0], dtb_full[0], skip_full[0]
    length = tokens.shape[0]
    live_mask, same_masks = protein_masks(prot_lens[0], clus_start[0], length, taps)
    keep_mask = same_masks[0]
    x_float = tokens.astype(jnp.float32)
    inv_rms = lax.rsqrt(jnp.mean(x_float * x_float, axis=1, keepdims=True) + EPSILON)
    x_hat = x_float * inv_rms
    normed = (x_hat * gain_full.astype(jnp.float32)).astype(jnp.bfloat16)
    inner_part = jnp.dot(normed, inner_w, preferred_element_type=jnp.float32)
    tap_weights = conv_full.astype(jnp.float32)
    shifted_parts = [
        shifted_down(inner_part, offset) * same_masks[offset - 1][:, None]
        for offset in range(1, taps)
    ]
    conv_pre = convb_full.astype(jnp.float32) + tap_weights[taps - 1] * inner_part
    for offset in range(1, taps):
        conv_pre = conv_pre + tap_weights[taps - 1 - offset] * shifted_parts[offset - 1]
    act_low = jax.nn.silu(conv_pre).astype(jnp.bfloat16)
    act_float = act_low.astype(jnp.float32)
    dbc_rows = jnp.dot(act_low, xproj_full, preferred_element_type=jnp.float32)
    step_rank = dbc_rows[:, :rank_width].astype(jnp.bfloat16)
    b_proj = dbc_rows[:, rank_width : rank_width + state_width]
    c_proj = dbc_rows[:, rank_width + state_width :]
    step_pre = jnp.dot(
        step_rank, dtproj_full, preferred_element_type=jnp.float32
    ) + dtb_full.astype(jnp.float32)
    step_size = jax.nn.softplus(step_pre)
    decay_rate = -jnp.exp(alog_full.astype(jnp.float32))
    feed = step_size * act_float
    step_long = jnp.where(keep_mask[:, None] > 0, step_size, NEVER)
    scanned, states_kept, (gate_w, out_full) = scan_forward(
        step_long, feed, b_proj, c_proj, decay_rate, (in_w[:, inner_width:], out_w), 2
    )
    gate_w = gate_w.reshape(-1, inner_width)
    out_full = out_full.reshape(-1, out_full.shape[2])
    gate_part = jnp.dot(normed, gate_w, preferred_element_type=jnp.float32)
    skip_float = skip_full.astype(jnp.float32)
    y_rows = scanned + skip_float * act_float
    gate_sig = jax.nn.sigmoid(gate_part)
    gate_silu = gate_part * gate_sig
    gated_low = (y_rows * gate_silu).astype(jnp.bfloat16)
    branch = jnp.dot(gated_low, out_full, preferred_element_type=jnp.float32)
    mixed = (x_float + live_mask[:, None] * branch).astype(jnp.bfloat16)
    back_taps = tap_weights
    cot_float = cotangent.astype(jnp.float32)
    d_branch = (live_mask[:, None] * cot_float).astype(jnp.bfloat16)
    out_local = rows_product(gated_low, d_branch)
    d_gated = transposed_product(d_branch, out_full)
    d_y = d_gated * gate_silu
    d_gate = d_gated * y_rows * gate_sig * (1.0 + gate_part * (1.0 - gate_sig))
    skip_local = jnp.sum(d_y * act_float, axis=0)
    d_gate_low = d_gate.astype(jnp.bfloat16)
    gate_local = rows_product(normed, d_gate_low)
    in_pieces = lambda v: v.astype(jnp.bfloat16).reshape((4, 2, 2, 2, v.shape[0] // 32, v.shape[1]))
    grad_feed, grad_step, rate_sum, grad_b, grad_c, early_sums = scan_backward(
        step_long, feed, b_proj, c_proj, d_y, states_kept, decay_rate, [in_pieces(gate_local), in_pieces(out_local)], 3
    )
    alog_local = rate_sum * decay_rate
    d_step = grad_feed * act_float + grad_step
    d_act = d_y * skip_full.astype(jnp.float32) + grad_feed * step_size
    d_step_pre = (d_step * jax.nn.sigmoid(step_pre)).astype(jnp.bfloat16)
    dtb_local = jnp.sum(d_step_pre.astype(jnp.float32), axis=0)
    dtproj_local = rows_product(d_step_pre, step_rank)
    d_rank = transposed_product(d_step_pre, dtproj_full)
    d_dbc = jnp.concatenate([d_rank, grad_b, grad_c], axis=1).astype(jnp.bfloat16)
    xproj_local = rows_product(act_low, d_dbc)
    d_act = d_act + transposed_product(d_dbc, xproj_full)
    pre_sig = jax.nn.sigmoid(conv_pre)
    d_pre = d_act * pre_sig * (1.0 + conv_pre * (1.0 - pre_sig))
    convb_local = jnp.sum(d_pre, axis=0)
    tap_rows = [
        jnp.sum(d_pre * shifted_parts[taps - 2 - index], axis=0) for index in range(taps - 1)
    ]
    tap_rows.append(jnp.sum(d_pre * inner_part, axis=0))
    conv_local = jnp.stack(tap_rows, axis=0)
    d_inner = back_taps[taps - 1] * d_pre
    for offset in range(1, taps):
        d_inner = d_inner + back_taps[taps - 1 - offset] * shifted_up(
            d_pre * same_masks[offset - 1][:, None], offset
        )
    d_inner_low = d_inner.astype(jnp.bfloat16)
    inner_local = rows_product(normed, d_inner_low)
    d_normed = transposed_product(d_inner_low, inner_w) + transposed_product(d_gate_low, gate_w)
    gain_local = jnp.sum(d_normed * x_hat, axis=0)
    d_hat = d_normed * gain_full.astype(jnp.float32)
    token_grad = cot_float + inv_rms * (
        d_hat - x_hat * jnp.mean(d_hat * x_hat, axis=1, keepdims=True)
    )
    gain_rows = jnp.pad(gain_local.reshape(4, -1), ((0, 0), (0, owned - norm_gain.shape[0]))).reshape(-1, 1)
    by_channel = (
        xproj_local,
        dtproj_local,
        alog_local.T,
        conv_local.T,
        convb_local[:, None],
        dtb_local[:, None],
        skip_local[:, None],
        gain_rows,
    )
    small_local = jnp.concatenate([v.astype(jnp.bfloat16) for v in by_channel], axis=1)
    small_local = jnp.pad(small_local, ((0, 0), (0, -small_local.shape[1] % 128)))
    late_sums = reduce_gradients([in_pieces(v) for v in (inner_local, small_local)], 4)
    in_rows = lambda v: v.reshape(-1, v.shape[-1]).astype(jnp.float32)
    gate_grad, out_grad, inner_grad, small = add_groups([in_rows(v) for v in (*early_sums, *late_sums)])
    in_grad = jnp.concatenate([inner_grad, gate_grad], axis=1)
    columns = []
    for v in by_channel:
        columns.append(small[:, : v.shape[1]])
        small = small[:, v.shape[1] :]
    xproj_grad, dtproj_grad, alog_grad, conv_grad, convb_grad, dtb_grad, skip_grad, gain_grad = columns
    dtproj_grad, alog_grad, conv_grad = dtproj_grad.T, alog_grad.T, conv_grad.T
    convb_grad, dtb_grad, skip_grad = convb_grad[:, 0], dtb_grad[:, 0], skip_grad[:, 0]
    gain_grad = gain_grad[: norm_gain.shape[0], 0]
    return (
        mixed,
        token_grad,
        gain_grad,
        in_grad,
        conv_grad,
        convb_grad,
        xproj_grad,
        dtproj_grad,
        dtb_grad,
        alog_grad,
        skip_grad,
        out_grad,
    )


def solution(mesh):
    in_specs = (
        P(("dp", "fsdp"), None),
        P(("dp", "fsdp"), None),
        P(("dp", "fsdp"), None),
        P(("dp", "fsdp"), None),
        P("fsdp"),
        P("fsdp", None),
        P(None, "fsdp"),
        P("fsdp"),
        P("fsdp", None),
        P(None, "fsdp"),
        P("fsdp"),
        P(None, "fsdp"),
        P("fsdp"),
        P("fsdp", None),
    )
    out_specs = (
        P(("dp", "fsdp"), None),
        P(("dp", "fsdp"), None),
        P("fsdp"),
        P("fsdp", None),
        P(None, "fsdp"),
        P("fsdp"),
        P("fsdp", None),
        P(None, "fsdp"),
        P("fsdp"),
        P(None, "fsdp"),
        P("fsdp"),
        P("fsdp", None),
    )
    return jax.shard_map(body, mesh=mesh, in_specs=in_specs, out_specs=out_specs, check_vma=False)
```

```python
import functools

import jax
import jax.numpy as jnp
from jax import lax
from jax.experimental import pallas as pl
from jax.experimental.pallas import tpu as pltpu
from jax.sharding import PartitionSpec as P

QLEN = 16
LANES = 128
WIDE = 256
NEVER = 1e30
LOG2E = 1.4426950408889634
FORWARD_STEPS = (0, 2, 3, 4, 5, 6)
BACKWARD_STEPS = (0, 3, 7, 10, 12, 14, 15)


EPSILON = 1e-05


def shifted_down(values, offset):
    padding = jnp.zeros((offset,) + values.shape[1:], values.dtype)
    return jnp.concatenate([padding, values[:-offset]], axis=0)


def protein_masks(lens_row, start_row, length, taps):
    protein_ends = jnp.cumsum(lens_row)
    protein_begins = protein_ends - lens_row
    flagged = (start_row > 0) & (lens_row > 0)
    position = jnp.arange(length, dtype=jnp.int32)
    cluster = jnp.sum(
        ((position[:, None] >= protein_begins[None, :]) & flagged[None, :]).astype(jnp.int32),
        axis=1,
    )
    live_mask = (position < protein_ends[-1]).astype(jnp.float32)
    same_masks = []
    for offset in range(1, taps):
        matching = (position >= offset) & (cluster == shifted_down(cluster, offset))
        same_masks.append(matching.astype(jnp.float32))
    return (live_mask, same_masks)


def rows_product(left, right):
    return lax.dot_general(
        left, right, (((0,), (0,)), ((), ())), preferred_element_type=jnp.float32
    )


def transposed_product(left, weight):
    return lax.dot_general(
        left, weight, (((1,), (1,)), ((), ())), preferred_element_type=jnp.float32
    )


MESH = pl.DeviceIdType.MESH
GROUP = 8


def own_bits():
    d, f = lax.axis_index("dp"), lax.axis_index("fsdp")
    inside = lax.rem(d, GROUP)
    return {
        "pair": f // 2,
        "core": lax.rem(f, 2),
        "high": inside // 4,
        "low": lax.rem(inside // 2, 2),
        "bit": lax.rem(inside, 2),
    }


def across(own, dim):
    d, f = lax.axis_index("dp"), lax.axis_index("fsdp")
    step = {"pair": 2, "core": 1, "high": 4, "low": 2, "bit": 1}[dim]
    flip = step * (1 - 2 * own[dim])
    return (d, f + flip) if dim in ("pair", "core") else (d + flip, f)


def greet(own, dims):
    barrier = pltpu.get_barrier_semaphore()
    for dim in dims:
        pl.semaphore_signal(barrier, inc=1, device_id=across(own, dim), device_id_type=MESH)
    pl.semaphore_wait(barrier, len(dims))


class Link:
    def __init__(self, own):
        self.own = own
        self.sent = []

    def copy(self, src, dst, sems, dim):
        return pltpu.make_async_remote_copy(
            src_ref=src,
            dst_ref=dst,
            send_sem=sems[0],
            recv_sem=sems[1],
            device_id=across(self.own, dim),
            device_id_type=MESH,
        )

    def send(self, described):
        self.copy(*described()).start()
        self.sent.append(described)

    def receive(self, ref, sems, dim):
        self.copy(ref, ref, sems, dim).wait_recv()

    def finish(self):
        for described in self.sent:
            self.copy(*described()).wait_send()


class Gather:
    def __init__(self, shards, outs, scratch):
        self.shards, self.outs = shards, outs
        self.count = len(shards)
        self.stage = scratch[: self.count]
        self.load_sem, self.core_sem, self.hop_sem, self.whole_sem = scratch[self.count :]
        self.own = own_bits()
        self.link = Link(self.own)
        pair, core = self.own["pair"], self.own["core"]
        self.mine = 2 * pair + core
        self.theirs = 2 * (1 - pair) + core
        self.sibling = 2 * pair + 1 - core
        self.beyond = 2 * (1 - pair) + 1 - core
        bit, low = self.own["bit"], self.own["low"]
        self.kinds = ((bit, low), (1 - bit, low), (bit, 1 - low), (1 - bit, 1 - low))
        self.stages = [self.begin, *(functools.partial(self.from_pair, half) for half in range(2))]
        self.stages += [*(functools.partial(self.from_near, half) for half in range(2)), self.from_far, self.end]

    def eighth(self, a, kind, half):
        rows = self.shards[a].shape[0] // 8
        bit, low = self.kinds[kind]
        return pl.ds(pl.multiple_of((2 * (bit + 2 * low) + half) * rows, rows), rows)

    def hop(self, a, kind, half):
        return self.hop_sem.at[0, a, kind, half], self.hop_sem.at[1, a, kind, half]

    def to_core(self, a, kind, half):
        return self.core_sem.at[0, a, kind, half], self.core_sem.at[1, a, kind, half]

    def whole(self, a):
        return self.whole_sem.at[0, a], self.whole_sem.at[1, a]

    def load(self, a):
        return pltpu.make_async_copy(self.shards[a], self.stage[a], self.load_sem.at[a])

    def store(self, a):
        return pltpu.make_async_copy(self.stage[a], self.outs[a].at[self.mine], self.load_sem.at[a])

    def begin(self):
        greet(self.own, ("core", "pair", "bit", "low"))
        for half in range(2):
            for a in range(self.count):
                self.link.send(functools.partial(self.to_pair, a, half))
        for a in range(self.count):
            self.load(a).start()
            self.link.send(functools.partial(self.own_to_core, a))

    def to_pair(self, a, half):
        rows = self.eighth(a, 0, half)
        return self.shards[a].at[rows], self.outs[a].at[self.mine, rows], self.hop(a, 0, half), "pair"

    def own_to_core(self, a):
        return self.shards[a], self.outs[a].at[self.mine], self.whole(a), "core"

    def came(self, a, kind, half):
        return self.outs[a].at[self.theirs, self.eighth(a, kind, half)]

    def onward(self, a, kind, half, new_kind, dim):
        ref = self.came(a, kind, half)
        return ref, ref, self.to_core(a, kind, half) if dim == "core" else self.hop(a, new_kind, half), dim

    def pass_on(self, a, kind, half, new_kind, dim):
        self.link.send(functools.partial(self.onward, a, kind, half, new_kind, dim))

    def arrive(self, a, kind, half, dim):
        self.link.receive(self.came(a, kind, half), self.hop(a, kind, half), dim)
        self.pass_on(a, kind, half, kind, "core")

    def from_pair(self, half):
        for a in range(self.count):
            self.arrive(a, 0, half, "pair")
            self.pass_on(a, 0, half, 1, "bit")
            self.pass_on(a, 0, half, 2, "low")
        if half == 1:
            for a in range(self.count):
                self.load(a).wait()
                self.store(a).start()

    def from_near(self, half):
        for a in range(self.count):
            self.arrive(a, 1, half, "bit")
            if half == 0:
                self.pass_on(a, 1, 0, 3, "low")
            self.arrive(a, 2, half, "low")
            if half == 1:
                self.pass_on(a, 2, 1, 3, "bit")

    def from_far(self):
        for a in range(self.count):
            self.arrive(a, 3, 0, "low")
            self.arrive(a, 3, 1, "bit")

    def end(self):
        for a in range(self.count):
            self.link.receive(self.outs[a].at[self.sibling], self.whole(a), "core")
            for kind in range(4):
                for half in range(2):
                    ref = self.outs[a].at[self.beyond, self.eighth(a, kind, half)]
                    self.link.receive(ref, self.to_core(a, kind, half), "core")
            self.store(a).wait()
        self.link.finish()

    @staticmethod
    def scratch(shards):
        count = len(shards)
        dma = pltpu.SemaphoreType.DMA
        staged = [pltpu.VMEM(s.shape, s.dtype) for s in shards]
        return staged + [dma((count,)), dma((2, count, 4, 2)), dma((2, count, 4, 2)), dma((2, count))]


def gather_kernel(count, *refs):
    for stage in Gather(refs[:count], refs[count : 2 * count], refs[2 * count :]).stages:
        stage()


def gathered_shape(shard):
    return jax.ShapeDtypeStruct((4,) + shard.shape, shard.dtype)


def gather_weights(shards, collective_id):
    count = len(shards)
    return pl.pallas_call(
        functools.partial(gather_kernel, count),
        out_shape=[gathered_shape(s) for s in shards],
        in_specs=[pl.BlockSpec(memory_space=pl.ANY)] * count,
        out_specs=[pl.BlockSpec(memory_space=pl.ANY)] * count,
        scratch_shapes=Gather.scratch(shards),
        compiler_params=pltpu.CompilerParams(
            collective_id=collective_id, has_side_effects=True, vmem_limit_bytes=32 << 20
        ),
        name="gather_weights",
    )(*shards)


def run_stages(stages, at_steps):
    for step in sorted(set(at_steps)):

        @pl.when(pl.program_id(0) == step)
        def _():
            for stage, at in zip(stages, at_steps):
                if at == step:
                    stage()


DIMS = ("pair", "high", "low", "bit")
HALVE = (("pair", "bit", "low", "high"), ("bit", "low", "pair", "high"), ("low", "pair", "bit", "high"))
SPREAD = (("high", "bit", "low"), ("high", "low", "bit"), ("high", "bit", "low"))
EVERY = slice(None)


def each_block(free, body):
    if not free:
        body(())
        return

    def step(i, carried):
        body(tuple(lax.rem(i // 2 ** (free - 1 - n), 2) for n in range(free)))
        return carried

    lax.fori_loop(0, 2**free, step, 0)


def cut_parts(shape):
    axis, tile = (1, 128) if shape[1] >= 512 else (0, 16)
    tiles = shape[axis] // tile
    sizes = [(tiles + 2 - k) // 3 * tile for k in range(3)]
    return [(axis, sum(sizes[:k]), sizes[k]) for k in range(3)]


class Reduction:
    def __init__(self, grads, outs, scratch):
        count = len(grads)
        self.grads, self.outs = grads, outs
        self.accs, self.cores, self.fulls = (scratch[i * count : (i + 1) * count] for i in range(3))
        rest = scratch[3 * count :]
        self.arrived = [[[rest[(s * count + a) * 3 + k] for k in range(3)] for a in range(count)] for s in range(4)]
        self.load_sem, self.core_sem, self.half_sem, self.full_sem, self.out_sem = rest[12 * count :]
        self.parts = [cut_parts(g.shape[4:]) for g in grads]
        self.jobs = [(k, a) for k in range(3) for a in range(count)]
        self.own = own_bits()
        self.link = Link(self.own)
        self.stages = [self.begin, self.join, *(functools.partial(self.halved, s) for s in range(4))]
        self.stages += [*(functools.partial(self.spread, s) for s in range(3)), self.end]

    def part(self, k, a):
        axis, start, size = self.parts[a][k]
        return (pl.ds(start, size), EVERY) if axis == 0 else (EVERY, pl.ds(start, size))

    def region(self, chosen, dims, k, a):
        return tuple(chosen.get(d, EVERY) for d in dims) + self.part(k, a)

    def loading(self, k, a, y):
        at = self.region({"pair": y}, DIMS, k, a)
        kept = (2 * y + self.own["core"],) + at[1:]
        return pltpu.make_async_copy(self.grads[a].at[kept], self.accs[a].at[at], self.load_sem.at[a, k, y])

    def begin(self):
        greet(self.own, ("core", "pair", "bit", "low", "high"))
        for k, a in self.jobs:
            for y in range(2):
                self.link.send(functools.partial(self.given, k, a, y))
                self.loading(k, a, y).start()

    def given(self, k, a, y):
        at = self.region({"pair": y}, DIMS, k, a)
        other = (2 * y + 1 - self.own["core"],) + at[1:]
        sems = (self.core_sem.at[0, a, k, y], self.core_sem.at[1, a, k, y])
        return self.grads[a].at[other], self.cores[a].at[at], sems, "core"

    def half(self, k, a, step):
        dim = HALVE[k][step]
        chosen = {d: self.own[d] for d in HALVE[k][:step]}
        chosen[dim] = 1 - self.own[dim]
        sems = (self.half_sem.at[0, a, k, step], self.half_sem.at[1, a, k, step])
        return self.accs[a].at[self.region(chosen, DIMS, k, a)], self.arrived[step][a][k], sems, dim

    def halve(self, k, a, step):
        self.link.send(functools.partial(self.half, k, a, step))

    def join(self):
        for k, a in self.jobs:
            for y in range(2):
                self.loading(k, a, y).wait()
                sems = (self.core_sem.at[0, a, k, y], self.core_sem.at[1, a, k, y])
                self.link.receive(self.cores[a].at[self.region({"pair": y}, DIMS, k, a)], sems, "core")

            def add(lead):
                at = lead + self.part(k, a)
                self.accs[a][at] = self.accs[a][at] + self.cores[a][at]

            each_block(4, add)
            self.halve(k, a, 0)

    def halved(self, step):
        for k, a in self.jobs:
            sems = (self.half_sem.at[0, a, k, step], self.half_sem.at[1, a, k, step])
            self.link.receive(self.arrived[step][a][k], sems, HALVE[k][step])
            chosen = {d: self.own[d] for d in HALVE[k][: step + 1]}
            free = [d for d in DIMS if d not in chosen]

            def add(lead):
                at = tuple(chosen[d] if d in chosen else lead[free.index(d)] for d in DIMS) + self.part(k, a)
                total = self.accs[a][at] + self.arrived[step][a][k][lead + (EVERY, EVERY)]
                if step < 3:
                    self.accs[a][at] = total
                else:
                    self.fulls[a][at[1:]] = total

            each_block(len(free), add)
            if step < 3:
                self.halve(k, a, step + 1)
            else:
                self.pass_on(k, a, 0)

    def held(self, k, a, step):
        chosen = {d: self.own[d] for d in SPREAD[k][step:]}
        here = self.fulls[a].at[self.region(chosen, DIMS[1:], k, a)]
        return here, here, (self.full_sem.at[0, a, k, step], self.full_sem.at[1, a, k, step]), SPREAD[k][step]

    def pass_on(self, k, a, step):
        self.link.send(functools.partial(self.held, k, a, step))

    def spread(self, step):
        for k, a in self.jobs:
            chosen = {d: self.own[d] for d in SPREAD[k][step:]}
            dim = SPREAD[k][step]
            chosen[dim] = 1 - self.own[dim]
            there = self.fulls[a].at[self.region(chosen, DIMS[1:], k, a)]
            self.link.receive(there, (self.full_sem.at[0, a, k, step], self.full_sem.at[1, a, k, step]), dim)
            if step < 2:
                self.pass_on(k, a, step + 1)

    def end(self):
        stores = [
            pltpu.make_async_copy(self.fulls[a], self.outs[a], self.out_sem.at[a]) for a in range(len(self.outs))
        ]
        for copy in stores:
            copy.start()
        for copy in stores:
            copy.wait()
        self.link.finish()

    @staticmethod
    def scratch(grads):
        count = len(grads)
        dma = pltpu.SemaphoreType.DMA
        low = jnp.bfloat16
        shapes = [pltpu.VMEM((2, 2, 2, 2) + g.shape[4:], low) for g in grads] * 2
        shapes += [pltpu.VMEM((2, 2, 2) + g.shape[4:], low) for g in grads]
        for step in range(4):
            for g in grads:
                for axis, _, size in cut_parts(g.shape[4:]):
                    block = (size, g.shape[5]) if axis == 0 else (g.shape[4], size)
                    shapes.append(pltpu.VMEM((2,) * (3 - step) + block, low))
        return shapes + [
            dma((count, 3, 2)),
            dma((2, count, 3, 2)),
            dma((2, count, 3, 4)),
            dma((2, count, 3, 3)),
            dma((count,)),
        ]


def reduce_kernel(count, *refs):
    for stage in Reduction(refs[:count], refs[count : 2 * count], refs[2 * count :]).stages:
        stage()


def reduce_gradients(grads, collective_id):
    count = len(grads)
    return pl.pallas_call(
        functools.partial(reduce_kernel, count),
        out_shape=[jax.ShapeDtypeStruct(g.shape[1:], g.dtype) for g in grads],
        in_specs=[pl.BlockSpec(memory_space=pl.ANY)] * count,
        out_specs=[pl.BlockSpec(memory_space=pl.ANY)] * count,
        scratch_shapes=Reduction.scratch(grads),
        compiler_params=pltpu.CompilerParams(
            collective_id=collective_id, has_side_effects=True, vmem_limit_bytes=56 << 20
        ),
        name="reduce_gradients",
    )(*grads)


def block_rows(values, row, rows):
    return values[row : row + 1, :]


def lane_index(shape):
    return lax.broadcasted_iota(jnp.int32, shape, 1)


def dot(left, right):
    return jnp.dot(left, right, preferred_element_type=jnp.float32)


def smooth(values):
    share = jax.nn.sigmoid(values)
    return values * share, share


TAPS = 4
BIAS_ROW, STEP_ROW, SKIP_ROW = 4, 5, 6


def front_kernel(tokens_ref, gain_ref, w_ref, rows_ref, xproj_ref, mask_ref, inner_ref, pre_ref, u_ref, dbc_ref, xn_ref, xnt_ref):
    @pl.when(pl.program_id(0) == 0)
    def _():
        x = tokens_ref[...].astype(jnp.float32)
        inv = lax.rsqrt(jnp.mean(x * x, axis=1, keepdims=True) + EPSILON)
        xn = (x * inv * gain_ref[...]).astype(jnp.bfloat16)
        xn_ref[...] = xn
        xnt_ref[...] = xn.T
        dbc_ref[...] = jnp.zeros_like(dbc_ref)

    inner = dot(xn_ref[...], w_ref[...])
    rows = rows_ref[...]
    pre = block_rows(rows, BIAS_ROW, 1) + block_rows(rows, TAPS - 1, 1) * inner
    for offset in range(1, TAPS):
        shifted = pltpu.roll(inner, offset, 0) * mask_ref[:, offset : offset + 1]
        pre = pre + block_rows(rows, TAPS - 1 - offset, 1) * shifted
    u = smooth(pre)[0].astype(jnp.bfloat16)
    inner_ref[...] = inner.astype(inner_ref.dtype)
    pre_ref[...] = pre
    u_ref[...] = u
    dbc_ref[...] += transposed_product(u, xproj_ref[...])


def whole_spec(shape):
    return pl.BlockSpec(shape, lambda i: (0,) * len(shape))


def columns_spec(rows, block):
    return pl.BlockSpec((rows, block), lambda i: (0, i))


def rows_spec(block, columns):
    return pl.BlockSpec((block, columns), lambda i: (i, 0))


def front(tokens, gain, inner_w, by_channel, xproj_t, masks, block=256):
    length, features = tokens.shape
    width = inner_w.shape[1]
    low, wide = jnp.bfloat16, jnp.float32
    return pl.pallas_call(
        front_kernel,
        grid=(width // block,),
        in_specs=[
            whole_spec(tokens.shape),
            whole_spec(gain.shape),
            columns_spec(features, block),
            columns_spec(by_channel.shape[0], block),
            columns_spec(LANES, block),
            whole_spec(masks.shape),
        ],
        out_specs=[
            columns_spec(length, block),
            columns_spec(length, block),
            columns_spec(length, block),
            whole_spec((length, LANES)),
            whole_spec((length, features)),
            whole_spec((features, length)),
        ],
        out_shape=[
            jax.ShapeDtypeStruct((length, width), low),
            jax.ShapeDtypeStruct((length, width), wide),
            jax.ShapeDtypeStruct((length, width), low),
            jax.ShapeDtypeStruct((length, LANES), wide),
            jax.ShapeDtypeStruct((length, features), low),
            jax.ShapeDtypeStruct((features, length), low),
        ],
        compiler_params=pltpu.CompilerParams(vmem_limit_bytes=48 << 20),
        name="front",
    )(tokens, gain, inner_w, by_channel, xproj_t, masks)


def spread_states(dbc, first, states):
    rows = QLEN * states
    repeated = jnp.broadcast_to(dbc[:, None, :], (QLEN, states, LANES)).reshape(rows, LANES)
    state = lax.broadcasted_iota(jnp.int32, (rows, LANES), 0) % states
    own = jnp.where(lane_index((rows, LANES)) == first + state, repeated, 0.0)
    return jnp.broadcast_to(jnp.sum(own, axis=1, keepdims=True), (rows, LANES))


def diagonal_states(dbc, first, states):
    rows = QLEN * states
    pick = (
        lax.broadcasted_iota(jnp.int32, (LANES, rows), 0) == first + lane_index((LANES, rows)) % states
    ).astype(jnp.bfloat16)
    tiled = dot(dbc.astype(jnp.bfloat16), pick)
    own = lane_index((QLEN, rows)) // states == lax.broadcasted_iota(jnp.int32, (QLEN, rows), 0)
    return jnp.where(own, tiled, 0.0).astype(jnp.bfloat16)


def step_rank(dbc, rank):
    return jnp.where(lane_index(dbc.shape) < rank, dbc, 0.0).astype(jnp.bfloat16)


def twice(values):
    return jnp.concatenate([values] * (WIDE // LANES), axis=1)


def forward_kernel(rank, group, count, u_ref, dbc_ref, mask_ref, rows_ref, dtproj_ref, rate_ref, *refs):
    shards, (y_ref, h_ref, dt_ref), outs = refs[:count], refs[count : count + 3], refs[count + 3 : 2 * count + 3]
    (state, long_s, feed_s, b_s, cblk_s), scratch = refs[2 * count + 3 : 2 * count + 8], refs[2 * count + 8 :]
    blocks, _, width = long_s.shape
    states = rate_ref.shape[0]
    span = QLEN * states
    gather = Gather(shards, outs, scratch)
    run_stages(gather.stages[:-1], FORWARD_STEPS)

    @pl.when(pl.program_id(0) == 0)
    def _():
        state[...] = jnp.zeros_like(state)

    rank_rows = step_rank(dbc_ref[...], rank)
    keep = mask_ref[:, 1:2] > 0
    for c in range(0, width, WIDE):
        s = slice(c, c + WIDE)
        dt = jax.nn.softplus(dot(rank_rows, dtproj_ref[:, s]) + rows_ref[STEP_ROW : STEP_ROW + 1, s])
        dt_ref[:, s] = dt
        long = jnp.where(keep, dt, NEVER)
        feed = dt * u_ref[:, s].astype(jnp.float32)
        for j in range(blocks):
            long_s[j, :, s] = long[j * QLEN : (j + 1) * QLEN]
            feed_s[j, :, s] = feed[j * QLEN : (j + 1) * QLEN]
    for j in range(blocks):
        dbc = dbc_ref[j * QLEN : (j + 1) * QLEN, :]
        b_s[j * span : (j + 1) * span, :] = spread_states(dbc, rank, states)
        cblk_s[j * QLEN : (j + 1) * QLEN, :] = diagonal_states(dbc, rank + states, states)

    def block(j, carried):
        r0 = pl.multiple_of(j * QLEN, QLEN)
        h0 = pl.multiple_of(j * span, span)
        for c0 in range(0, width, group * WIDE):
            columns = [slice(c, c + WIDE) for c in range(c0, c0 + group * WIDE, WIDE)]
            held = [state[:, s] for s in columns]
            rates = [rate_ref[:, s] for s in columns]
            for t in range(QLEN):
                b_t = twice(b_s[pl.ds(h0 + t * states, states), :])
                for k, s in enumerate(columns):
                    decay = jnp.exp2(long_s[j, t : t + 1, s] * rates[k])
                    held[k] = decay * held[k] + b_t * feed_s[j, t : t + 1, s]
                    h_ref[pl.ds(h0 + t * states, states), s] = held[k].astype(h_ref.dtype)
            for k, s in enumerate(columns):
                state[:, s] = held[k]
            s = slice(c0, c0 + group * WIDE)
            y_ref[pl.ds(r0, QLEN), s] = dot(cblk_s[pl.ds(r0, QLEN), :], h_ref[pl.ds(h0, span), s])
        return carried

    lax.fori_loop(0, blocks, block, 0)
    run_stages(gather.stages[-1:], (pl.num_programs(0) - 1,))


def scan_forward(rank, u, dbc, masks, by_channel, dtproj, rate2, shards, collective_id, blocks=2, group=2):
    count = len(shards)
    anywhere = [pl.BlockSpec(memory_space=pl.ANY)] * count
    tokens, width = u.shape
    states = rate2.shape[0]
    rows = blocks * QLEN
    y, h, dt, *gathered = pl.pallas_call(
        functools.partial(forward_kernel, rank, group, count),
        grid=(tokens // rows,),
        in_specs=[
            rows_spec(rows, width),
            rows_spec(rows, LANES),
            rows_spec(rows, masks.shape[1]),
            whole_spec(by_channel.shape),
            whole_spec(dtproj.shape),
            whole_spec(rate2.shape),
            *anywhere,
        ],
        out_specs=[rows_spec(rows, width), rows_spec(rows * states, width), rows_spec(rows, width), *anywhere],
        out_shape=[
            jax.ShapeDtypeStruct((tokens, width), jnp.float32),
            jax.ShapeDtypeStruct((tokens * states, width), jnp.bfloat16),
            jax.ShapeDtypeStruct((tokens, width), jnp.float32),
            *(gathered_shape(s) for s in shards),
        ],
        scratch_shapes=[
            pltpu.VMEM((states, width), jnp.float32),
            pltpu.VMEM((blocks, QLEN, width), jnp.float32),
            pltpu.VMEM((blocks, QLEN, width), jnp.float32),
            pltpu.VMEM((rows * states, LANES), jnp.float32),
            pltpu.VMEM((rows, QLEN * states), jnp.bfloat16),
            *Gather.scratch(shards),
        ],
        compiler_params=pltpu.CompilerParams(
            collective_id=collective_id, has_side_effects=True, vmem_limit_bytes=48 << 20
        ),
        name="scan_forward",
    )(u, dbc, masks, by_channel, dtproj, rate2, *shards)
    return y, h, dt, gathered


def middle_kernel(
    xn_ref, xnt_ref, gate_ref, y_ref, u_ref, rows_ref, out_ref, cot_ref, tokens_ref, mask_ref,
    mixed_ref, dy_ref, dgate_ref, outgrad_ref, gategrad_ref, skip_ref, dxn_ref, branch, dbranch
):
    live = mask_ref[:, 0:1]

    @pl.when(pl.program_id(0) == 0)
    def _():
        branch[...] = jnp.zeros_like(branch)
        dxn_ref[...] = jnp.zeros_like(dxn_ref)
        dbranch[...] = (live * cot_ref[...].astype(jnp.float32)).astype(jnp.bfloat16)

    gate = dot(xn_ref[...], gate_ref[...])
    opened, share = smooth(gate)
    u = u_ref[...].astype(jnp.float32)
    y = y_ref[...] + rows_ref[SKIP_ROW : SKIP_ROW + 1, :] * u
    gated = (y * opened).astype(jnp.bfloat16)
    d_branch = dbranch[...]
    branch[...] += dot(gated, out_ref[...])
    outgrad_ref[...] = rows_product(gated, d_branch).astype(outgrad_ref.dtype)
    d_gated = transposed_product(d_branch, out_ref[...])
    d_y = d_gated * opened
    dy_ref[...] = d_y
    skip_ref[...] = jnp.sum(d_y * u, axis=0, keepdims=True)
    d_gate = (d_gated * y * share * (1.0 + gate * (1.0 - share))).astype(jnp.bfloat16)
    dgate_ref[...] = d_gate
    gategrad_ref[...] = dot(xnt_ref[...], d_gate).astype(gategrad_ref.dtype)
    dxn_ref[...] += transposed_product(d_gate, gate_ref[...])

    @pl.when(pl.program_id(0) == pl.num_programs(0) - 1)
    def _():
        mixed_ref[...] = (tokens_ref[...].astype(jnp.float32) + live * branch[...]).astype(mixed_ref.dtype)


def middle(xn, xnt, gate_w, y, u, by_channel, out_w, cotangent, tokens, masks, block=256):
    length, features = tokens.shape
    width = gate_w.shape[1]
    low, wide = jnp.bfloat16, jnp.float32
    channels = columns_spec(length, block)
    return pl.pallas_call(
        middle_kernel,
        grid=(width // block,),
        in_specs=[
            whole_spec(xn.shape),
            whole_spec(xnt.shape),
            columns_spec(features, block),
            channels,
            channels,
            columns_spec(by_channel.shape[0], block),
            rows_spec(block, features),
            whole_spec(tokens.shape),
            whole_spec(tokens.shape),
            whole_spec(masks.shape),
        ],
        out_specs=[
            whole_spec(tokens.shape),
            channels,
            channels,
            rows_spec(block, features),
            columns_spec(features, block),
            columns_spec(1, block),
            whole_spec(tokens.shape),
        ],
        out_shape=[
            jax.ShapeDtypeStruct(tokens.shape, low),
            jax.ShapeDtypeStruct((length, width), wide),
            jax.ShapeDtypeStruct((length, width), low),
            jax.ShapeDtypeStruct((width, features), low),
            jax.ShapeDtypeStruct((features, width), low),
            jax.ShapeDtypeStruct((1, width), wide),
            jax.ShapeDtypeStruct(tokens.shape, wide),
        ],
        scratch_shapes=[pltpu.VMEM(tokens.shape, wide), pltpu.VMEM(tokens.shape, low)],
        compiler_params=pltpu.CompilerParams(vmem_limit_bytes=56 << 20),
        name="middle",
    )(xn, xnt, gate_w, y, u, by_channel, out_w, cotangent, tokens, masks)


def backward_kernel(rank, count, u_ref, dt_ref, dy_ref, dbc_ref, mask_ref, h_ref, before_ref, rows_ref, dtproj_ref, rate2_ref, rate_ref, *refs):
    grads, (du_ref, ddbc_ref, ldt_ref, dtproj_grad, bias_grad) = refs[:count], refs[count : count + 5]
    outs, refs = refs[count + 5 : 2 * count + 5], refs[2 * count + 5 :]
    message, long_s, feed_s, c_s, bblk_s, g_s, lrate_s, db_s, dc_s, before_s, e_s, lsum_s, small_s = refs[:13]
    blocks, _, width = dt_ref.shape
    states = rate_ref.shape[0]
    span = QLEN * states
    low, wide = jnp.bfloat16, jnp.float32
    reduction = Reduction(grads, outs, refs[13:])
    early = len(BACKWARD_STEPS)
    run_stages(reduction.stages[:early], BACKWARD_STEPS)

    @pl.when(pl.program_id(0) == 0)
    def _():
        message[...] = jnp.zeros_like(message)
        ldt_ref[...] = jnp.zeros_like(ldt_ref)
        dtproj_grad[...] = jnp.zeros_like(dtproj_grad)
        bias_grad[...] = jnp.zeros_like(bias_grad)

    for j in range(blocks):
        own = slice(j * QLEN, (j + 1) * QLEN)
        keep = mask_ref[own, 1:2] > 0
        for c in range(0, width, WIDE):
            s = slice(c, c + WIDE)
            dt = dt_ref[j, :, s]
            long_s[j, :, s] = jnp.where(keep, dt, NEVER)
            feed_s[j, :, s] = dt * u_ref[own, s].astype(wide)
        dbc = dbc_ref[own, :]
        c_s[j * span : (j + 1) * span, :] = spread_states(dbc, rank + states, states)
        bblk_s[own, :] = diagonal_states(dbc, rank, states)
    by_token = (
        lane_index((QLEN, span)) // states == lax.broadcasted_iota(jnp.int32, (QLEN, span), 0)
    ).astype(low)
    state_of = lax.broadcasted_iota(jnp.int32, (span, LANES), 0) % states
    at_b = lane_index((span, LANES)) == rank + state_of
    at_c = lane_index((span, LANES)) == rank + states + state_of

    def block(step, carried):
        j = blocks - 1 - step
        r0 = pl.multiple_of(j * QLEN, QLEN)
        h0 = pl.multiple_of(j * span, span)

        @pl.when(j == 0)
        def _():
            before_s[...] = before_ref[...]

        @pl.when(j > 0)
        def _():
            before_s[...] = h_ref[pl.ds(pl.multiple_of(jnp.maximum(h0 - states, 0), states), states), :]

        db_s[...] = jnp.zeros_like(db_s)
        dc_s[...] = jnp.zeros_like(dc_s)
        for c in range(0, width, WIDE):
            s = slice(c, c + WIDE)
            held, rate2, rate, total = message[:, s], rate2_ref[:, s], rate_ref[:, s], ldt_ref[:, s]
            pending = None
            now = h_ref[pl.ds(h0 + (QLEN - 1) * states, states), s]
            for t in reversed(range(QLEN)):
                at = slice(t * states, (t + 1) * states)
                d_y = jnp.broadcast_to(dy_ref[j, t : t + 1, s], (states, WIDE))
                g = twice(c_s[pl.ds(h0 + t * states, states), :]) * d_y + held
                g_low = g.astype(low)
                g_s[at, s] = g_low
                dt = jnp.broadcast_to(long_s[j, t : t + 1, s], (states, WIDE))
                held = jnp.exp2(dt * rate2) * g
                before = before_s[:, s] if t == 0 else h_ref[pl.ds(h0 + (t - 1) * states, states), s]
                l = held.astype(low) * before
                lrate_s[at, s] = l * rate
                ldt = l * dt.astype(low)
                if pending is None:
                    pending = ldt
                else:
                    total = total + (pending + ldt).astype(wide)
                    pending = None
                feed = jnp.broadcast_to(feed_s[j, t : t + 1, s], (states, WIDE))
                for sums, product in ((db_s, g_low * feed.astype(low)), (dc_s, now * d_y.astype(low))):
                    sums[at, :] += (product[:, :LANES] + product[:, LANES:]).astype(wide)
                now = before
            message[:, s] = held
            ldt_ref[:, s] = total
            e_s[pl.ds(r0, QLEN), s] = dot(bblk_s[pl.ds(r0, QLEN), :], g_s[:, s])
            lsum_s[pl.ds(r0, QLEN), s] = dot(by_token, lrate_s[:, s])
        d_b = jnp.sum(db_s[...], axis=1, keepdims=True)
        d_c = jnp.sum(dc_s[...], axis=1, keepdims=True)
        placed = jnp.where(at_b, d_b, jnp.where(at_c, d_c, 0.0)).astype(low)
        small_s[pl.ds(r0, QLEN), :] = dot(by_token, placed)
        return carried

    lax.fori_loop(0, blocks, block, 0)
    rank_rows = step_rank(dbc_ref[...], rank)
    d_rank = jnp.zeros(rank_rows.shape, wide)
    tokens = blocks * QLEN
    for c in range(0, width, WIDE):
        s = slice(c, c + WIDE)
        dt = dt_ref[:, :, s].reshape(tokens, WIDE)
        d_y = dy_ref[:, :, s].reshape(tokens, WIDE)
        e = e_s[:, s]
        share = jnp.where(dt < 0.01, dt * (1.0 - dt * (0.5 - dt * (1.0 / 6.0))), 1.0 - jnp.exp(-dt))
        d_dt = e * u_ref[:, s].astype(wide) + lsum_s[:, s]
        d_step = (d_dt * share).astype(low)
        bias_grad[:, s] += jnp.sum(d_step.astype(wide), axis=0, keepdims=True)
        dtproj_grad[:, s] += rows_product(rank_rows, d_step)
        d_rank += transposed_product(d_step, dtproj_ref[:, s])
        du_ref[:, s] = d_y * rows_ref[SKIP_ROW : SKIP_ROW + 1, s] + e * dt
    ddbc_ref[...] = (jnp.where(lane_index(d_rank.shape) < rank, d_rank, 0.0) + small_s[...]).astype(low)
    late = reduction.stages[early:]
    run_stages(late, (pl.num_programs(0) - 1,) * len(late))


def scan_backward(rank, u, dt, d_y, dbc, masks, h, by_channel, dtproj, rate2, rate, grads, collective_id, blocks=2):
    count = len(grads)
    anywhere = [pl.BlockSpec(memory_space=pl.ANY)] * count
    tokens, width = u.shape
    states = rate2.shape[0]
    rows = blocks * QLEN
    steps = tokens // rows
    low, wide = jnp.bfloat16, jnp.float32
    back = lambda i: (steps - 1 - i, 0)
    flat = lambda columns: pl.BlockSpec((rows, columns), back)
    cubes = pl.BlockSpec((blocks, QLEN, width), lambda i: (steps - 1 - i, 0, 0))
    in_blocks = lambda v: v.reshape(tokens // QLEN, QLEN, width)
    du, ddbc, ldt, dtproj_grad, bias_grad, *sums = pl.pallas_call(
        functools.partial(backward_kernel, rank, count),
        grid=(steps,),
        in_specs=[
            flat(width),
            cubes,
            cubes,
            flat(LANES),
            flat(masks.shape[1]),
            pl.BlockSpec((rows * states, width), back),
            pl.BlockSpec((states, width), lambda i: (jnp.maximum((steps - 1 - i) * rows - 1, 0), 0)),
            whole_spec(by_channel.shape),
            whole_spec(dtproj.shape),
            whole_spec(rate2.shape),
            whole_spec(rate.shape),
            *anywhere,
        ],
        out_specs=[
            flat(width),
            flat(LANES),
            whole_spec(rate2.shape),
            whole_spec(dtproj.shape),
            whole_spec((1, width)),
            *anywhere,
        ],
        out_shape=[
            jax.ShapeDtypeStruct((tokens, width), wide),
            jax.ShapeDtypeStruct((tokens, LANES), low),
            jax.ShapeDtypeStruct(rate2.shape, wide),
            jax.ShapeDtypeStruct(dtproj.shape, wide),
            jax.ShapeDtypeStruct((1, width), wide),
            *(jax.ShapeDtypeStruct(g.shape[1:], g.dtype) for g in grads),
        ],
        scratch_shapes=[
            pltpu.VMEM((states, width), wide),
            pltpu.VMEM((blocks, QLEN, width), wide),
            pltpu.VMEM((blocks, QLEN, width), wide),
            pltpu.VMEM((rows * states, LANES), wide),
            pltpu.VMEM((rows, QLEN * states), low),
            pltpu.VMEM((QLEN * states, width), low),
            pltpu.VMEM((QLEN * states, width), low),
            pltpu.VMEM((QLEN * states, LANES), wide),
            pltpu.VMEM((QLEN * states, LANES), wide),
            pltpu.VMEM((states, width), low),
            pltpu.VMEM((rows, width), wide),
            pltpu.VMEM((rows, width), wide),
            pltpu.VMEM((rows, LANES), wide),
            *Reduction.scratch(grads),
        ],
        compiler_params=pltpu.CompilerParams(
            collective_id=collective_id, has_side_effects=True, vmem_limit_bytes=56 << 20
        ),
        name="scan_backward",
    )(u, in_blocks(dt), in_blocks(d_y), dbc, masks, h, h, by_channel, dtproj, rate2, rate, *grads)
    return du, ddbc, ldt, dtproj_grad, bias_grad, sums


def tail_kernel(
    du_ref, ddbc_ref, xproj_ref, u_ref, inner_ref, pre_ref, rows_ref, mask_ref, xnt_ref, w_ref, dgate_ref, tokens_ref, cot_ref, gain_ref,
    innergrad_ref, xprojgrad_ref, rowgrad_ref, tokengrad_ref, gaingrad_ref, dxn
):
    wide = jnp.float32

    @pl.when(pl.program_id(0) == 0)
    def _():
        dxn[...] = dgate_ref[...]

    rows = rows_ref[...]
    pre = pre_ref[...]
    share = jax.nn.sigmoid(pre)
    d_u = du_ref[...] + dot(ddbc_ref[...], xproj_ref[...])
    d_pre = d_u * share * (1.0 + pre * (1.0 - share))
    inner = inner_ref[...].astype(wide)
    d_inner = block_rows(rows, TAPS - 1, 1) * d_pre
    sums = [None] * 8
    sums[TAPS - 1] = jnp.sum(d_pre * inner, axis=0, keepdims=True)
    sums[BIAS_ROW] = jnp.sum(d_pre, axis=0, keepdims=True)
    for offset in range(1, TAPS):
        same = d_pre * mask_ref[:, offset : offset + 1]
        back = pltpu.roll(same, same.shape[0] - offset, 0)
        sums[TAPS - 1 - offset] = jnp.sum(back * inner, axis=0, keepdims=True)
        d_inner = d_inner + block_rows(rows, TAPS - 1 - offset, 1) * back
    nothing = jnp.zeros_like(sums[0])
    rowgrad_ref[...] = jnp.concatenate([nothing if v is None else v for v in sums], axis=0)
    xprojgrad_ref[...] = rows_product(ddbc_ref[...], u_ref[...])
    d_inner = d_inner.astype(jnp.bfloat16)
    innergrad_ref[...] = dot(xnt_ref[...], d_inner).astype(innergrad_ref.dtype)
    dxn[...] += transposed_product(d_inner, w_ref[...])

    @pl.when(pl.program_id(0) == pl.num_programs(0) - 1)
    def _():
        x = tokens_ref[...].astype(wide)
        inv = lax.rsqrt(jnp.mean(x * x, axis=1, keepdims=True) + EPSILON)
        x_hat = x * inv
        gaingrad_ref[...] = jnp.sum(dxn[...] * x_hat, axis=0, keepdims=True)
        d_hat = dxn[...] * gain_ref[...]
        level = jnp.mean(d_hat * x_hat, axis=1, keepdims=True)
        tokengrad_ref[...] = cot_ref[...].astype(wide) + inv * (d_hat - x_hat * level)


def tail(du, ddbc, xproj_t, u, inner, pre, by_channel, masks, xnt, inner_w, dxn_gate, tokens, cotangent, gain, block=256):
    length, features = tokens.shape
    width = inner_w.shape[1]
    low, wide = jnp.bfloat16, jnp.float32
    channels = columns_spec(length, block)
    return pl.pallas_call(
        tail_kernel,
        grid=(width // block,),
        in_specs=[
            channels,
            whole_spec(ddbc.shape),
            columns_spec(LANES, block),
            channels,
            channels,
            channels,
            columns_spec(by_channel.shape[0], block),
            whole_spec(masks.shape),
            whole_spec(xnt.shape),
            columns_spec(features, block),
            whole_spec(dxn_gate.shape),
            whole_spec(tokens.shape),
            whole_spec(tokens.shape),
            whole_spec(gain.shape),
        ],
        out_specs=[
            columns_spec(features, block),
            columns_spec(LANES, block),
            columns_spec(8, block),
            whole_spec(tokens.shape),
            whole_spec((1, features)),
        ],
        out_shape=[
            jax.ShapeDtypeStruct((features, width), low),
            jax.ShapeDtypeStruct((LANES, width), wide),
            jax.ShapeDtypeStruct((8, width), wide),
            jax.ShapeDtypeStruct(tokens.shape, wide),
            jax.ShapeDtypeStruct((1, features), wide),
        ],
        scratch_shapes=[pltpu.VMEM(tokens.shape, wide)],
        compiler_params=pltpu.CompilerParams(vmem_limit_bytes=56 << 20),
        name="tail",
    )(du, ddbc, xproj_t, u, inner, pre, by_channel, masks, xnt, inner_w, dxn_gate, tokens, cotangent, gain)


def add_groups(sums):
    groups = lax.axis_size("dp") // GROUP
    if groups == 1:
        return sums
    alike = [[g * GROUP + i for g in range(groups)] for i in range(GROUP)]
    return lax.psum(sums, "dp", axis_index_groups=alike)


def body(
    tokens,
    cotangent,
    prot_lens,
    clus_start,
    norm_gain,
    in_w,
    conv_w,
    conv_b,
    xproj_w,
    dtproj_w,
    dt_bias,
    a_log,
    d_skip,
    out_w,
):
    length = tokens.shape[0]
    features = norm_gain.shape[0]
    width = in_w.shape[1] // 2
    rank, owned = dtproj_w.shape
    states = a_log.shape[0]
    live_mask, same_masks = protein_masks(prot_lens[0], clus_start[0], length, TAPS)
    masks = jnp.stack([live_mask, *same_masks], axis=1)
    fill = lambda v: jnp.pad(v, ((0, 0), (0, owned - v.shape[1])))
    packed = jnp.concatenate(
        [dtproj_w, a_log, xproj_w.T, conv_w, conv_b[None], dt_bias[None], d_skip[None], fill(norm_gain[None])], axis=0
    )
    used = packed.shape[0]
    packed = jnp.pad(packed, ((0, -used % LANES), (0, 0)))
    inner_w, packed = gather_weights((in_w[:, :width], packed), 1)
    inner_w = inner_w.reshape(-1, width)
    gain = packed[:, used - 1, :features].reshape(1, -1).astype(jnp.float32)
    packed = jnp.swapaxes(packed, 0, 1).reshape(packed.shape[1], -1)
    dtproj = packed[:LANES]
    decay_rate = -jnp.exp(packed[rank : rank + states].astype(jnp.float32))
    rate2 = decay_rate * LOG2E
    xproj_t = packed[rank + states : rank + states + LANES]
    by_channel = packed[used - 8 : used].astype(jnp.float32)
    inner, pre, u, dbc, xn, xnt = front(tokens, gain, inner_w, by_channel, xproj_t, masks)
    y, h, dt, (gate_w, out_full) = scan_forward(
        rank, u, dbc, masks, by_channel, dtproj, rate2, (in_w[:, width:], out_w), 2
    )
    gate_w = gate_w.reshape(-1, width)
    out_full = out_full.reshape(-1, out_full.shape[2])
    mixed, d_y, _, out_local, gate_local, skip_local, dxn_gate = middle(
        xn, xnt, gate_w, y, u, by_channel, out_full, cotangent, tokens, masks
    )
    in_pieces = lambda v: v.reshape((4, 2, 2, 2, v.shape[0] // 32, v.shape[1]))
    du, ddbc, ldt, dtproj_local, dtb_local, early_sums = scan_backward(
        rank,
        u,
        dt,
        d_y,
        dbc,
        masks,
        h,
        by_channel,
        dtproj,
        rate2,
        decay_rate.astype(jnp.bfloat16),
        [in_pieces(gate_local), in_pieces(out_local)],
        3,
    )
    inner_local, xproj_local, row_local, token_grad, gain_local = tail(
        du, ddbc, xproj_t, u, inner, pre, by_channel, masks, xnt, inner_w, dxn_gate, tokens, cotangent, gain
    )
    small_local = jnp.concatenate(
        [
            dtproj_local[:rank],
            ldt * decay_rate,
            xproj_local[: xproj_w.shape[1]],
            row_local[: TAPS + 1],
            dtb_local,
            skip_local,
            fill(gain_local.reshape(4, -1)).reshape(1, -1),
        ],
        axis=0,
    ).astype(jnp.bfloat16)
    small_local = jnp.pad(small_local, ((0, -used % LANES), (0, 0)))
    small_local = jnp.swapaxes(small_local.reshape(small_local.shape[0], 4, owned), 0, 1)
    small_local = small_local.reshape(4, 2, 2, 2, -1, owned)
    late_sums = reduce_gradients([in_pieces(inner_local), small_local], 4)
    in_rows = lambda v: v.reshape(-1, v.shape[-1]).astype(jnp.float32)
    gate_grad, out_grad, inner_grad, small = add_groups([in_rows(v) for v in (*early_sums, *late_sums)])
    in_grad = jnp.concatenate([inner_grad, gate_grad], axis=1)
    dtproj_grad, alog_grad, xproj_grad = small[:rank], small[rank : rank + states], small[rank + states : used - 8].T
    conv_grad, convb_grad, dtb_grad, skip_grad = small[used - 8 : used - 4], small[used - 4], small[used - 3], small[used - 2]
    return (
        mixed,
        token_grad,
        small[used - 1, :features],
        in_grad,
        conv_grad,
        convb_grad,
        xproj_grad,
        dtproj_grad,
        dtb_grad,
        alog_grad,
        skip_grad,
        out_grad,
    )


def solution(mesh):
    in_specs = (
        P(("dp", "fsdp"), None),
        P(("dp", "fsdp"), None),
        P(("dp", "fsdp"), None),
        P(("dp", "fsdp"), None),
        P("fsdp"),
        P("fsdp", None),
        P(None, "fsdp"),
        P("fsdp"),
        P("fsdp", None),
        P(None, "fsdp"),
        P("fsdp"),
        P(None, "fsdp"),
        P("fsdp"),
        P("fsdp", None),
    )
    out_specs = (
        P(("dp", "fsdp"), None),
        P(("dp", "fsdp"), None),
        P("fsdp"),
        P("fsdp", None),
        P(None, "fsdp"),
        P("fsdp"),
        P("fsdp", None),
        P(None, "fsdp"),
        P("fsdp"),
        P(None, "fsdp"),
        P("fsdp"),
        P("fsdp", None),
    )
    return jax.shard_map(body, mesh=mesh, in_specs=in_specs, out_specs=out_specs, check_vma=False)
```

```python
import functools

import jax
import jax.numpy as jnp
from jax import lax
from jax.experimental import pallas as pl
from jax.experimental.pallas import tpu as pltpu
from jax.sharding import PartitionSpec as P

QLEN = 16
LANES = 128
WIDE = 256
SPREAD_TIMES = (4, 7, 11)
INNER_TIMES = (0, 1, 4, 6, 7, 8, 9, 10, 12)
SMALL_TIMES = (0, 1, 3, 4, 5, 6, 7, 8, 9)
NEVER = 1e30
LOG2E = 1.4426950408889634
FORWARD_STEPS = (0, 4, 7, 9, 12, 14)
BACKWARD_TIMES = (0, 3, 8, 11, 13, 16)


EPSILON = 1e-05


def shifted_down(values, offset):
    padding = jnp.zeros((offset,) + values.shape[1:], values.dtype)
    return jnp.concatenate([padding, values[:-offset]], axis=0)


def protein_masks(lens_row, start_row, length, taps):
    protein_ends = jnp.cumsum(lens_row)
    protein_begins = protein_ends - lens_row
    flagged = (start_row > 0) & (lens_row > 0)
    position = jnp.arange(length, dtype=jnp.int32)
    cluster = jnp.sum(
        ((position[:, None] >= protein_begins[None, :]) & flagged[None, :]).astype(jnp.int32),
        axis=1,
    )
    live_mask = (position < protein_ends[-1]).astype(jnp.float32)
    same_masks = []
    for offset in range(1, taps):
        matching = (position >= offset) & (cluster == shifted_down(cluster, offset))
        same_masks.append(matching.astype(jnp.float32))
    return (live_mask, same_masks)


def rows_product(left, right):
    return lax.dot_general(
        left, right, (((0,), (0,)), ((), ())), preferred_element_type=jnp.float32
    )


def transposed_product(left, weight):
    return lax.dot_general(
        left, weight, (((1,), (1,)), ((), ())), preferred_element_type=jnp.float32
    )


MESH = pl.DeviceIdType.MESH
GROUP = 8


def own_bits():
    d, f = lax.axis_index("dp"), lax.axis_index("fsdp")
    inside = lax.rem(d, GROUP)
    return {
        "pair": f // 2,
        "core": lax.rem(f, 2),
        "high": inside // 4,
        "low": lax.rem(inside // 2, 2),
        "bit": lax.rem(inside, 2),
    }


def across(own, dim):
    d, f = lax.axis_index("dp"), lax.axis_index("fsdp")
    step = {"pair": 2, "core": 1, "high": 4, "low": 2, "bit": 1}[dim]
    flip = step * (1 - 2 * own[dim])
    return (d, f + flip) if dim in ("pair", "core") else (d + flip, f)


def greet(own, dims):
    barrier = pltpu.get_barrier_semaphore()
    for dim in dims:
        pl.semaphore_signal(barrier, inc=1, device_id=across(own, dim), device_id_type=MESH)
    pl.semaphore_wait(barrier, len(dims))


class Link:
    def __init__(self, own):
        self.own = own
        self.sent = []

    def copy(self, src, dst, sems, dim):
        return pltpu.make_async_remote_copy(
            src_ref=src,
            dst_ref=dst,
            send_sem=sems[0],
            recv_sem=sems[1],
            device_id=across(self.own, dim),
            device_id_type=MESH,
        )

    def send(self, described):
        self.copy(*described()).start()
        self.sent.append(described)

    def receive(self, ref, sems, dim):
        self.copy(ref, ref, sems, dim).wait_recv()

    def finish(self):
        for described in self.sent:
            self.copy(*described()).wait_send()


class Gather:
    def __init__(self, shards, outs, scratch):
        self.shards, self.outs = shards, outs
        self.count = len(shards)
        self.stage = scratch[: self.count]
        self.load_sem, self.core_sem, self.hop_sem, self.whole_sem = scratch[self.count :]
        self.own = own_bits()
        self.link = Link(self.own)
        pair, core = self.own["pair"], self.own["core"]
        self.mine = 2 * pair + core
        self.theirs = 2 * (1 - pair) + core
        self.sibling = 2 * pair + 1 - core
        self.beyond = 2 * (1 - pair) + 1 - core
        bit, low = self.own["bit"], self.own["low"]
        self.kinds = ((bit, low), (1 - bit, low), (bit, 1 - low), (1 - bit, 1 - low))
        self.stages = [self.begin, *(functools.partial(self.from_pair, half) for half in range(2))]
        self.stages += [*(functools.partial(self.from_near, half) for half in range(2)), self.from_far, self.end]

    def eighth(self, a, kind, half):
        rows = self.shards[a].shape[0] // 8
        bit, low = self.kinds[kind]
        return pl.ds(pl.multiple_of((2 * (bit + 2 * low) + half) * rows, rows), rows)

    def hop(self, a, kind, half):
        return self.hop_sem.at[0, a, kind, half], self.hop_sem.at[1, a, kind, half]

    def to_core(self, a, kind, half):
        return self.core_sem.at[0, a, kind, half], self.core_sem.at[1, a, kind, half]

    def whole(self, a):
        return self.whole_sem.at[0, a], self.whole_sem.at[1, a]

    def load(self, a):
        return pltpu.make_async_copy(self.shards[a], self.stage[a], self.load_sem.at[a])

    def store(self, a):
        return pltpu.make_async_copy(self.stage[a], self.outs[a].at[self.mine], self.load_sem.at[a])

    def begin(self):
        greet(self.own, ("core", "pair", "bit", "low"))
        for half in range(2):
            for a in range(self.count):
                self.link.send(functools.partial(self.to_pair, a, half))
        for a in range(self.count):
            self.load(a).start()
            self.link.send(functools.partial(self.own_to_core, a))

    def to_pair(self, a, half):
        rows = self.eighth(a, 0, half)
        return self.shards[a].at[rows], self.outs[a].at[self.mine, rows], self.hop(a, 0, half), "pair"

    def own_to_core(self, a):
        return self.shards[a], self.outs[a].at[self.mine], self.whole(a), "core"

    def came(self, a, kind, half):
        return self.outs[a].at[self.theirs, self.eighth(a, kind, half)]

    def onward(self, a, kind, half, new_kind, dim):
        ref = self.came(a, kind, half)
        return ref, ref, self.to_core(a, kind, half) if dim == "core" else self.hop(a, new_kind, half), dim

    def pass_on(self, a, kind, half, new_kind, dim):
        self.link.send(functools.partial(self.onward, a, kind, half, new_kind, dim))

    def arrive(self, a, kind, half, dim):
        self.link.receive(self.came(a, kind, half), self.hop(a, kind, half), dim)
        self.pass_on(a, kind, half, kind, "core")

    def from_pair(self, half):
        for a in range(self.count):
            self.arrive(a, 0, half, "pair")
            self.pass_on(a, 0, half, 1, "bit")
            self.pass_on(a, 0, half, 2, "low")
        if half == 1:
            for a in range(self.count):
                self.load(a).wait()
                self.store(a).start()

    def from_near(self, half):
        for a in range(self.count):
            self.arrive(a, 1, half, "bit")
            if half == 0:
                self.pass_on(a, 1, 0, 3, "low")
            self.arrive(a, 2, half, "low")
            if half == 1:
                self.pass_on(a, 2, 1, 3, "bit")

    def from_far(self):
        for a in range(self.count):
            self.arrive(a, 3, 0, "low")
            self.arrive(a, 3, 1, "bit")

    def end(self):
        for a in range(self.count):
            self.link.receive(self.outs[a].at[self.sibling], self.whole(a), "core")
            for kind in range(4):
                for half in range(2):
                    ref = self.outs[a].at[self.beyond, self.eighth(a, kind, half)]
                    self.link.receive(ref, self.to_core(a, kind, half), "core")
            self.store(a).wait()
        self.link.finish()

    @staticmethod
    def scratch(shards):
        count = len(shards)
        dma = pltpu.SemaphoreType.DMA
        staged = [pltpu.VMEM(s.shape, s.dtype) for s in shards]
        return staged + [dma((count,)), dma((2, count, 4, 2)), dma((2, count, 4, 2)), dma((2, count))]


def gather_kernel(count, *refs):
    for stage in Gather(refs[:count], refs[count : 2 * count], refs[2 * count :]).stages:
        stage()


def gathered_shape(shard):
    return jax.ShapeDtypeStruct((4,) + shard.shape, shard.dtype)


def gather_weights(shards, collective_id):
    count = len(shards)
    return pl.pallas_call(
        functools.partial(gather_kernel, count),
        out_shape=[gathered_shape(s) for s in shards],
        in_specs=[pl.BlockSpec(memory_space=pl.ANY)] * count,
        out_specs=[pl.BlockSpec(memory_space=pl.ANY)] * count,
        scratch_shapes=Gather.scratch(shards),
        compiler_params=pltpu.CompilerParams(
            collective_id=collective_id, has_side_effects=True, vmem_limit_bytes=32 << 20
        ),
        name="gather_weights",
    )(*shards)


def run_stages(stages, at_steps):
    for step in sorted(set(at_steps)):

        @pl.when(pl.program_id(0) == step)
        def _():
            for stage, at in zip(stages, at_steps):
                if at == step:
                    stage()


DIMS = ("pair", "high", "low", "bit")
PARTS = 4
MIXED = (
    ("pair", "bit", "low", "high"),
    ("bit", "low", "pair", "high"),
    ("low", "pair", "bit", "high"),
    ("pair", "low", "bit", "high"),
)
PAIR_FIRST = (("pair", "bit", "low", "high"), ("pair", "low", "bit", "high")) * 2
SPREAD = (("high", "low", "bit"), ("high", "bit", "low"), ("high", "low", "bit"), ("high", "low", "bit"))
EVERY = slice(None)


def each_block(free, body):
    if not free:
        body(())
        return

    def step(i, carried):
        body(tuple(lax.rem(i // 2 ** (free - 1 - n), 2) for n in range(free)))
        return carried

    lax.fori_loop(0, 2**free, step, 0)


def part_columns(columns, k):
    return pl.ds(k * (columns // PARTS), columns // PARTS)


def region(chosen, dims, columns, k):
    return tuple(chosen.get(d, EVERY) for d in dims) + (EVERY, part_columns(columns, k))


class Halving:
    def __init__(self, link, orders, local, scratch, given=None):
        self.link, self.own, self.orders, self.local, self.given = link, link.own, orders, local, given
        self.cores, *self.arrived, self.load_sem, self.core_sem, self.half_sem = scratch
        self.columns = local.shape[-1]

    def lead(self, core):
        return () if self.given is not None else (core,)

    def of_pair(self, y, k):
        return region({"pair": y}, DIMS, self.columns, k)

    def loading(self, k, y):
        at = self.of_pair(y, k)
        kept = (2 * y + self.own["core"],) + at[1:]
        return pltpu.make_async_copy(self.given.at[kept], self.local.at[at], self.load_sem.at[k, y])

    def giving(self, k, y):
        at = self.of_pair(y, k)
        other = 1 - self.own["core"]
        if self.given is not None:
            src = self.given.at[(2 * y + other,) + at[1:]]
        else:
            src = self.local.at[(other,) + at]
        return src, self.cores.at[at], (self.core_sem.at[0, k, y], self.core_sem.at[1, k, y]), "core"

    def give(self, k):
        for y in range(2):
            self.link.send(functools.partial(self.giving, k, y))
            if self.given is not None:
                self.loading(k, y).start()

    def join(self, k):
        for y in range(2):
            if self.given is not None:
                self.loading(k, y).wait()
            sems = (self.core_sem.at[0, k, y], self.core_sem.at[1, k, y])
            self.link.receive(self.cores.at[self.of_pair(y, k)], sems, "core")

        def add(index):
            at = index + (EVERY, part_columns(self.columns, k))
            kept = self.lead(self.own["core"]) + at
            self.local[kept] = self.local[kept] + self.cores[at]

        each_block(4, add)
        self.halve(k, 0)

    def half(self, k, step):
        dim = self.orders[k][step]
        chosen = {d: self.own[d] for d in self.orders[k][:step]}
        chosen[dim] = 1 - self.own[dim]
        at = self.lead(self.own["core"]) + region(chosen, DIMS, self.columns, k)
        sems = (self.half_sem.at[0, k, step], self.half_sem.at[1, k, step])
        return self.local.at[at], self.arrived[step].at[k], sems, dim

    def halve(self, k, step):
        self.link.send(functools.partial(self.half, k, step))

    def halved(self, k, step, done=None):
        sems = (self.half_sem.at[0, k, step], self.half_sem.at[1, k, step])
        self.link.receive(self.arrived[step].at[k], sems, self.orders[k][step])
        chosen = {d: self.own[d] for d in self.orders[k][: step + 1]}
        free = [d for d in DIMS if d not in chosen]

        def add(index):
            at = tuple(chosen[d] if d in chosen else index[free.index(d)] for d in DIMS)
            kept = self.lead(self.own["core"]) + at + (EVERY, part_columns(self.columns, k))
            total = self.local[kept] + self.arrived[step][(k,) + index + (EVERY, EVERY)]
            if step < 3:
                self.local[kept] = total
            else:
                done(k, total)

        each_block(len(free), add)
        if step < 3:
            self.halve(k, step + 1)

    @staticmethod
    def scratch(rows, columns):
        dma = pltpu.SemaphoreType.DMA
        low = jnp.bfloat16
        shapes = [pltpu.VMEM((2, 2, 2, 2, rows, columns), low)]
        shapes += [pltpu.VMEM((PARTS,) + (2,) * (3 - step) + (rows, columns // PARTS), low) for step in range(4)]
        return shapes + [dma((PARTS, 2)), dma((2, PARTS, 2)), dma((2, PARTS, 4))]


class Spreading:
    def __init__(self, link, full, sems):
        self.link, self.own, self.full, self.sems = link, link.own, full, sems
        self.columns = full.shape[-1]

    def put(self, k, value):
        at = tuple(self.own[d] for d in DIMS[1:]) + (EVERY, part_columns(self.columns, k))
        self.full[at] = value
        self.pass_on(k, 0)

    def held(self, k, step):
        chosen = {d: self.own[d] for d in SPREAD[k][step:]}
        here = self.full.at[region(chosen, DIMS[1:], self.columns, k)]
        return here, here, (self.sems.at[0, k, step], self.sems.at[1, k, step]), SPREAD[k][step]

    def pass_on(self, k, step):
        self.link.send(functools.partial(self.held, k, step))

    def take(self, k, step):
        dim = SPREAD[k][step]
        chosen = {d: self.own[d] for d in SPREAD[k][step:]}
        chosen[dim] = 1 - self.own[dim]
        there = self.full.at[region(chosen, DIMS[1:], self.columns, k)]
        self.link.receive(there, (self.sems.at[0, k, step], self.sems.at[1, k, step]), dim)
        if step < 2:
            self.pass_on(k, step + 1)

    @staticmethod
    def scratch(rows, columns):
        return [pltpu.VMEM((2, 2, 2, rows, columns), jnp.bfloat16), pltpu.SemaphoreType.DMA((2, PARTS, 3))]


def run_events(events, last):
    events = sorted(events, key=lambda event: event[0])
    for step in range(last + 1):
        actions = [action for time, action in events if min(int(time), last) == step]
        if actions:

            @pl.when(pl.program_id(0) == step)
            def _():
                for action in actions:
                    action()


def block_rows(values, row, rows):
    return values[row : row + 1, :]


def lane_index(shape):
    return lax.broadcasted_iota(jnp.int32, shape, 1)


def dot(left, right):
    return jnp.dot(left, right, preferred_element_type=jnp.float32)


def smooth(values):
    share = jax.nn.sigmoid(values)
    return values * share, share


TAPS = 4
BIAS_ROW, STEP_ROW, SKIP_ROW, GAIN_ROW = 4, 5, 6, 7


def front_kernel(tokens_ref, gain_ref, w_ref, rows_ref, xproj_ref, mask_ref, inner_ref, pre_ref, u_ref, dbc_ref, xn_ref, xnt_ref):
    @pl.when(pl.program_id(0) == 0)
    def _():
        x = tokens_ref[...].astype(jnp.float32)
        inv = lax.rsqrt(jnp.mean(x * x, axis=1, keepdims=True) + EPSILON)
        xn = (x * inv * gain_ref[...]).astype(jnp.bfloat16)
        xn_ref[...] = xn
        xnt_ref[...] = xn.T
        dbc_ref[...] = jnp.zeros_like(dbc_ref)

    inner = dot(xn_ref[...], w_ref[...])
    rows = rows_ref[...]
    pre = block_rows(rows, BIAS_ROW, 1) + block_rows(rows, TAPS - 1, 1) * inner
    for offset in range(1, TAPS):
        shifted = pltpu.roll(inner, offset, 0) * mask_ref[:, offset : offset + 1]
        pre = pre + block_rows(rows, TAPS - 1 - offset, 1) * shifted
    u = smooth(pre)[0].astype(jnp.bfloat16)
    inner_ref[...] = inner.astype(inner_ref.dtype)
    pre_ref[...] = pre
    u_ref[...] = u
    dbc_ref[...] += transposed_product(u, xproj_ref[...])


def whole_spec(shape):
    return pl.BlockSpec(shape, lambda i: (0,) * len(shape))


def columns_spec(rows, block):
    return pl.BlockSpec((rows, block), lambda i: (0, i))


def rows_spec(block, columns):
    return pl.BlockSpec((block, columns), lambda i: (i, 0))


def front(tokens, gain, inner_w, by_channel, xproj_t, masks, block=512):
    length, features = tokens.shape
    width = inner_w.shape[1]
    low, wide = jnp.bfloat16, jnp.float32
    return pl.pallas_call(
        front_kernel,
        grid=(width // block,),
        in_specs=[
            whole_spec(tokens.shape),
            whole_spec(gain.shape),
            columns_spec(features, block),
            columns_spec(by_channel.shape[0], block),
            columns_spec(LANES, block),
            whole_spec(masks.shape),
        ],
        out_specs=[
            columns_spec(length, block),
            columns_spec(length, block),
            columns_spec(length, block),
            whole_spec((length, LANES)),
            whole_spec((length, features)),
            whole_spec((features, length)),
        ],
        out_shape=[
            jax.ShapeDtypeStruct((length, width), low),
            jax.ShapeDtypeStruct((length, width), wide),
            jax.ShapeDtypeStruct((length, width), low),
            jax.ShapeDtypeStruct((length, LANES), wide),
            jax.ShapeDtypeStruct((length, features), low),
            jax.ShapeDtypeStruct((features, length), low),
        ],
        compiler_params=pltpu.CompilerParams(vmem_limit_bytes=48 << 20),
        name="front",
    )(tokens, gain, inner_w, by_channel, xproj_t, masks)


def spread_states(dbc, first, states):
    rows = QLEN * states
    repeated = jnp.broadcast_to(dbc[:, None, :], (QLEN, states, LANES)).reshape(rows, LANES)
    state = lax.broadcasted_iota(jnp.int32, (rows, LANES), 0) % states
    own = jnp.where(lane_index((rows, LANES)) == first + state, repeated, 0.0)
    return jnp.broadcast_to(jnp.sum(own, axis=1, keepdims=True), (rows, LANES))


def diagonal_states(dbc, first, states):
    rows = QLEN * states
    pick = (
        lax.broadcasted_iota(jnp.int32, (LANES, rows), 0) == first + lane_index((LANES, rows)) % states
    ).astype(jnp.bfloat16)
    tiled = dot(dbc.astype(jnp.bfloat16), pick)
    own = lane_index((QLEN, rows)) // states == lax.broadcasted_iota(jnp.int32, (QLEN, rows), 0)
    return jnp.where(own, tiled, 0.0).astype(jnp.bfloat16)


def step_rank(dbc, rank):
    return jnp.where(lane_index(dbc.shape) < rank, dbc, 0.0).astype(jnp.bfloat16)


def twice(values):
    return jnp.concatenate([values] * (WIDE // LANES), axis=1)


def forward_kernel(rank, group, count, u_ref, dbc_ref, mask_ref, rows_ref, dtproj_ref, rate_ref, *refs):
    shards, (y_ref, h_ref, dt_ref), outs = refs[:count], refs[count : count + 3], refs[count + 3 : 2 * count + 3]
    (state, long_s, feed_s, b_s, cblk_s), scratch = refs[2 * count + 3 : 2 * count + 8], refs[2 * count + 8 :]
    blocks, _, width = long_s.shape
    states = rate_ref.shape[0]
    span = QLEN * states
    gather = Gather(shards, outs, scratch)
    run_stages(gather.stages[:-1], FORWARD_STEPS)

    @pl.when(pl.program_id(0) == 0)
    def _():
        state[...] = jnp.zeros_like(state)

    rank_rows = step_rank(dbc_ref[...], rank)
    keep = mask_ref[:, 1:2] > 0
    for c in range(0, width, WIDE):
        s = slice(c, c + WIDE)
        dt = jax.nn.softplus(dot(rank_rows, dtproj_ref[:, s]) + rows_ref[STEP_ROW : STEP_ROW + 1, s])
        dt_ref[:, s] = dt
        long = jnp.where(keep, dt, NEVER)
        feed = dt * u_ref[:, s].astype(jnp.float32)
        for j in range(blocks):
            long_s[j, :, s] = long[j * QLEN : (j + 1) * QLEN]
            feed_s[j, :, s] = feed[j * QLEN : (j + 1) * QLEN]
    for j in range(blocks):
        dbc = dbc_ref[j * QLEN : (j + 1) * QLEN, :]
        b_s[j * span : (j + 1) * span, :] = spread_states(dbc, rank, states)
        cblk_s[j * QLEN : (j + 1) * QLEN, :] = diagonal_states(dbc, rank + states, states)

    def block(j, carried):
        r0 = pl.multiple_of(j * QLEN, QLEN)
        h0 = pl.multiple_of(j * span, span)
        for c0 in range(0, width, group * WIDE):
            columns = [slice(c, c + WIDE) for c in range(c0, c0 + group * WIDE, WIDE)]
            held = [state[:, s] for s in columns]
            rates = [rate_ref[:, s] for s in columns]
            for t in range(QLEN):
                b_t = twice(b_s[pl.ds(h0 + t * states, states), :])
                for k, s in enumerate(columns):
                    decay = jnp.exp2(long_s[j, t : t + 1, s] * rates[k])
                    held[k] = decay * held[k] + b_t * feed_s[j, t : t + 1, s]
                    h_ref[pl.ds(h0 + t * states, states), s] = held[k].astype(h_ref.dtype)
            for k, s in enumerate(columns):
                state[:, s] = held[k]
            s = slice(c0, c0 + group * WIDE)
            y_ref[pl.ds(r0, QLEN), s] = dot(cblk_s[pl.ds(r0, QLEN), :], h_ref[pl.ds(h0, span), s])
        return carried

    lax.fori_loop(0, blocks, block, 0)
    run_stages(gather.stages[-1:], (pl.num_programs(0) - 1,))


def scan_forward(rank, u, dbc, masks, by_channel, dtproj, rate2, shards, collective_id, blocks=2, group=2):
    count = len(shards)
    anywhere = [pl.BlockSpec(memory_space=pl.ANY)] * count
    tokens, width = u.shape
    states = rate2.shape[0]
    rows = blocks * QLEN
    y, h, dt, *gathered = pl.pallas_call(
        functools.partial(forward_kernel, rank, group, count),
        grid=(tokens // rows,),
        in_specs=[
            rows_spec(rows, width),
            rows_spec(rows, LANES),
            rows_spec(rows, masks.shape[1]),
            whole_spec(by_channel.shape),
            whole_spec(dtproj.shape),
            whole_spec(rate2.shape),
            *anywhere,
        ],
        out_specs=[rows_spec(rows, width), rows_spec(rows * states, width), rows_spec(rows, width), *anywhere],
        out_shape=[
            jax.ShapeDtypeStruct((tokens, width), jnp.float32),
            jax.ShapeDtypeStruct((tokens * states, width), jnp.bfloat16),
            jax.ShapeDtypeStruct((tokens, width), jnp.float32),
            *(gathered_shape(s) for s in shards),
        ],
        scratch_shapes=[
            pltpu.VMEM((states, width), jnp.float32),
            pltpu.VMEM((blocks, QLEN, width), jnp.float32),
            pltpu.VMEM((blocks, QLEN, width), jnp.float32),
            pltpu.VMEM((rows * states, LANES), jnp.float32),
            pltpu.VMEM((rows, QLEN * states), jnp.bfloat16),
            *Gather.scratch(shards),
        ],
        compiler_params=pltpu.CompilerParams(
            collective_id=collective_id, has_side_effects=True, vmem_limit_bytes=48 << 20
        ),
        name="scan_forward",
    )(u, dbc, masks, by_channel, dtproj, rate2, *shards)
    return y, h, dt, gathered


def middle_kernel(
    xn_ref, xnt_ref, gate_ref, y_ref, u_ref, rows_ref, out_ref, cot_ref, tokens_ref, mask_ref,
    mixed_ref, dy_ref, dgate_ref, outgrad_ref, gategrad_ref, skip_ref, dxn_ref, branch, dbranch
):
    live = mask_ref[:, 0:1]

    @pl.when(pl.program_id(0) == 0)
    def _():
        branch[...] = jnp.zeros_like(branch)
        dxn_ref[...] = jnp.zeros_like(dxn_ref)
        dbranch[...] = (live * cot_ref[...].astype(jnp.float32)).astype(jnp.bfloat16)

    gate = dot(xn_ref[...], gate_ref[...])
    opened, share = smooth(gate)
    u = u_ref[...].astype(jnp.float32)
    y = y_ref[...] + rows_ref[SKIP_ROW : SKIP_ROW + 1, :] * u
    gated = (y * opened).astype(jnp.bfloat16)
    d_branch = dbranch[...]
    branch[...] += dot(gated, out_ref[...])
    outgrad_ref[...] = rows_product(gated, d_branch).astype(outgrad_ref.dtype)
    d_gated = transposed_product(d_branch, out_ref[...])
    d_y = d_gated * opened
    dy_ref[...] = d_y
    skip_ref[...] = jnp.sum(d_y * u, axis=0, keepdims=True)
    d_gate = (d_gated * y * share * (1.0 + gate * (1.0 - share))).astype(jnp.bfloat16)
    dgate_ref[...] = d_gate
    gategrad_ref[...] = dot(xnt_ref[...], d_gate).astype(gategrad_ref.dtype)
    dxn_ref[...] += transposed_product(d_gate, gate_ref[...])

    @pl.when(pl.program_id(0) == pl.num_programs(0) - 1)
    def _():
        mixed_ref[...] = (tokens_ref[...].astype(jnp.float32) + live * branch[...]).astype(mixed_ref.dtype)


def middle(xn, xnt, gate_w, y, u, by_channel, out_w, cotangent, tokens, masks, block=512):
    length, features = tokens.shape
    width = gate_w.shape[1]
    low, wide = jnp.bfloat16, jnp.float32
    channels = columns_spec(length, block)
    return pl.pallas_call(
        middle_kernel,
        grid=(width // block,),
        in_specs=[
            whole_spec(xn.shape),
            whole_spec(xnt.shape),
            columns_spec(features, block),
            channels,
            channels,
            columns_spec(by_channel.shape[0], block),
            rows_spec(block, features),
            whole_spec(tokens.shape),
            whole_spec(tokens.shape),
            whole_spec(masks.shape),
        ],
        out_specs=[
            whole_spec(tokens.shape),
            channels,
            channels,
            rows_spec(block, features),
            columns_spec(features, block),
            columns_spec(1, block),
            whole_spec(tokens.shape),
        ],
        out_shape=[
            jax.ShapeDtypeStruct(tokens.shape, low),
            jax.ShapeDtypeStruct((length, width), wide),
            jax.ShapeDtypeStruct((length, width), low),
            jax.ShapeDtypeStruct((width, features), low),
            jax.ShapeDtypeStruct((features, width), low),
            jax.ShapeDtypeStruct((1, width), wide),
            jax.ShapeDtypeStruct(tokens.shape, wide),
        ],
        scratch_shapes=[pltpu.VMEM(tokens.shape, wide), pltpu.VMEM(tokens.shape, low)],
        compiler_params=pltpu.CompilerParams(vmem_limit_bytes=56 << 20),
        name="middle",
    )(xn, xnt, gate_w, y, u, by_channel, out_w, cotangent, tokens, masks)


def backward_kernel(rank, count, steps, u_ref, dt_ref, dy_ref, dbc_ref, mask_ref, h_ref, before_ref, rows_ref, dtproj_ref, rate2_ref, rate_ref, *refs):
    grads, (du_ref, ddbc_ref, ldt_ref, dtproj_grad, bias_grad) = refs[:count], refs[count : count + 5]
    sums, refs = refs[count + 5 : 2 * count + 5], refs[2 * count + 5 :]
    message, long_s, feed_s, c_s, bblk_s, g_s, lrate_s, db_s, dc_s, before_s, e_s, lsum_s, small_s = refs[:13]
    blocks, _, width = dt_ref.shape
    states = rate_ref.shape[0]
    span = QLEN * states
    low, wide = jnp.bfloat16, jnp.float32
    link = Link(own_bits())
    per = (len(refs) - 13) // count
    halvings = []
    for a in range(count):
        local, *scratch = refs[13 + a * per : 13 + (a + 1) * per]
        halvings.append(Halving(link, MIXED, local, scratch, given=grads[a]))

    def keep_sum(out, k, total):
        out[:, part_columns(out.shape[1], k)] = total

    events = [(0, lambda: greet(link.own, ("core", "pair", "bit", "low", "high")))]
    for k in range(PARTS):
        for halving, out in zip(halvings, sums):
            give, join, *times = BACKWARD_TIMES
            events += [(give, functools.partial(halving.give, k)), (join, functools.partial(halving.join, k))]
            events += [
                (time, functools.partial(halving.halved, k, step, functools.partial(keep_sum, out)))
                for step, time in enumerate(times)
            ]
    final = steps - 1
    run_events([event for event in events if event[0] <= final], final)

    @pl.when(pl.program_id(0) == 0)
    def _():
        message[...] = jnp.zeros_like(message)
        ldt_ref[...] = jnp.zeros_like(ldt_ref)
        dtproj_grad[...] = jnp.zeros_like(dtproj_grad)
        bias_grad[...] = jnp.zeros_like(bias_grad)

    for j in range(blocks):
        own = slice(j * QLEN, (j + 1) * QLEN)
        keep = mask_ref[own, 1:2] > 0
        for c in range(0, width, WIDE):
            s = slice(c, c + WIDE)
            dt = dt_ref[j, :, s]
            long_s[j, :, s] = jnp.where(keep, dt, NEVER)
            feed_s[j, :, s] = dt * u_ref[own, s].astype(wide)
        dbc = dbc_ref[own, :]
        c_s[j * span : (j + 1) * span, :] = spread_states(dbc, rank + states, states)
        bblk_s[own, :] = diagonal_states(dbc, rank, states)
    by_token = (
        lane_index((QLEN, span)) // states == lax.broadcasted_iota(jnp.int32, (QLEN, span), 0)
    ).astype(low)
    state_of = lax.broadcasted_iota(jnp.int32, (span, LANES), 0) % states
    at_b = lane_index((span, LANES)) == rank + state_of
    at_c = lane_index((span, LANES)) == rank + states + state_of

    def block(step, carried):
        j = blocks - 1 - step
        r0 = pl.multiple_of(j * QLEN, QLEN)
        h0 = pl.multiple_of(j * span, span)

        @pl.when(j == 0)
        def _():
            before_s[...] = before_ref[...]

        @pl.when(j > 0)
        def _():
            before_s[...] = h_ref[pl.ds(pl.multiple_of(jnp.maximum(h0 - states, 0), states), states), :]

        db_s[...] = jnp.zeros_like(db_s)
        dc_s[...] = jnp.zeros_like(dc_s)
        for c in range(0, width, WIDE):
            s = slice(c, c + WIDE)
            held, rate2, rate, total = message[:, s], rate2_ref[:, s], rate_ref[:, s], ldt_ref[:, s]
            pending = None
            now = h_ref[pl.ds(h0 + (QLEN - 1) * states, states), s]
            for t in reversed(range(QLEN)):
                at = slice(t * states, (t + 1) * states)
                d_y = jnp.broadcast_to(dy_ref[j, t : t + 1, s], (states, WIDE))
                g = twice(c_s[pl.ds(h0 + t * states, states), :]) * d_y + held
                g_low = g.astype(low)
                g_s[at, s] = g_low
                dt = jnp.broadcast_to(long_s[j, t : t + 1, s], (states, WIDE))
                held = jnp.exp2(dt * rate2) * g
                before = before_s[:, s] if t == 0 else h_ref[pl.ds(h0 + (t - 1) * states, states), s]
                l = held.astype(low) * before
                lrate_s[at, s] = l * rate
                ldt = l * dt.astype(low)
                if pending is None:
                    pending = ldt
                else:
                    total = total + (pending + ldt).astype(wide)
                    pending = None
                feed = jnp.broadcast_to(feed_s[j, t : t + 1, s], (states, WIDE))
                for sums, product in ((db_s, g_low * feed.astype(low)), (dc_s, now * d_y.astype(low))):
                    sums[at, :] += (product[:, :LANES] + product[:, LANES:]).astype(wide)
                now = before
            message[:, s] = held
            ldt_ref[:, s] = total
            e_s[pl.ds(r0, QLEN), s] = dot(bblk_s[pl.ds(r0, QLEN), :], g_s[:, s])
            lsum_s[pl.ds(r0, QLEN), s] = dot(by_token, lrate_s[:, s])
        d_b = jnp.sum(db_s[...], axis=1, keepdims=True)
        d_c = jnp.sum(dc_s[...], axis=1, keepdims=True)
        placed = jnp.where(at_b, d_b, jnp.where(at_c, d_c, 0.0)).astype(low)
        small_s[pl.ds(r0, QLEN), :] = dot(by_token, placed)
        return carried

    lax.fori_loop(0, blocks, block, 0)
    rank_rows = step_rank(dbc_ref[...], rank)
    d_rank = jnp.zeros(rank_rows.shape, wide)
    tokens = blocks * QLEN
    for c in range(0, width, WIDE):
        s = slice(c, c + WIDE)
        dt = dt_ref[:, :, s].reshape(tokens, WIDE)
        d_y = dy_ref[:, :, s].reshape(tokens, WIDE)
        e = e_s[:, s]
        share = jnp.where(dt < 0.01, dt * (1.0 - dt * (0.5 - dt * (1.0 / 6.0))), 1.0 - jnp.exp(-dt))
        d_dt = e * u_ref[:, s].astype(wide) + lsum_s[:, s]
        d_step = (d_dt * share).astype(low)
        bias_grad[:, s] += jnp.sum(d_step.astype(wide), axis=0, keepdims=True)
        dtproj_grad[:, s] += rows_product(rank_rows, d_step)
        d_rank += transposed_product(d_step, dtproj_ref[:, s])
        du_ref[:, s] = d_y * rows_ref[SKIP_ROW : SKIP_ROW + 1, s] + e * dt
    ddbc_ref[...] = (jnp.where(lane_index(d_rank.shape) < rank, d_rank, 0.0) + small_s[...]).astype(low)
    run_events([event for event in events if event[0] > final] + [(steps, link.finish)], final)


def scan_backward(rank, u, dt, d_y, dbc, masks, h, by_channel, dtproj, rate2, rate, grads, collective_id, blocks=2):
    count = len(grads)
    anywhere = [pl.BlockSpec(memory_space=pl.ANY)] * count
    tokens, width = u.shape
    states = rate2.shape[0]
    rows = blocks * QLEN
    steps = tokens // rows
    low, wide = jnp.bfloat16, jnp.float32
    back = lambda i: (steps - 1 - i, 0)
    flat = lambda columns: pl.BlockSpec((rows, columns), back)
    cubes = pl.BlockSpec((blocks, QLEN, width), lambda i: (steps - 1 - i, 0, 0))
    in_blocks = lambda v: v.reshape(tokens // QLEN, QLEN, width)
    du, ddbc, ldt, dtproj_grad, bias_grad, *sums = pl.pallas_call(
        functools.partial(backward_kernel, rank, count, steps),
        grid=(steps,),
        in_specs=[
            flat(width),
            cubes,
            cubes,
            flat(LANES),
            flat(masks.shape[1]),
            pl.BlockSpec((rows * states, width), back),
            pl.BlockSpec((states, width), lambda i: (jnp.maximum((steps - 1 - i) * rows - 1, 0), 0)),
            whole_spec(by_channel.shape),
            whole_spec(dtproj.shape),
            whole_spec(rate2.shape),
            whole_spec(rate.shape),
            *anywhere,
        ],
        out_specs=[
            flat(width),
            flat(LANES),
            whole_spec(rate2.shape),
            whole_spec(dtproj.shape),
            whole_spec((1, width)),
            *(whole_spec(g.shape[4:]) for g in grads),
        ],
        out_shape=[
            jax.ShapeDtypeStruct((tokens, width), wide),
            jax.ShapeDtypeStruct((tokens, LANES), low),
            jax.ShapeDtypeStruct(rate2.shape, wide),
            jax.ShapeDtypeStruct(dtproj.shape, wide),
            jax.ShapeDtypeStruct((1, width), wide),
            *(jax.ShapeDtypeStruct(g.shape[4:], g.dtype) for g in grads),
        ],
        scratch_shapes=[
            pltpu.VMEM((states, width), wide),
            pltpu.VMEM((blocks, QLEN, width), wide),
            pltpu.VMEM((blocks, QLEN, width), wide),
            pltpu.VMEM((rows * states, LANES), wide),
            pltpu.VMEM((rows, QLEN * states), low),
            pltpu.VMEM((QLEN * states, width), low),
            pltpu.VMEM((QLEN * states, width), low),
            pltpu.VMEM((QLEN * states, LANES), wide),
            pltpu.VMEM((QLEN * states, LANES), wide),
            pltpu.VMEM((states, width), low),
            pltpu.VMEM((rows, width), wide),
            pltpu.VMEM((rows, width), wide),
            pltpu.VMEM((rows, LANES), wide),
            *(
                shape
                for g in grads
                for shape in (pltpu.VMEM((2, 2, 2, 2) + g.shape[4:], low), *Halving.scratch(*g.shape[4:]))
            ),
        ],
        compiler_params=pltpu.CompilerParams(
            collective_id=collective_id, has_side_effects=True, vmem_limit_bytes=56 << 20
        ),
        name="scan_backward",
    )(u, in_blocks(dt), in_blocks(d_y), dbc, masks, h, h, by_channel, dtproj, rate2, rate, *grads)
    return du, ddbc, ldt, dtproj_grad, bias_grad, sums


def tail_kernel(
    steps, rank, count, du_ref, ddbc_ref, xproj_ref, u_ref, inner_ref, pre_ref, rows_ref, mask_ref, xnt_ref, w_ref, dgate_ref, tokens_ref, cot_ref, gain_ref,
    dtproj_ref, alog_ref, bias_ref, skip_ref, *refs
):
    wide, low = jnp.float32, jnp.bfloat16
    pieces, tokengrad_ref, outs = refs[:count], refs[count], refs[count + 1 : 2 * count + 3]
    refs = refs[2 * count + 3 :]
    dxn, xproj_s, row_s, inner_s, small_s, out_sem = refs[:6]
    link = Link(own_bits())
    halving_refs, spreading_refs = refs[6 : 6 + 16], refs[6 + 16 :]
    spreadings = [Spreading(link, *spreading_refs[2 * a : 2 * a + 2]) for a in range(count + 2)]
    inner_sum = Halving(link, PAIR_FIRST, inner_s, halving_refs[:8])
    small_sum = Halving(link, PAIR_FIRST, small_s, halving_refs[8:])
    block = du_ref.shape[1]
    here = pl.program_id(0)
    columns = pl.ds(pl.multiple_of(here * block, block), block)
    final = steps - 1

    def start():
        greet(link.own, ("core", "pair", "bit", "low", "high"))
        for k in range(PARTS):
            for piece, spreading in zip(pieces, spreadings):
                spreading.put(k, piece[:, part_columns(piece.shape[1], k)])

    def add_up(events, halving, spreading, k, first, times):
        give, join, *halves = times[:6]
        events += [(first + give, functools.partial(halving.give, k)), (first + join, functools.partial(halving.join, k))]
        events += [
            (first + time, functools.partial(halving.halved, k, step, spreading.put)) for step, time in enumerate(halves)
        ]
        events += [
            (first + time, functools.partial(spreading.take, k, step)) for step, time in enumerate(times[6:])
        ]

    events = []
    for k in range(PARTS):
        for spreading in spreadings[:count]:
            events += [(time, functools.partial(spreading.take, k, step)) for step, time in enumerate(SPREAD_TIMES)]
        ready = (k + 1) * steps // PARTS - 1
        add_up(events, inner_sum, spreadings[count], k, ready, INNER_TIMES)
        add_up(events, small_sum, spreadings[count + 1], k, final, SMALL_TIMES)
    run_events([(0, start)], final)

    @pl.when(here == 0)
    def _():
        dxn[...] = dgate_ref[...]

    rows = rows_ref[...]
    pre = pre_ref[...]
    share = jax.nn.sigmoid(pre)
    d_u = du_ref[...] + dot(ddbc_ref[...], xproj_ref[...])
    d_pre = d_u * share * (1.0 + pre * (1.0 - share))
    inner = inner_ref[...].astype(wide)
    d_inner = block_rows(rows, TAPS - 1, 1) * d_pre
    sums = [None] * 8
    sums[TAPS - 1] = jnp.sum(d_pre * inner, axis=0, keepdims=True)
    sums[BIAS_ROW] = jnp.sum(d_pre, axis=0, keepdims=True)
    for offset in range(1, TAPS):
        same = d_pre * mask_ref[:, offset : offset + 1]
        back = pltpu.roll(same, same.shape[0] - offset, 0)
        sums[TAPS - 1 - offset] = jnp.sum(back * inner, axis=0, keepdims=True)
        d_inner = d_inner + block_rows(rows, TAPS - 1 - offset, 1) * back
    nothing = jnp.zeros_like(sums[0])
    row_s[:, columns] = jnp.concatenate([nothing if v is None else v for v in sums], axis=0)
    xproj_s[:, columns] = rows_product(ddbc_ref[...], u_ref[...])
    d_inner = d_inner.astype(low)
    inner_grad = dot(xnt_ref[...], d_inner).astype(low)
    size = inner_grad.shape[0] // 4
    for shard in range(4):
        own_rows = inner_grad[shard * size : (shard + 1) * size]
        inner_s[shard % 2, shard // 2, :, :, :, :, columns] = own_rows.reshape(2, 2, 2, size // 8, block)
    dxn[...] += transposed_product(d_inner, w_ref[...])

    @pl.when(here == final)
    def _():
        x = tokens_ref[...].astype(wide)
        inv = lax.rsqrt(jnp.mean(x * x, axis=1, keepdims=True) + EPSILON)
        x_hat = x * inv
        gain_grad = jnp.sum(dxn[...] * x_hat, axis=0, keepdims=True)
        d_hat = dxn[...] * gain_ref[...]
        level = jnp.mean(d_hat * x_hat, axis=1, keepdims=True)
        tokengrad_ref[...] = cot_ref[...].astype(wide) + inv * (d_hat - x_hat * level)
        owned = xproj_s.shape[1] // 4
        states = alog_ref.shape[0]
        part = gain_grad.shape[1] // 4
        row = lax.broadcasted_iota(jnp.int32, (8, owned), 0)
        for shard in range(4):
            own = slice(shard * owned, (shard + 1) * owned)
            gains = jnp.concatenate(
                [gain_grad[:, shard * part : (shard + 1) * part], jnp.zeros((1, owned - part), wide)], axis=1
            )
            rows = row_s[:, own]
            for at, extra in ((STEP_ROW, bias_ref[:, own]), (SKIP_ROW, skip_ref[:, own]), (GAIN_ROW, gains)):
                rows = jnp.where(row == at, extra, rows)
            stacked = [dtproj_ref[:rank, own], alog_ref[:, own], xproj_s[: rank + 2 * states, own], rows]
            height = 8 * small_s.shape[5]
            stacked.append(jnp.zeros((height - sum(v.shape[0] for v in stacked), owned), wide))
            stacked = jnp.concatenate(stacked, axis=0).astype(low)
            small_s[shard % 2, shard // 2] = stacked.reshape(2, 2, 2, height // 8, owned)

    run_events(events, final)

    @pl.when(here == final)
    def _():
        stores = [pltpu.make_async_copy(s.full, o, out_sem.at[i]) for i, (s, o) in enumerate(zip(spreadings, outs))]
        for copy in stores:
            copy.start()
        for copy in stores:
            copy.wait()
        link.finish()


def tail(
    rank, du, ddbc, xproj_t, u, inner, pre, by_channel, masks, xnt, inner_w, dxn_gate, tokens, cotangent, gain,
    dtproj_grad, alog_grad, bias_grad, skip_grad, pieces, collective_id, block=256,
):
    length, features = tokens.shape
    width = inner_w.shape[1]
    count = len(pieces)
    steps = width // block
    inner_shape = (features // 32, width)
    used = 2 * rank + 3 * alog_grad.shape[0] + 8
    small_shape = ((used + -used % LANES) // 8, width // 4)
    shapes = [*(p.shape for p in pieces), inner_shape, small_shape]
    low, wide = jnp.bfloat16, jnp.float32
    channels = columns_spec(length, block)
    token_grad, *sums = pl.pallas_call(
        functools.partial(tail_kernel, steps, rank, count),
        grid=(steps,),
        in_specs=[
            channels,
            whole_spec(ddbc.shape),
            columns_spec(LANES, block),
            channels,
            channels,
            channels,
            columns_spec(by_channel.shape[0], block),
            whole_spec(masks.shape),
            whole_spec(xnt.shape),
            columns_spec(features, block),
            whole_spec(dxn_gate.shape),
            whole_spec(tokens.shape),
            whole_spec(tokens.shape),
            whole_spec(gain.shape),
            whole_spec(dtproj_grad.shape),
            whole_spec(alog_grad.shape),
            whole_spec(bias_grad.shape),
            whole_spec(skip_grad.shape),
            *(whole_spec(p.shape) for p in pieces),
        ],
        out_specs=[whole_spec(tokens.shape), *[pl.BlockSpec(memory_space=pl.ANY)] * (count + 2)],
        out_shape=[
            jax.ShapeDtypeStruct(tokens.shape, wide),
            *(jax.ShapeDtypeStruct((2, 2, 2) + shape, low) for shape in shapes),
        ],
        scratch_shapes=[
            pltpu.VMEM(tokens.shape, wide),
            pltpu.VMEM((LANES, width), wide),
            pltpu.VMEM((8, width), wide),
            pltpu.VMEM((2, 2, 2, 2, 2) + inner_shape, low),
            pltpu.VMEM((2, 2, 2, 2, 2) + small_shape, low),
            pltpu.SemaphoreType.DMA((count + 2,)),
            *Halving.scratch(*inner_shape),
            *Halving.scratch(*small_shape),
            *(shape for s in shapes for shape in Spreading.scratch(*s)),
        ],
        compiler_params=pltpu.CompilerParams(
            collective_id=collective_id, has_side_effects=True, vmem_limit_bytes=58 << 20
        ),
        name="tail",
    )(
        du, ddbc, xproj_t, u, inner, pre, by_channel, masks, xnt, inner_w, dxn_gate, tokens, cotangent, gain,
        dtproj_grad, alog_grad, bias_grad, skip_grad, *pieces,
    )
    return token_grad, sums


def add_groups(sums):
    groups = lax.axis_size("dp") // GROUP
    if groups == 1:
        return sums
    alike = [[g * GROUP + i for g in range(groups)] for i in range(GROUP)]
    return lax.psum(sums, "dp", axis_index_groups=alike)


def body(
    tokens,
    cotangent,
    prot_lens,
    clus_start,
    norm_gain,
    in_w,
    conv_w,
    conv_b,
    xproj_w,
    dtproj_w,
    dt_bias,
    a_log,
    d_skip,
    out_w,
):
    length = tokens.shape[0]
    features = norm_gain.shape[0]
    width = in_w.shape[1] // 2
    rank, owned = dtproj_w.shape
    states = a_log.shape[0]
    live_mask, same_masks = protein_masks(prot_lens[0], clus_start[0], length, TAPS)
    masks = jnp.stack([live_mask, *same_masks], axis=1)
    fill = lambda v: jnp.pad(v, ((0, 0), (0, owned - v.shape[1])))
    packed = jnp.concatenate(
        [dtproj_w, a_log, xproj_w.T, conv_w, conv_b[None], dt_bias[None], d_skip[None], fill(norm_gain[None])], axis=0
    )
    used = packed.shape[0]
    packed = jnp.pad(packed, ((0, -used % LANES), (0, 0)))
    inner_w, packed = gather_weights((in_w[:, :width], packed), 1)
    inner_w = inner_w.reshape(-1, width)
    gain = packed[:, used - 1, :features].reshape(1, -1).astype(jnp.float32)
    packed = jnp.swapaxes(packed, 0, 1).reshape(packed.shape[1], -1)
    dtproj = packed[:LANES]
    decay_rate = -jnp.exp(packed[rank : rank + states].astype(jnp.float32))
    rate2 = decay_rate * LOG2E
    xproj_t = packed[rank + states : rank + states + LANES]
    by_channel = packed[used - 8 : used].astype(jnp.float32)
    inner, pre, u, dbc, xn, xnt = front(tokens, gain, inner_w, by_channel, xproj_t, masks)
    y, h, dt, (gate_w, out_full) = scan_forward(
        rank, u, dbc, masks, by_channel, dtproj, rate2, (in_w[:, width:], out_w), 2
    )
    gate_w = gate_w.reshape(-1, width)
    out_full = out_full.reshape(-1, out_full.shape[2])
    mixed, d_y, _, out_local, gate_local, skip_local, dxn_gate = middle(
        xn, xnt, gate_w, y, u, by_channel, out_full, cotangent, tokens, masks
    )
    in_pieces = lambda v: v.reshape((4, 2, 2, 2, v.shape[0] // 32, v.shape[1]))
    du, ddbc, ldt, dtproj_local, dtb_local, early_pieces = scan_backward(
        rank,
        u,
        dt,
        d_y,
        dbc,
        masks,
        h,
        by_channel,
        dtproj,
        rate2,
        decay_rate.astype(jnp.bfloat16),
        [in_pieces(gate_local), in_pieces(out_local)],
        3,
    )
    token_grad, sums = tail(
        rank,
        du,
        ddbc,
        xproj_t,
        u,
        inner,
        pre,
        by_channel,
        masks,
        xnt,
        inner_w,
        dxn_gate,
        tokens,
        cotangent,
        gain,
        dtproj_local,
        ldt * decay_rate,
        dtb_local,
        skip_local,
        early_pieces,
        4,
    )
    in_rows = lambda v: v.reshape(-1, v.shape[-1]).astype(jnp.float32)
    gate_grad, out_grad, inner_grad, small = add_groups([in_rows(v) for v in sums])
    in_grad = jnp.concatenate([inner_grad, gate_grad], axis=1)
    dtproj_grad, alog_grad, xproj_grad = small[:rank], small[rank : rank + states], small[rank + states : used - 8].T
    conv_grad, convb_grad, dtb_grad, skip_grad = small[used - 8 : used - 4], small[used - 4], small[used - 3], small[used - 2]
    return (
        mixed,
        token_grad,
        small[used - 1, :features],
        in_grad,
        conv_grad,
        convb_grad,
        xproj_grad,
        dtproj_grad,
        dtb_grad,
        alog_grad,
        skip_grad,
        out_grad,
    )


def solution(mesh):
    in_specs = (
        P(("dp", "fsdp"), None),
        P(("dp", "fsdp"), None),
        P(("dp", "fsdp"), None),
        P(("dp", "fsdp"), None),
        P("fsdp"),
        P("fsdp", None),
        P(None, "fsdp"),
        P("fsdp"),
        P("fsdp", None),
        P(None, "fsdp"),
        P("fsdp"),
        P(None, "fsdp"),
        P("fsdp"),
        P("fsdp", None),
    )
    out_specs = (
        P(("dp", "fsdp"), None),
        P(("dp", "fsdp"), None),
        P("fsdp"),
        P("fsdp", None),
        P(None, "fsdp"),
        P("fsdp"),
        P("fsdp", None),
        P(None, "fsdp"),
        P("fsdp"),
        P(None, "fsdp"),
        P("fsdp"),
        P("fsdp", None),
    )
    return jax.shard_map(body, mesh=mesh, in_specs=in_specs, out_specs=out_specs, check_vma=False)
```

```python
import functools

import jax
import jax.numpy as jnp
from jax import lax
from jax.experimental import pallas as pl
from jax.experimental.pallas import tpu as pltpu
from jax.sharding import PartitionSpec as P

QLEN = 16
LANES = 128
WIDE = 256
SPREAD_TIMES = ((4.02, 7.06, 13.1), (6.02, 12.02, 13.16))
INNER_TIMES = (
    (1, 3.02, 7.04, 12.04, 13.2, 13.32, 13.44, 13.52, 13.62),
    (3, 4.04, 10.04, 13.02, 13.12, 13.28, 13.42, 13.48, 13.6),
    (5, 7.02, 13.06, 13.22, 13.34, 13.46, 13.58, 13.7, 13.78),
    (7, 9.02, 13.08, 13.24, 13.36, 13.5, 13.64, 13.72, 13.8),
)
SMALL_TIMES = ((7, 10.02, 13.14, 13.26, 13.38, 13.54, 13.66, 13.74, 13.82),)
GAIN_TIMES = ((12.01, 13.04, 13.18, 13.3, 13.4, 13.56, 13.68, 13.76, 13.84),)
DXN_TIMES = (8, 9.5, 10.5, 11.5)
NORM_TIME = 12
NEVER = 1e30
LOG2E = 1.4426950408889634
FORWARD_STEPS = (0, 4, 7, 9, 12, 14)
BACKWARD_TIMES = (
    ((0, 2.1, 6.1, 9.1, 11.1, 13.1), (0, 3.1, 7.1, 10.1, 12.1, 14.1)),
    ((0, 4.1, 8.1, 11.2, 13.2, 15.1), (0, 5.1, 9.2, 12.2, 14.2, 16.1)),
)


EPSILON = 1e-05


def rows_product(left, right):
    return lax.dot_general(
        left, right, (((0,), (0,)), ((), ())), preferred_element_type=jnp.float32
    )


def transposed_product(left, weight):
    return lax.dot_general(
        left, weight, (((1,), (1,)), ((), ())), preferred_element_type=jnp.float32
    )


MESH = pl.DeviceIdType.MESH
GROUP = 8


def own_bits():
    d, f = lax.axis_index("dp"), lax.axis_index("fsdp")
    inside = lax.rem(d, GROUP)
    return {
        "pair": f // 2,
        "core": lax.rem(f, 2),
        "high": inside // 4,
        "low": lax.rem(inside // 2, 2),
        "bit": lax.rem(inside, 2),
    }


def across(own, dim):
    d, f = lax.axis_index("dp"), lax.axis_index("fsdp")
    step = {"pair": 2, "core": 1, "high": 4, "low": 2, "bit": 1}[dim]
    flip = step * (1 - 2 * own[dim])
    return (d, f + flip) if dim in ("pair", "core") else (d + flip, f)


def greet(own, dims):
    barrier = pltpu.get_barrier_semaphore()
    for dim in dims:
        pl.semaphore_signal(barrier, inc=1, device_id=across(own, dim), device_id_type=MESH)
    pl.semaphore_wait(barrier, len(dims))


class Link:
    def __init__(self, own):
        self.own = own
        self.sent = []

    def copy(self, src, dst, sems, dim):
        return pltpu.make_async_remote_copy(
            src_ref=src,
            dst_ref=dst,
            send_sem=sems[0],
            recv_sem=sems[1],
            device_id=across(self.own, dim),
            device_id_type=MESH,
        )

    def send(self, described):
        self.copy(*described()).start()
        self.sent.append(described)

    def receive(self, ref, sems, dim):
        self.copy(ref, ref, sems, dim).wait_recv()

    def finish(self):
        for described in self.sent:
            self.copy(*described()).wait_send()


class Gather:
    def __init__(self, shards, outs, scratch, made=None):
        self.shards, self.outs, self.made = shards, outs, made
        self.count = len(shards)
        self.stage = scratch[: self.count]
        self.load_sem, self.core_sem, self.hop_sem, self.whole_sem = scratch[self.count :]
        self.own = own_bits()
        self.link = Link(self.own)
        pair, core = self.own["pair"], self.own["core"]
        self.mine = 2 * pair + core
        self.theirs = 2 * (1 - pair) + core
        self.sibling = 2 * pair + 1 - core
        self.beyond = 2 * (1 - pair) + 1 - core
        bit, low = self.own["bit"], self.own["low"]
        self.kinds = ((bit, low), (1 - bit, low), (bit, 1 - low), (1 - bit, 1 - low))
        self.stages = [self.begin, *(functools.partial(self.from_pair, half) for half in range(2))]
        self.stages += [*(functools.partial(self.from_near, half) for half in range(2)), self.from_far, self.end]

    def eighth(self, a, kind, half):
        rows = self.shards[a].shape[0] // 8
        bit, low = self.kinds[kind]
        return pl.ds(pl.multiple_of((2 * (bit + 2 * low) + half) * rows, rows), rows)

    def hop(self, a, kind, half):
        return self.hop_sem.at[0, a, kind, half], self.hop_sem.at[1, a, kind, half]

    def to_core(self, a, kind, half):
        return self.core_sem.at[0, a, kind, half], self.core_sem.at[1, a, kind, half]

    def whole(self, a):
        return self.whole_sem.at[0, a], self.whole_sem.at[1, a]

    def load(self, a):
        return pltpu.make_async_copy(self.shards[a], self.stage[a], self.load_sem.at[a])

    def in_place(self, a):
        return self.made is not None and a == self.count - 1

    def store(self, a):
        return pltpu.make_async_copy(self.stage[a], self.outs[a].at[self.mine], self.load_sem.at[a])

    def begin(self):
        greet(self.own, ("core", "pair", "bit", "low"))
        for a in range(self.count):
            if self.in_place(a):
                self.made()
            for half in range(2):
                self.link.send(functools.partial(self.to_pair, a, half))
        for a in range(self.count):
            if not self.in_place(a):
                self.load(a).start()
            self.link.send(functools.partial(self.own_to_core, a))

    def to_pair(self, a, half):
        rows = self.eighth(a, 0, half)
        return self.shards[a].at[rows], self.outs[a].at[self.mine, rows], self.hop(a, 0, half), "pair"

    def own_to_core(self, a):
        return self.shards[a], self.outs[a].at[self.mine], self.whole(a), "core"

    def came(self, a, kind, half):
        return self.outs[a].at[self.theirs, self.eighth(a, kind, half)]

    def onward(self, a, kind, half, new_kind, dim):
        ref = self.came(a, kind, half)
        return ref, ref, self.to_core(a, kind, half) if dim == "core" else self.hop(a, new_kind, half), dim

    def pass_on(self, a, kind, half, new_kind, dim):
        self.link.send(functools.partial(self.onward, a, kind, half, new_kind, dim))

    def arrive(self, a, kind, half, dim):
        self.link.receive(self.came(a, kind, half), self.hop(a, kind, half), dim)
        self.pass_on(a, kind, half, kind, "core")

    def from_pair(self, half):
        for a in range(self.count):
            self.arrive(a, 0, half, "pair")
            self.pass_on(a, 0, half, 1, "bit")
            self.pass_on(a, 0, half, 2, "low")
        if half == 1:
            for a in range(self.count):
                if not self.in_place(a):
                    self.load(a).wait()
                self.store(a).start()

    def from_near(self, half):
        for a in range(self.count):
            self.arrive(a, 1, half, "bit")
            if half == 0:
                self.pass_on(a, 1, 0, 3, "low")
            self.arrive(a, 2, half, "low")
            if half == 1:
                self.pass_on(a, 2, 1, 3, "bit")

    def from_far(self):
        for a in range(self.count):
            self.arrive(a, 3, 0, "low")
            self.arrive(a, 3, 1, "bit")

    def end(self):
        for a in range(self.count):
            self.link.receive(self.outs[a].at[self.sibling], self.whole(a), "core")
            for kind in range(4):
                for half in range(2):
                    ref = self.outs[a].at[self.beyond, self.eighth(a, kind, half)]
                    self.link.receive(ref, self.to_core(a, kind, half), "core")
            self.store(a).wait()
        self.link.finish()

    @staticmethod
    def scratch(shapes):
        count = len(shapes)
        dma = pltpu.SemaphoreType.DMA
        staged = [pltpu.VMEM(shape, jnp.bfloat16) for shape in shapes]
        return staged + [dma((count,)), dma((2, count, 4, 2)), dma((2, count, 4, 2)), dma((2, count))]


def gather_kernel(
    width, in_ref, dtproj_ref, alog_ref, xproj_ref, taps_ref, bias_ref, step_ref, skip_ref, gain_ref, inner_out, packed_out, *scratch
):
    packed = scratch[1]

    def pack():
        low = packed.dtype
        rank, states, columns = dtproj_ref.shape[0], alog_ref.shape[0], xproj_ref.shape[1]
        eye = (
            lax.broadcasted_iota(jnp.int32, (columns, columns), 0) == lane_index((columns, columns))
        ).astype(low)
        at = rank + states + columns
        owned = packed.shape[1]
        wide = jnp.float32
        packed[:rank, :] = dtproj_ref[...]
        packed[rank : rank + states, :] = alog_ref[...]
        packed[rank + states : at, :] = transposed_product(eye, xproj_ref[...]).astype(low)
        row = lax.broadcasted_iota(jnp.int32, (16, owned), 0)
        rows = jnp.concatenate([taps_ref[...].astype(wide), jnp.zeros((16 - TAPS, owned), wide)], axis=0)
        for place, ref in ((BIAS_ROW, bias_ref), (STEP_ROW, step_ref), (SKIP_ROW, skip_ref), (GAIN_ROW, gain_ref)):
            values = ref[...].astype(wide).reshape(1, ref.shape[0])
            if ref.shape[0] < owned:
                values = jnp.concatenate([values, jnp.zeros((1, owned - ref.shape[0]), wide)], axis=1)
            rows = jnp.where(row == place, values, rows)
        packed[at : at + 16, :] = rows.astype(low)
        packed[at + 16 :, :] = jnp.zeros((packed.shape[0] - at - 16, owned), low)

    gather = Gather((in_ref.at[:, pl.ds(0, width)], packed), (inner_out, packed_out), scratch, made=pack)
    for stage in gather.stages:
        stage()


def gathered_shape(shape):
    return jax.ShapeDtypeStruct((4,) + shape, jnp.bfloat16)


def gather_weights(in_w, dtproj_w, a_log, xproj_w, conv_w, vectors, collective_id):
    anywhere, vmem = pl.BlockSpec(memory_space=pl.ANY), pl.BlockSpec(memory_space=pltpu.VMEM)
    used = dtproj_w.shape[0] + a_log.shape[0] + xproj_w.shape[1] + TAPS + len(vectors)
    shapes = [(in_w.shape[0], in_w.shape[1] // 2), (used + -used % LANES, conv_w.shape[1])]
    return pl.pallas_call(
        functools.partial(gather_kernel, shapes[0][1]),
        out_shape=[gathered_shape(shape) for shape in shapes],
        in_specs=[anywhere] + [vmem] * (4 + len(vectors)),
        out_specs=[anywhere, anywhere],
        scratch_shapes=Gather.scratch(shapes),
        compiler_params=pltpu.CompilerParams(
            collective_id=collective_id, has_side_effects=True, vmem_limit_bytes=60 << 20
        ),
        name="gather_weights",
    )(in_w, dtproj_w, a_log, xproj_w, conv_w, *vectors)


def run_stages(stages, at_steps):
    for step in sorted(set(at_steps)):

        @pl.when(pl.program_id(0) == step)
        def _():
            for stage, at in zip(stages, at_steps):
                if at == step:
                    stage()


DIMS = ("pair", "high", "low", "bit")
MIXED = (
    ("pair", "bit", "low", "high"),
    ("bit", "low", "pair", "high"),
    ("low", "pair", "bit", "high"),
    ("pair", "low", "bit", "high"),
)
PAIR_FIRST = (("pair", "bit", "low", "high"), ("pair", "low", "bit", "high"))
LOW_FIRST, BIT_FIRST = ("high", "low", "bit"), ("high", "bit", "low")
EARLY_ORDERS = (MIXED[:2], MIXED[2:])
TAIL_ORDERS = (None, None, PAIR_FIRST * 2, PAIR_FIRST[:1], PAIR_FIRST[:1])
TAIL_SPREADS = ((LOW_FIRST,), (BIT_FIRST,), (LOW_FIRST, BIT_FIRST, LOW_FIRST, BIT_FIRST), (LOW_FIRST,), (LOW_FIRST,))
EVERY = slice(None)


def each_block(free, body):
    if not free:
        body(())
        return

    def step(i, carried):
        body(tuple(lax.rem(i // 2 ** (free - 1 - n), 2) for n in range(free)))
        return carried

    lax.fori_loop(0, 2**free, step, 0)


def part_columns(columns, parts, k):
    return pl.ds(k * (columns // parts), columns // parts)


def region(chosen, dims, columns):
    return tuple(chosen.get(d, EVERY) for d in dims) + (EVERY, columns)


class Halving:
    def __init__(self, link, orders, local, scratch, given=None):
        self.link, self.own, self.orders, self.local, self.given = link, link.own, orders, local, given
        self.cores, *self.arrived, self.load_sem, self.core_sem, self.half_sem = scratch
        self.parts = len(orders)

    def columns(self, k):
        return part_columns(self.local.shape[-1], self.parts, k)

    def lead(self, core):
        return () if self.given is not None else (core,)

    def of_pair(self, y, k):
        return region({"pair": y}, DIMS, self.columns(k))

    def loading(self, k, y):
        at = self.of_pair(y, k)
        kept = (2 * y + self.own["core"],) + at[1:]
        return pltpu.make_async_copy(self.given.at[kept], self.local.at[at], self.load_sem.at[k, y])

    def giving(self, k, y):
        at = self.of_pair(y, k)
        other = 1 - self.own["core"]
        if self.given is not None:
            src = self.given.at[(2 * y + other,) + at[1:]]
        else:
            src = self.local.at[(other,) + at]
        return src, self.cores.at[at], (self.core_sem.at[0, k, y], self.core_sem.at[1, k, y]), "core"

    def give(self, k):
        for y in range(2):
            self.link.send(functools.partial(self.giving, k, y))
            if self.given is not None:
                self.loading(k, y).start()

    def join(self, k):
        for y in range(2):
            if self.given is not None:
                self.loading(k, y).wait()
            sems = (self.core_sem.at[0, k, y], self.core_sem.at[1, k, y])
            self.link.receive(self.cores.at[self.of_pair(y, k)], sems, "core")

        def add(index):
            at = index + (EVERY, self.columns(k))
            kept = self.lead(self.own["core"]) + at
            self.local[kept] = self.local[kept] + self.cores[at]

        each_block(4, add)
        self.halve(k, 0)

    def half(self, k, step):
        dim = self.orders[k][step]
        chosen = {d: self.own[d] for d in self.orders[k][:step]}
        chosen[dim] = 1 - self.own[dim]
        at = self.lead(self.own["core"]) + region(chosen, DIMS, self.columns(k))
        sems = (self.half_sem.at[0, k, step], self.half_sem.at[1, k, step])
        return self.local.at[at], self.arrived[step].at[k], sems, dim

    def halve(self, k, step):
        self.link.send(functools.partial(self.half, k, step))

    def halved(self, k, step, done=None):
        sems = (self.half_sem.at[0, k, step], self.half_sem.at[1, k, step])
        self.link.receive(self.arrived[step].at[k], sems, self.orders[k][step])
        chosen = {d: self.own[d] for d in self.orders[k][: step + 1]}
        free = [d for d in DIMS if d not in chosen]

        def add(index):
            at = tuple(chosen[d] if d in chosen else index[free.index(d)] for d in DIMS)
            kept = self.lead(self.own["core"]) + at + (EVERY, self.columns(k))
            total = self.local[kept] + self.arrived[step][(k,) + index + (EVERY, EVERY)]
            if step < 3:
                self.local[kept] = total
            else:
                done(k, total)

        each_block(len(free), add)
        if step < 3:
            self.halve(k, step + 1)

    @staticmethod
    def scratch(shape, parts):
        rows, columns = shape
        dma = pltpu.SemaphoreType.DMA
        low = jnp.bfloat16
        shapes = [pltpu.VMEM((2, 2, 2, 2, rows, columns), low)]
        shapes += [pltpu.VMEM((parts,) + (2,) * (3 - step) + (rows, columns // parts), low) for step in range(4)]
        return shapes + [dma((parts, 2)), dma((2, parts, 2)), dma((2, parts, 4))]


class Spreading:
    def __init__(self, link, orders, full, sems):
        self.link, self.own, self.orders, self.full, self.sems = link, link.own, orders, full, sems
        self.parts = len(orders)

    def columns(self, k):
        return part_columns(self.full.shape[-1], self.parts, k)

    def put(self, k, value):
        at = tuple(self.own[d] for d in DIMS[1:]) + (EVERY, self.columns(k))
        self.full[at] = value
        self.pass_on(k, 0)

    def held(self, k, step):
        chosen = {d: self.own[d] for d in self.orders[k][step:]}
        here = self.full.at[region(chosen, DIMS[1:], self.columns(k))]
        return here, here, (self.sems.at[0, k, step], self.sems.at[1, k, step]), self.orders[k][step]

    def pass_on(self, k, step):
        self.link.send(functools.partial(self.held, k, step))

    def take(self, k, step):
        dim = self.orders[k][step]
        chosen = {d: self.own[d] for d in self.orders[k][step:]}
        chosen[dim] = 1 - self.own[dim]
        there = self.full.at[region(chosen, DIMS[1:], self.columns(k))]
        self.link.receive(there, (self.sems.at[0, k, step], self.sems.at[1, k, step]), dim)
        if step < 2:
            self.pass_on(k, step + 1)

    @staticmethod
    def scratch(shape, parts):
        return [pltpu.VMEM((2, 2, 2) + shape, jnp.bfloat16), pltpu.SemaphoreType.DMA((2, parts, 3))]


def run_events(events, last):
    events = sorted(events, key=lambda event: event[0])
    for step in range(last + 1):
        actions = [action for time, action in events if min(int(time), last) == step]
        if actions:

            @pl.when(pl.program_id(0) == step)
            def _():
                for action in actions:
                    action()


def block_rows(values, row, rows):
    return values[row : row + 1, :]


def lane_index(shape):
    return lax.broadcasted_iota(jnp.int32, shape, 1)


def dot(left, right):
    return jnp.dot(left, right, preferred_element_type=jnp.float32)


def smooth(values):
    share = jax.nn.sigmoid(values)
    return values * share, share


TAPS = 4
BIAS_ROW, STEP_ROW, SKIP_ROW, GAIN_ROW = 4, 5, 6, 7


def row_masks(lens_ref, start_ref, length):
    shape = (length, LANES)
    position = lax.broadcasted_iota(jnp.int32, shape, 0)
    cluster = jnp.zeros(shape, jnp.int32)
    begin = 0
    for slot in range(lens_ref.shape[1]):
        size = lens_ref[0, slot]
        flag = jnp.where((start_ref[0, slot] > 0) & (size > 0), 1, 0)
        cluster = cluster + jnp.where(position >= begin, flag, 0)
        begin = begin + size
    lane = lane_index(shape)
    masks = jnp.where((lane == 0) & (position < begin), 1.0, 0.0)
    for offset in range(1, TAPS):
        same = (lane == offset) & (position >= offset) & (cluster == pltpu.roll(cluster, offset, 0))
        masks = jnp.where(same, 1.0, masks)
    return masks


def front_kernel(
    lens_ref, start_ref, tokens_ref, gain_ref, w_ref, rows_ref, xproj_ref, inner_ref, pre_ref, u_ref, dbc_ref, xn_ref, xnt_ref, mask_ref
):
    @pl.when(pl.program_id(0) == 0)
    def _():
        mask_ref[...] = row_masks(lens_ref, start_ref, mask_ref.shape[0])
        x = tokens_ref[...].astype(jnp.float32)
        inv = lax.rsqrt(jnp.mean(x * x, axis=1, keepdims=True) + EPSILON)
        xn = (x * inv * gain_ref[...]).astype(jnp.bfloat16)
        xn_ref[...] = xn
        xnt_ref[...] = xn.T
        dbc_ref[...] = jnp.zeros_like(dbc_ref)

    inner = dot(xn_ref[...], w_ref[...])
    rows = rows_ref[...]
    pre = block_rows(rows, BIAS_ROW, 1) + block_rows(rows, TAPS - 1, 1) * inner
    for offset in range(1, TAPS):
        shifted = pltpu.roll(inner, offset, 0) * mask_ref[:, offset : offset + 1]
        pre = pre + block_rows(rows, TAPS - 1 - offset, 1) * shifted
    u = smooth(pre)[0].astype(jnp.bfloat16)
    inner_ref[...] = inner.astype(inner_ref.dtype)
    pre_ref[...] = pre
    u_ref[...] = u
    dbc_ref[...] += transposed_product(u, xproj_ref[...])


def whole_spec(shape):
    return pl.BlockSpec(shape, lambda i: (0,) * len(shape))


def columns_spec(rows, block):
    return pl.BlockSpec((rows, block), lambda i: (0, i))


def rows_spec(block, columns):
    return pl.BlockSpec((block, columns), lambda i: (i, 0))


def front(lens, starts, tokens, gain, inner_w, by_channel, xproj_t, block=512):
    length, features = tokens.shape
    width = inner_w.shape[1]
    low, wide = jnp.bfloat16, jnp.float32
    return pl.pallas_call(
        front_kernel,
        grid=(width // block,),
        in_specs=[
            pl.BlockSpec(memory_space=pltpu.SMEM),
            pl.BlockSpec(memory_space=pltpu.SMEM),
            whole_spec(tokens.shape),
            whole_spec(gain.shape),
            columns_spec(features, block),
            columns_spec(by_channel.shape[0], block),
            columns_spec(LANES, block),
        ],
        out_specs=[
            columns_spec(length, block),
            columns_spec(length, block),
            columns_spec(length, block),
            whole_spec((length, LANES)),
            whole_spec((length, features)),
            whole_spec((features, length)),
            whole_spec((length, LANES)),
        ],
        out_shape=[
            jax.ShapeDtypeStruct((length, width), low),
            jax.ShapeDtypeStruct((length, width), wide),
            jax.ShapeDtypeStruct((length, width), low),
            jax.ShapeDtypeStruct((length, LANES), wide),
            jax.ShapeDtypeStruct((length, features), low),
            jax.ShapeDtypeStruct((features, length), low),
            jax.ShapeDtypeStruct((length, LANES), wide),
        ],
        compiler_params=pltpu.CompilerParams(vmem_limit_bytes=60 << 20),
        name="front",
    )(lens, starts, tokens, gain, inner_w, by_channel, xproj_t)


def spread_states(dbc, first, states):
    rows = QLEN * states
    repeated = jnp.broadcast_to(dbc[:, None, :], (QLEN, states, LANES)).reshape(rows, LANES)
    state = lax.broadcasted_iota(jnp.int32, (rows, LANES), 0) % states
    own = jnp.where(lane_index((rows, LANES)) == first + state, repeated, 0.0)
    return jnp.broadcast_to(jnp.sum(own, axis=1, keepdims=True), (rows, LANES))


def diagonal_states(dbc, first, states):
    rows = QLEN * states
    pick = (
        lax.broadcasted_iota(jnp.int32, (LANES, rows), 0) == first + lane_index((LANES, rows)) % states
    ).astype(jnp.bfloat16)
    tiled = dot(dbc.astype(jnp.bfloat16), pick)
    own = lane_index((QLEN, rows)) // states == lax.broadcasted_iota(jnp.int32, (QLEN, rows), 0)
    return jnp.where(own, tiled, 0.0).astype(jnp.bfloat16)


def step_rank(dbc, rank):
    return jnp.where(lane_index(dbc.shape) < rank, dbc, 0.0).astype(jnp.bfloat16)


def twice(values):
    return jnp.concatenate([values] * (WIDE // LANES), axis=1)


def forward_kernel(rank, group, count, u_ref, dbc_ref, mask_ref, rows_ref, dtproj_ref, rate_ref, *refs):
    shards, (y_ref, h_ref, dt_ref), outs = refs[:count], refs[count : count + 3], refs[count + 3 : 2 * count + 3]
    (state, long_s, feed_s, b_s, cblk_s), scratch = refs[2 * count + 3 : 2 * count + 8], refs[2 * count + 8 :]
    blocks, _, width = long_s.shape
    states = rate_ref.shape[0]
    span = QLEN * states
    in_ref, out_ref = shards
    gather = Gather((in_ref.at[:, pl.ds(width, width)], out_ref), outs, scratch)
    run_stages(gather.stages[:-1], FORWARD_STEPS)

    @pl.when(pl.program_id(0) == 0)
    def _():
        state[...] = jnp.zeros_like(state)

    rank_rows = step_rank(dbc_ref[...], rank)
    keep = mask_ref[:, 1:2] > 0
    for c in range(0, width, WIDE):
        s = slice(c, c + WIDE)
        dt = jax.nn.softplus(dot(rank_rows, dtproj_ref[:, s]) + rows_ref[STEP_ROW : STEP_ROW + 1, s])
        dt_ref[:, s] = dt
        long = jnp.where(keep, dt, NEVER)
        feed = dt * u_ref[:, s].astype(jnp.float32)
        for j in range(blocks):
            long_s[j, :, s] = long[j * QLEN : (j + 1) * QLEN]
            feed_s[j, :, s] = feed[j * QLEN : (j + 1) * QLEN]
    for j in range(blocks):
        dbc = dbc_ref[j * QLEN : (j + 1) * QLEN, :]
        b_s[j * span : (j + 1) * span, :] = spread_states(dbc, rank, states)
        cblk_s[j * QLEN : (j + 1) * QLEN, :] = diagonal_states(dbc, rank + states, states)

    def block(j, carried):
        r0 = pl.multiple_of(j * QLEN, QLEN)
        h0 = pl.multiple_of(j * span, span)
        for c0 in range(0, width, group * WIDE):
            columns = [slice(c, c + WIDE) for c in range(c0, c0 + group * WIDE, WIDE)]
            held = [state[:, s] for s in columns]
            rates = [rate_ref[:, s] for s in columns]
            for t in range(QLEN):
                b_t = twice(b_s[pl.ds(h0 + t * states, states), :])
                for k, s in enumerate(columns):
                    decay = jnp.exp2(long_s[j, t : t + 1, s] * rates[k])
                    held[k] = decay * held[k] + b_t * feed_s[j, t : t + 1, s]
                    h_ref[pl.ds(h0 + t * states, states), s] = held[k].astype(h_ref.dtype)
            for k, s in enumerate(columns):
                state[:, s] = held[k]
            s = slice(c0, c0 + group * WIDE)
            y_ref[pl.ds(r0, QLEN), s] = dot(cblk_s[pl.ds(r0, QLEN), :], h_ref[pl.ds(h0, span), s])
        return carried

    lax.fori_loop(0, blocks, block, 0)
    run_stages(gather.stages[-1:], (pl.num_programs(0) - 1,))


def scan_forward(rank, u, dbc, masks, by_channel, dtproj, rate2, shards, collective_id, blocks=2, group=2):
    count = len(shards)
    shapes = [(shards[0].shape[0], shards[0].shape[1] // 2), shards[1].shape]
    anywhere = [pl.BlockSpec(memory_space=pl.ANY)] * count
    tokens, width = u.shape
    states = rate2.shape[0]
    rows = blocks * QLEN
    y, h, dt, *gathered = pl.pallas_call(
        functools.partial(forward_kernel, rank, group, count),
        grid=(tokens // rows,),
        in_specs=[
            rows_spec(rows, width),
            rows_spec(rows, LANES),
            rows_spec(rows, masks.shape[1]),
            whole_spec(by_channel.shape),
            whole_spec(dtproj.shape),
            whole_spec(rate2.shape),
            *anywhere,
        ],
        out_specs=[rows_spec(rows, width), rows_spec(rows * states, width), rows_spec(rows, width), *anywhere],
        out_shape=[
            jax.ShapeDtypeStruct((tokens, width), jnp.float32),
            jax.ShapeDtypeStruct((tokens * states, width), jnp.bfloat16),
            jax.ShapeDtypeStruct((tokens, width), jnp.float32),
            *(gathered_shape(shape) for shape in shapes),
        ],
        scratch_shapes=[
            pltpu.VMEM((states, width), jnp.float32),
            pltpu.VMEM((blocks, QLEN, width), jnp.float32),
            pltpu.VMEM((blocks, QLEN, width), jnp.float32),
            pltpu.VMEM((rows * states, LANES), jnp.float32),
            pltpu.VMEM((rows, QLEN * states), jnp.bfloat16),
            *Gather.scratch(shapes),
        ],
        compiler_params=pltpu.CompilerParams(
            collective_id=collective_id, has_side_effects=True, vmem_limit_bytes=60 << 20
        ),
        name="scan_forward",
    )(u, dbc, masks, by_channel, dtproj, rate2, *shards)
    return y, h, dt, gathered


def middle_kernel(
    xn_ref, xnt_ref, gate_ref, y_ref, u_ref, rows_ref, out_ref, cot_ref, tokens_ref, mask_ref,
    mixed_ref, dy_ref, dgate_ref, outgrad_ref, gategrad_ref, skip_ref, dxn_ref, branch, dbranch
):
    live = mask_ref[:, 0:1]

    @pl.when(pl.program_id(0) == 0)
    def _():
        branch[...] = jnp.zeros_like(branch)
        dxn_ref[...] = jnp.zeros_like(dxn_ref)
        dbranch[...] = (live * cot_ref[...].astype(jnp.float32)).astype(jnp.bfloat16)

    gate = dot(xn_ref[...], gate_ref[...])
    opened, share = smooth(gate)
    u = u_ref[...].astype(jnp.float32)
    y = y_ref[...] + rows_ref[SKIP_ROW : SKIP_ROW + 1, :] * u
    gated = (y * opened).astype(jnp.bfloat16)
    d_branch = dbranch[...]
    branch[...] += dot(gated, out_ref[...])
    outgrad_ref[...] = rows_product(gated, d_branch).astype(outgrad_ref.dtype)
    d_gated = transposed_product(d_branch, out_ref[...])
    d_y = d_gated * opened
    dy_ref[...] = d_y
    skip_ref[...] = jnp.sum(d_y * u, axis=0, keepdims=True)
    d_gate = (d_gated * y * share * (1.0 + gate * (1.0 - share))).astype(jnp.bfloat16)
    dgate_ref[...] = d_gate
    gategrad_ref[...] = dot(xnt_ref[...], d_gate).astype(gategrad_ref.dtype)
    dxn_ref[...] += transposed_product(d_gate, gate_ref[...])

    @pl.when(pl.program_id(0) == pl.num_programs(0) - 1)
    def _():
        mixed_ref[...] = (tokens_ref[...].astype(jnp.float32) + live * branch[...]).astype(mixed_ref.dtype)


def middle(xn, xnt, gate_w, y, u, by_channel, out_w, cotangent, tokens, masks, block=512):
    length, features = tokens.shape
    width = gate_w.shape[1]
    low, wide = jnp.bfloat16, jnp.float32
    channels = columns_spec(length, block)
    return pl.pallas_call(
        middle_kernel,
        grid=(width // block,),
        in_specs=[
            whole_spec(xn.shape),
            whole_spec(xnt.shape),
            columns_spec(features, block),
            channels,
            channels,
            columns_spec(by_channel.shape[0], block),
            rows_spec(block, features),
            whole_spec(tokens.shape),
            whole_spec(tokens.shape),
            whole_spec(masks.shape),
        ],
        out_specs=[
            whole_spec(tokens.shape),
            channels,
            channels,
            rows_spec(block, features),
            columns_spec(features, block),
            columns_spec(1, block),
            whole_spec(tokens.shape),
        ],
        out_shape=[
            jax.ShapeDtypeStruct(tokens.shape, low),
            jax.ShapeDtypeStruct((length, width), wide),
            jax.ShapeDtypeStruct((length, width), low),
            jax.ShapeDtypeStruct((width, features), low),
            jax.ShapeDtypeStruct((features, width), low),
            jax.ShapeDtypeStruct((1, width), wide),
            jax.ShapeDtypeStruct(tokens.shape, wide),
        ],
        scratch_shapes=[pltpu.VMEM(tokens.shape, wide), pltpu.VMEM(tokens.shape, low)],
        compiler_params=pltpu.CompilerParams(vmem_limit_bytes=60 << 20),
        name="middle",
    )(xn, xnt, gate_w, y, u, by_channel, out_w, cotangent, tokens, masks)


def backward_kernel(rank, count, steps, u_ref, dt_ref, dy_ref, dbc_ref, mask_ref, h_ref, before_ref, rows_ref, dtproj_ref, rate2_ref, rate_ref, *refs):
    grads, (du_ref, ddbc_ref, ldt_ref, dtproj_grad, bias_grad) = refs[:count], refs[count : count + 5]
    sums, refs = refs[count + 5 : 2 * count + 5], refs[2 * count + 5 :]
    message, long_s, feed_s, c_s, bblk_s, g_s, lrate_s, db_s, dc_s, before_s, e_s, lsum_s, small_s = refs[:13]
    blocks, _, width = dt_ref.shape
    states = rate_ref.shape[0]
    span = QLEN * states
    low, wide = jnp.bfloat16, jnp.float32
    link = Link(own_bits())
    per = (len(refs) - 13) // count
    halvings = []
    for a in range(count):
        local, *scratch = refs[13 + a * per : 13 + (a + 1) * per]
        halvings.append(Halving(link, EARLY_ORDERS[a], local, scratch, given=grads[a]))

    def keep_sum(out, parts, k, total):
        out[:, part_columns(out.shape[1], parts, k)] = total

    events = [(0, lambda: greet(link.own, ("core", "pair", "bit", "low", "high")))]
    for halving, out, part_times in zip(halvings, sums, BACKWARD_TIMES):
        done = functools.partial(keep_sum, out, halving.parts)
        for k, (give, join, *times) in enumerate(part_times):
            events += [(give, functools.partial(halving.give, k)), (join, functools.partial(halving.join, k))]
            events += [(time, functools.partial(halving.halved, k, step, done)) for step, time in enumerate(times)]
    final = steps - 1
    run_events([event for event in events if event[0] <= final], final)

    @pl.when(pl.program_id(0) == 0)
    def _():
        message[...] = jnp.zeros_like(message)
        ldt_ref[...] = jnp.zeros_like(ldt_ref)
        dtproj_grad[...] = jnp.zeros_like(dtproj_grad)
        bias_grad[...] = jnp.zeros_like(bias_grad)

    for j in range(blocks):
        own = slice(j * QLEN, (j + 1) * QLEN)
        keep = mask_ref[own, 1:2] > 0
        for c in range(0, width, WIDE):
            s = slice(c, c + WIDE)
            dt = dt_ref[j, :, s]
            long_s[j, :, s] = jnp.where(keep, dt, NEVER)
            feed_s[j, :, s] = dt * u_ref[own, s].astype(wide)
        dbc = dbc_ref[own, :]
        c_s[j * span : (j + 1) * span, :] = spread_states(dbc, rank + states, states)
        bblk_s[own, :] = diagonal_states(dbc, rank, states)
    by_token = (
        lane_index((QLEN, span)) // states == lax.broadcasted_iota(jnp.int32, (QLEN, span), 0)
    ).astype(low)
    state_of = lax.broadcasted_iota(jnp.int32, (span, LANES), 0) % states
    at_b = lane_index((span, LANES)) == rank + state_of
    at_c = lane_index((span, LANES)) == rank + states + state_of

    def block(step, carried):
        j = blocks - 1 - step
        r0 = pl.multiple_of(j * QLEN, QLEN)
        h0 = pl.multiple_of(j * span, span)

        @pl.when(j == 0)
        def _():
            before_s[...] = before_ref[...]

        @pl.when(j > 0)
        def _():
            before_s[...] = h_ref[pl.ds(pl.multiple_of(jnp.maximum(h0 - states, 0), states), states), :]

        db_s[...] = jnp.zeros_like(db_s)
        dc_s[...] = jnp.zeros_like(dc_s)
        for c in range(0, width, WIDE):
            s = slice(c, c + WIDE)
            held, rate2, rate, total = message[:, s], rate2_ref[:, s], rate_ref[:, s], ldt_ref[:, s]
            pending = None
            now = h_ref[pl.ds(h0 + (QLEN - 1) * states, states), s]
            for t in reversed(range(QLEN)):
                at = slice(t * states, (t + 1) * states)
                d_y = jnp.broadcast_to(dy_ref[j, t : t + 1, s], (states, WIDE))
                g = twice(c_s[pl.ds(h0 + t * states, states), :]) * d_y + held
                g_low = g.astype(low)
                g_s[at, s] = g_low
                dt = jnp.broadcast_to(long_s[j, t : t + 1, s], (states, WIDE))
                held = jnp.exp2(dt * rate2) * g
                before = before_s[:, s] if t == 0 else h_ref[pl.ds(h0 + (t - 1) * states, states), s]
                l = held.astype(low) * before
                lrate_s[at, s] = l * rate
                ldt = l * dt.astype(low)
                if pending is None:
                    pending = ldt
                else:
                    total = total + (pending + ldt).astype(wide)
                    pending = None
                feed = jnp.broadcast_to(feed_s[j, t : t + 1, s], (states, WIDE))
                for sums, product in ((db_s, g_low * feed.astype(low)), (dc_s, now * d_y.astype(low))):
                    sums[at, :] += (product[:, :LANES] + product[:, LANES:]).astype(wide)
                now = before
            message[:, s] = held
            ldt_ref[:, s] = total
            e_s[pl.ds(r0, QLEN), s] = dot(bblk_s[pl.ds(r0, QLEN), :], g_s[:, s])
            lsum_s[pl.ds(r0, QLEN), s] = dot(by_token, lrate_s[:, s])
        d_b = jnp.sum(db_s[...], axis=1, keepdims=True)
        d_c = jnp.sum(dc_s[...], axis=1, keepdims=True)
        placed = jnp.where(at_b, d_b, jnp.where(at_c, d_c, 0.0)).astype(low)
        small_s[pl.ds(r0, QLEN), :] = dot(by_token, placed)
        return carried

    lax.fori_loop(0, blocks, block, 0)
    rank_rows = step_rank(dbc_ref[...], rank)
    d_rank = jnp.zeros(rank_rows.shape, wide)
    tokens = blocks * QLEN
    for c in range(0, width, WIDE):
        s = slice(c, c + WIDE)
        dt = dt_ref[:, :, s].reshape(tokens, WIDE)
        d_y = dy_ref[:, :, s].reshape(tokens, WIDE)
        e = e_s[:, s]
        share = jnp.where(dt < 0.01, dt * (1.0 - dt * (0.5 - dt * (1.0 / 6.0))), 1.0 - jnp.exp(-dt))
        d_dt = e * u_ref[:, s].astype(wide) + lsum_s[:, s]
        d_step = (d_dt * share).astype(low)
        bias_grad[:, s] += jnp.sum(d_step.astype(wide), axis=0, keepdims=True)
        dtproj_grad[:, s] += rows_product(rank_rows, d_step)
        d_rank += transposed_product(d_step, dtproj_ref[:, s])
        du_ref[:, s] = d_y * rows_ref[SKIP_ROW : SKIP_ROW + 1, s] + e * dt
    ddbc_ref[...] = (jnp.where(lane_index(d_rank.shape) < rank, d_rank, 0.0) + small_s[...]).astype(low)
    run_events([event for event in events if event[0] > final] + [(steps, link.finish)], final)


def scan_backward(rank, u, dt, d_y, dbc, masks, h, by_channel, dtproj, rate2, rate, grads, collective_id, blocks=2):
    count = len(grads)
    anywhere = [pl.BlockSpec(memory_space=pl.ANY)] * count
    tokens, width = u.shape
    states = rate2.shape[0]
    rows = blocks * QLEN
    steps = tokens // rows
    low, wide = jnp.bfloat16, jnp.float32
    back = lambda i: (steps - 1 - i, 0)
    flat = lambda columns: pl.BlockSpec((rows, columns), back)
    cubes = pl.BlockSpec((blocks, QLEN, width), lambda i: (steps - 1 - i, 0, 0))
    in_blocks = lambda v: v.reshape(tokens // QLEN, QLEN, width)
    du, ddbc, ldt, dtproj_grad, bias_grad, *sums = pl.pallas_call(
        functools.partial(backward_kernel, rank, count, steps),
        grid=(steps,),
        in_specs=[
            flat(width),
            cubes,
            cubes,
            flat(LANES),
            flat(masks.shape[1]),
            pl.BlockSpec((rows * states, width), back),
            pl.BlockSpec((states, width), lambda i: (jnp.maximum((steps - 1 - i) * rows - 1, 0), 0)),
            whole_spec(by_channel.shape),
            whole_spec(dtproj.shape),
            whole_spec(rate2.shape),
            whole_spec(rate.shape),
            *anywhere,
        ],
        out_specs=[
            flat(width),
            flat(LANES),
            whole_spec(rate2.shape),
            whole_spec(dtproj.shape),
            whole_spec((1, width)),
            *(whole_spec(g.shape[4:]) for g in grads),
        ],
        out_shape=[
            jax.ShapeDtypeStruct((tokens, width), wide),
            jax.ShapeDtypeStruct((tokens, LANES), low),
            jax.ShapeDtypeStruct(rate2.shape, wide),
            jax.ShapeDtypeStruct(dtproj.shape, wide),
            jax.ShapeDtypeStruct((1, width), wide),
            *(jax.ShapeDtypeStruct(g.shape[4:], g.dtype) for g in grads),
        ],
        scratch_shapes=[
            pltpu.VMEM((states, width), wide),
            pltpu.VMEM((blocks, QLEN, width), wide),
            pltpu.VMEM((blocks, QLEN, width), wide),
            pltpu.VMEM((rows * states, LANES), wide),
            pltpu.VMEM((rows, QLEN * states), low),
            pltpu.VMEM((QLEN * states, width), low),
            pltpu.VMEM((QLEN * states, width), low),
            pltpu.VMEM((QLEN * states, LANES), wide),
            pltpu.VMEM((QLEN * states, LANES), wide),
            pltpu.VMEM((states, width), low),
            pltpu.VMEM((rows, width), wide),
            pltpu.VMEM((rows, width), wide),
            pltpu.VMEM((rows, LANES), wide),
            *(
                shape
                for g, orders in zip(grads, EARLY_ORDERS)
                for shape in (pltpu.VMEM((2, 2, 2, 2) + g.shape[4:], low), *Halving.scratch(g.shape[4:], len(orders)))
            ),
        ],
        compiler_params=pltpu.CompilerParams(
            collective_id=collective_id, has_side_effects=True, vmem_limit_bytes=60 << 20
        ),
        name="scan_backward",
    )(u, in_blocks(dt), in_blocks(d_y), dbc, masks, h, h, by_channel, dtproj, rate2, rate, *grads)
    return du, ddbc, ldt, dtproj_grad, bias_grad, sums


def tail_kernel(
    steps, rank, count, du_ref, ddbc_ref, xproj_ref, u_ref, inner_ref, pre_ref, rows_ref, mask_ref, xnt_ref, w_ref, dgate_ref, tokens_ref, cot_ref, gain_ref,
    dtproj_ref, alog_ref, bias_ref, skip_ref, *refs
):
    wide, low = jnp.float32, jnp.bfloat16
    pieces, tokengrad_ref, outs = refs[:count], refs[count], refs[count + 1 : 2 * count + 4]
    refs = refs[2 * count + 4 :]
    w_s, x_s, cot_s, dxn, dinner_s, xproj_s, row_s, inner_s, small_s, gain_s, load_sem, out_sem = refs[:12]
    link = Link(own_bits())
    halving_refs, spreading_refs = refs[12 : 12 + 24], refs[12 + 24 :]
    spreadings = [Spreading(link, orders, *spreading_refs[2 * a : 2 * a + 2]) for a, orders in enumerate(TAIL_SPREADS)]
    inner_sum = Halving(link, TAIL_ORDERS[2], inner_s, halving_refs[:8])
    small_sum = Halving(link, TAIL_ORDERS[3], small_s, halving_refs[8:16])
    gain_sum = Halving(link, TAIL_ORDERS[4], gain_s, halving_refs[16:])
    block = du_ref.shape[1]
    here = pl.program_id(0)
    columns = pl.ds(pl.multiple_of(here * block, block), block)
    final = steps - 1

    loads = [(w_ref, w_s), (tokens_ref, x_s), (cot_ref, cot_s), (dgate_ref, dxn)]
    loads = [functools.partial(pltpu.make_async_copy, src, dst, load_sem.at[i]) for i, (src, dst) in enumerate(loads)]

    def start():
        for load in loads:
            load().start()
        greet(link.own, ("core", "pair", "bit", "low", "high"))
        for piece, spreading in zip(pieces, spreadings):
            for k in range(spreading.parts):
                spreading.put(k, piece[:, spreading.columns(k)])

    def add_up(events, halving, spreading, part_times):
        for k, times in enumerate(part_times):
            give, join, *halves = times[:6]
            events += [(give, functools.partial(halving.give, k)), (join, functools.partial(halving.join, k))]
            events += [
                (time, functools.partial(halving.halved, k, step, spreading.put)) for step, time in enumerate(halves)
            ]
            events += [(time, functools.partial(spreading.take, k, step)) for step, time in enumerate(times[6:])]

    events = []
    for spreading, times in zip(spreadings, SPREAD_TIMES):
        events += [(time, functools.partial(spreading.take, 0, step)) for step, time in enumerate(times)]
    add_up(events, inner_sum, spreadings[count], INNER_TIMES)
    add_up(events, small_sum, spreadings[count + 1], SMALL_TIMES)
    add_up(events, gain_sum, spreadings[count + 2], GAIN_TIMES)

    def through_inner(chunk):
        if chunk == 0:
            for load in loads:
                load().wait()
        size = dinner_s.shape[1] // len(DXN_TIMES)
        own = slice(chunk * size, (chunk + 1) * size)
        dxn[...] += transposed_product(dinner_s[:, own], w_s[:, own])

    def through_norm():
        x = x_s[...].astype(wide)
        inv = lax.rsqrt(jnp.mean(x * x, axis=1, keepdims=True) + EPSILON)
        x_hat = x * inv
        gain_grad = jnp.sum(dxn[...] * x_hat, axis=0, keepdims=True)
        d_hat = dxn[...] * gain_ref[...]
        level = jnp.mean(d_hat * x_hat, axis=1, keepdims=True)
        tokengrad_ref[...] = cot_s[...].astype(wide) + inv * (d_hat - x_hat * level)
        size = gain_grad.shape[1] // 4
        rows, lanes = gain_s.shape[5:]
        gain_s[...] = jnp.zeros_like(gain_s)
        for shard in range(4):
            parts = [gain_grad[:, c : c + lanes] for c in range(shard * size, (shard + 1) * size, lanes)]
            block = jnp.concatenate(parts + [jnp.zeros((rows - len(parts), lanes), wide)], axis=0)
            gain_s[shard % 2, shard // 2, 0, 0, 0] = block.astype(low)

    events += [(time, functools.partial(through_inner, chunk)) for chunk, time in enumerate(DXN_TIMES)]
    events.append((NORM_TIME, through_norm))
    run_events([(0, start)], final)

    rows = rows_ref[...]
    pre = pre_ref[...]
    share = jax.nn.sigmoid(pre)
    d_u = du_ref[...] + dot(ddbc_ref[...], xproj_ref[...])
    d_pre = d_u * share * (1.0 + pre * (1.0 - share))
    inner = inner_ref[...].astype(wide)
    d_inner = block_rows(rows, TAPS - 1, 1) * d_pre
    sums = [None] * 8
    sums[TAPS - 1] = jnp.sum(d_pre * inner, axis=0, keepdims=True)
    sums[BIAS_ROW] = jnp.sum(d_pre, axis=0, keepdims=True)
    for offset in range(1, TAPS):
        same = d_pre * mask_ref[:, offset : offset + 1]
        back = pltpu.roll(same, same.shape[0] - offset, 0)
        sums[TAPS - 1 - offset] = jnp.sum(back * inner, axis=0, keepdims=True)
        d_inner = d_inner + block_rows(rows, TAPS - 1 - offset, 1) * back
    nothing = jnp.zeros_like(sums[0])
    row_s[:, columns] = jnp.concatenate([nothing if v is None else v for v in sums], axis=0)
    xproj_s[:, columns] = rows_product(ddbc_ref[...], u_ref[...])
    d_inner = d_inner.astype(low)
    inner_grad = dot(xnt_ref[...], d_inner).astype(low)
    size = inner_grad.shape[0] // 4
    for shard in range(4):
        own_rows = inner_grad[shard * size : (shard + 1) * size]
        inner_s[shard % 2, shard // 2, :, :, :, :, columns] = own_rows.reshape(2, 2, 2, size // 8, block)
    dinner_s[:, columns] = d_inner

    @pl.when(here == final)
    def _():
        owned = xproj_s.shape[1] // 4
        states = alog_ref.shape[0]
        row = lax.broadcasted_iota(jnp.int32, (8, owned), 0)
        for shard in range(4):
            own = slice(shard * owned, (shard + 1) * owned)
            rows = row_s[:, own]
            for at, extra in ((STEP_ROW, bias_ref[:, own]), (SKIP_ROW, skip_ref[:, own])):
                rows = jnp.where(row == at, extra, rows)
            stacked = [dtproj_ref[:rank, own], alog_ref[:, own], xproj_s[: rank + 2 * states, own], rows]
            height = 8 * small_s.shape[5]
            stacked.append(jnp.zeros((height - sum(v.shape[0] for v in stacked), owned), wide))
            stacked = jnp.concatenate(stacked, axis=0).astype(low)
            small_s[shard % 2, shard // 2] = stacked.reshape(2, 2, 2, height // 8, owned)

    run_events(events, final)

    @pl.when(here == final)
    def _():
        stores = [pltpu.make_async_copy(s.full, o, out_sem.at[i]) for i, (s, o) in enumerate(zip(spreadings, outs))]
        for copy in stores:
            copy.start()
        for copy in stores:
            copy.wait()
        link.finish()


def tail(
    rank, du, ddbc, xproj_t, u, inner, pre, by_channel, masks, xnt, inner_w, dxn_gate, tokens, cotangent, gain,
    dtproj_grad, alog_grad, bias_grad, skip_grad, pieces, collective_id, block=256,
):
    length, features = tokens.shape
    width = inner_w.shape[1]
    count = len(pieces)
    steps = width // block
    inner_shape = (features // 32, width)
    used = 2 * rank + 3 * alog_grad.shape[0] + 8
    small_shape = ((used + -used % LANES) // 8, width // 4)
    gain_shape = (16, LANES)
    shapes = [*(p.shape for p in pieces), inner_shape, small_shape, gain_shape]
    low, wide = jnp.bfloat16, jnp.float32
    channels = columns_spec(length, block)
    token_grad, *sums = pl.pallas_call(
        functools.partial(tail_kernel, steps, rank, count),
        grid=(steps,),
        in_specs=[
            channels,
            whole_spec(ddbc.shape),
            columns_spec(LANES, block),
            channels,
            channels,
            channels,
            columns_spec(by_channel.shape[0], block),
            whole_spec(masks.shape),
            whole_spec(xnt.shape),
            *[pl.BlockSpec(memory_space=pl.ANY)] * 4,
            whole_spec(gain.shape),
            whole_spec(dtproj_grad.shape),
            whole_spec(alog_grad.shape),
            whole_spec(bias_grad.shape),
            whole_spec(skip_grad.shape),
            *(whole_spec(p.shape) for p in pieces),
        ],
        out_specs=[whole_spec(tokens.shape), *[pl.BlockSpec(memory_space=pl.ANY)] * (count + 3)],
        out_shape=[
            jax.ShapeDtypeStruct(tokens.shape, wide),
            *(jax.ShapeDtypeStruct((2, 2, 2) + shape, low) for shape in shapes),
        ],
        scratch_shapes=[
            pltpu.VMEM(inner_w.shape, low),
            pltpu.VMEM(tokens.shape, low),
            pltpu.VMEM(tokens.shape, low),
            pltpu.VMEM(tokens.shape, wide),
            pltpu.VMEM((length, width), low),
            pltpu.VMEM((LANES, width), wide),
            pltpu.VMEM((8, width), wide),
            pltpu.VMEM((2, 2, 2, 2, 2) + inner_shape, low),
            pltpu.VMEM((2, 2, 2, 2, 2) + small_shape, low),
            pltpu.VMEM((2, 2, 2, 2, 2) + gain_shape, low),
            pltpu.SemaphoreType.DMA((4,)),
            pltpu.SemaphoreType.DMA((count + 3,)),
            *Halving.scratch(inner_shape, len(TAIL_ORDERS[2])),
            *Halving.scratch(small_shape, len(TAIL_ORDERS[3])),
            *Halving.scratch(gain_shape, len(TAIL_ORDERS[4])),
            *(v for shape, orders in zip(shapes, TAIL_SPREADS) for v in Spreading.scratch(shape, len(orders))),
        ],
        compiler_params=pltpu.CompilerParams(
            collective_id=collective_id, has_side_effects=True, vmem_limit_bytes=60 << 20
        ),
        name="tail",
    )(
        du, ddbc, xproj_t, u, inner, pre, by_channel, masks, xnt, inner_w, dxn_gate, tokens, cotangent, gain,
        dtproj_grad, alog_grad, bias_grad, skip_grad, *pieces,
    )
    return token_grad, sums


def finish_kernel(
    rank, states, gate_ref, out_ref, inner_ref, small_ref, gain_ref,
    in_grad, out_grad, dtproj_grad, alog_grad, xproj_grad, conv_grad, convb_grad, dtb_grad, skip_grad, gain_grad
):
    wide = jnp.float32
    width = inner_ref.shape[1]
    in_grad[:, :width] = inner_ref[...].astype(wide)
    in_grad[:, width:] = gate_ref[...].astype(wide)
    out_grad[...] = out_ref[...].astype(wide)

    @pl.when(pl.program_id(0) == 0)
    def _():
        small = small_ref[...].astype(wide)
        used = 2 * rank + 3 * states
        dtproj_grad[...] = small[:rank]
        alog_grad[...] = small[rank : rank + states]
        xproj_grad[...] = small[rank + states : rank + states + LANES].T[:, : rank + 2 * states]
        rows = small[used : used + 8]
        conv_grad[...] = rows[:TAPS]
        for ref, row in ((convb_grad, BIAS_ROW), (dtb_grad, STEP_ROW), (skip_grad, SKIP_ROW)):
            ref[...] = rows[row : row + 1]
        for part in range(gain_grad.shape[1] // LANES):
            gain_grad[:, part * LANES : (part + 1) * LANES] = gain_ref[part : part + 1, :].astype(wide)


def finish(rank, states, gate, out, inner, small, gain, features, steps=4):
    wide = jnp.float32
    owned = small.shape[1]
    width = inner.shape[1]
    small_shapes = [(rank, owned), (states, owned), (owned, rank + 2 * states), (TAPS, owned)]
    small_shapes += [(1, owned)] * 3 + [(1, features)]
    in_shape, out_shape = (inner.shape[0], 2 * width), out.shape
    return pl.pallas_call(
        functools.partial(finish_kernel, rank, states),
        grid=(steps,),
        in_specs=[
            rows_spec(gate.shape[0] // steps, width),
            rows_spec(out.shape[0] // steps, out.shape[1]),
            rows_spec(inner.shape[0] // steps, width),
            whole_spec(small.shape),
            whole_spec(gain.shape),
        ],
        out_specs=[
            rows_spec(in_shape[0] // steps, in_shape[1]),
            rows_spec(out_shape[0] // steps, out_shape[1]),
            *(whole_spec(shape) for shape in small_shapes),
        ],
        out_shape=[jax.ShapeDtypeStruct(shape, wide) for shape in (in_shape, out_shape, *small_shapes)],
        compiler_params=pltpu.CompilerParams(vmem_limit_bytes=60 << 20),
        name="finish",
    )(gate, out, inner, small, gain)


def add_groups(sums):
    groups = lax.axis_size("dp") // GROUP
    if groups == 1:
        return sums
    alike = [[g * GROUP + i for g in range(groups)] for i in range(GROUP)]
    return lax.psum(sums, "dp", axis_index_groups=alike)


def body(
    tokens,
    cotangent,
    prot_lens,
    clus_start,
    norm_gain,
    in_w,
    conv_w,
    conv_b,
    xproj_w,
    dtproj_w,
    dt_bias,
    a_log,
    d_skip,
    out_w,
):
    features = norm_gain.shape[0]
    width = in_w.shape[1] // 2
    rank, owned = dtproj_w.shape
    states = a_log.shape[0]
    used = 2 * rank + 3 * states + 8
    inner_w, packed = gather_weights(in_w, dtproj_w, a_log, xproj_w, conv_w, (conv_b, dt_bias, d_skip, norm_gain), 1)
    inner_w = inner_w.reshape(-1, width)
    gain = packed[:, used - 1, :features].reshape(1, -1).astype(jnp.float32)
    packed = jnp.swapaxes(packed, 0, 1).reshape(packed.shape[1], -1)
    dtproj = packed[:LANES]
    decay_rate = -jnp.exp(packed[rank : rank + states].astype(jnp.float32))
    rate2 = decay_rate * LOG2E
    xproj_t = packed[rank + states : rank + states + LANES]
    by_channel = packed[used - 8 : used].astype(jnp.float32)
    inner, pre, u, dbc, xn, xnt, masks = front(prot_lens, clus_start, tokens, gain, inner_w, by_channel, xproj_t)
    y, h, dt, (gate_w, out_full) = scan_forward(
        rank, u, dbc, masks, by_channel, dtproj, rate2, (in_w, out_w), 2
    )
    gate_w = gate_w.reshape(-1, width)
    out_full = out_full.reshape(-1, out_full.shape[2])
    mixed, d_y, _, out_local, gate_local, skip_local, dxn_gate = middle(
        xn, xnt, gate_w, y, u, by_channel, out_full, cotangent, tokens, masks
    )
    in_pieces = lambda v: v.reshape((4, 2, 2, 2, v.shape[0] // 32, v.shape[1]))
    du, ddbc, ldt, dtproj_local, dtb_local, early_pieces = scan_backward(
        rank,
        u,
        dt,
        d_y,
        dbc,
        masks,
        h,
        by_channel,
        dtproj,
        rate2,
        decay_rate.astype(jnp.bfloat16),
        [in_pieces(gate_local), in_pieces(out_local)],
        3,
    )
    token_grad, sums = tail(
        rank,
        du,
        ddbc,
        xproj_t,
        u,
        inner,
        pre,
        by_channel,
        masks,
        xnt,
        inner_w,
        dxn_gate,
        tokens,
        cotangent,
        gain,
        dtproj_local,
        ldt * decay_rate,
        dtb_local,
        skip_local,
        early_pieces,
        4,
    )
    sums = [v.reshape(-1, v.shape[-1]) for v in sums]
    grads = add_groups(finish(rank, states, *sums, features))
    in_grad, out_grad, dtproj_grad, alog_grad, xproj_grad, conv_grad, convb_grad, dtb_grad, skip_grad, gain_grad = grads
    return (
        mixed,
        token_grad,
        gain_grad[0],
        in_grad,
        conv_grad,
        convb_grad[0],
        xproj_grad,
        dtproj_grad,
        dtb_grad[0],
        alog_grad,
        skip_grad[0],
        out_grad,
    )


def solution(mesh):
    in_specs = (
        P(("dp", "fsdp"), None),
        P(("dp", "fsdp"), None),
        P(("dp", "fsdp"), None),
        P(("dp", "fsdp"), None),
        P("fsdp"),
        P("fsdp", None),
        P(None, "fsdp"),
        P("fsdp"),
        P("fsdp", None),
        P(None, "fsdp"),
        P("fsdp"),
        P(None, "fsdp"),
        P("fsdp"),
        P("fsdp", None),
    )
    out_specs = (
        P(("dp", "fsdp"), None),
        P(("dp", "fsdp"), None),
        P("fsdp"),
        P("fsdp", None),
        P(None, "fsdp"),
        P("fsdp"),
        P("fsdp", None),
        P(None, "fsdp"),
        P("fsdp"),
        P(None, "fsdp"),
        P("fsdp"),
        P("fsdp", None),
    )
    return jax.shard_map(body, mesh=mesh, in_specs=in_specs, out_specs=out_specs, check_vma=False)
```

```python
import functools

import jax
import jax.numpy as jnp
from jax import lax
from jax.experimental import pallas as pl
from jax.experimental.pallas import tpu as pltpu
from jax.sharding import PartitionSpec as P

QLEN = 16
LANES = 128
WIDE = 256
SPREAD_TIMES = ((4.02, 7.06, 13.1), (6.02, 12.02, 13.16))
INNER_TIMES = (
    (1, 3.02, 7.04, 12.04, 13.2, 13.32, 13.44, 13.52, 13.62),
    (3, 4.04, 10.04, 13.02, 13.12, 13.28, 13.42, 13.48, 13.6),
    (5, 7.02, 13.06, 13.22, 13.34, 13.46, 13.58, 13.7, 13.78),
    (7, 9.02, 13.08, 13.24, 13.36, 13.5, 13.64, 13.72, 13.8),
)
SMALL_TIMES = ((7, 10.02, 13.14, 13.26, 13.38, 13.54, 13.66, 13.74, 13.82),)
GAIN_TIMES = ((12.01, 13.04, 13.18, 13.3, 13.4, 13.56, 13.68, 13.76, 13.84),)
DXN_TIMES = (8, 9.5, 10.5, 11.5)
NORM_TIME = 12
NEVER = 1e30
LOG2E = 1.4426950408889634
FORWARD_STEPS = (0, 4, 6, 7, 7, 9, 9, 11, 11, 13, 13, 13, 14)
BACKWARD_TIMES = (
    ((0, 2.1, 6.1, 9.1, 11.1, 13.1), (0, 3.1, 7.1, 10.1, 12.1, 14.1)),
    ((0, 4.1, 8.1, 11.2, 13.2, 15.1), (0, 5.1, 9.2, 12.2, 14.2, 16.1)),
)


EPSILON = 1e-05


def rows_product(left, right):
    return lax.dot_general(
        left, right, (((0,), (0,)), ((), ())), preferred_element_type=jnp.float32
    )


def transposed_product(left, weight):
    return lax.dot_general(
        left, weight, (((1,), (1,)), ((), ())), preferred_element_type=jnp.float32
    )


MESH = pl.DeviceIdType.MESH
GROUP = 8


def own_bits():
    d, f = lax.axis_index("dp"), lax.axis_index("fsdp")
    inside = lax.rem(d, GROUP)
    return {
        "pair": f // 2,
        "core": lax.rem(f, 2),
        "high": inside // 4,
        "low": lax.rem(inside // 2, 2),
        "bit": lax.rem(inside, 2),
    }


def across(own, dim):
    d, f = lax.axis_index("dp"), lax.axis_index("fsdp")
    step = {"pair": 2, "core": 1, "high": 4, "low": 2, "bit": 1}[dim]
    flip = step * (1 - 2 * own[dim])
    return (d, f + flip) if dim in ("pair", "core") else (d + flip, f)


def greet(own, dims):
    barrier = pltpu.get_barrier_semaphore()
    for dim in dims:
        pl.semaphore_signal(barrier, inc=1, device_id=across(own, dim), device_id_type=MESH)
    pl.semaphore_wait(barrier, len(dims))


class Link:
    def __init__(self, own):
        self.own = own
        self.sent = []

    def copy(self, src, dst, sems, dim):
        return pltpu.make_async_remote_copy(
            src_ref=src,
            dst_ref=dst,
            send_sem=sems[0],
            recv_sem=sems[1],
            device_id=across(self.own, dim),
            device_id_type=MESH,
        )

    def send(self, described):
        self.copy(*described()).start()
        self.sent.append(described)

    def receive(self, ref, sems, dim):
        self.copy(ref, ref, sems, dim).wait_recv()

    def finish(self):
        for described in self.sent:
            self.copy(*described()).wait_send()


class Gather:
    def __init__(self, shards, outs, scratch, made=None):
        self.shards, self.outs, self.made = shards, outs, made
        self.count = len(shards)
        self.stage = scratch[: self.count]
        self.load_sem, self.core_sem, self.hop_sem, self.whole_sem = scratch[self.count :]
        self.own = own_bits()
        self.link = Link(self.own)
        pair, core = self.own["pair"], self.own["core"]
        self.mine = 2 * pair + core
        self.theirs = 2 * (1 - pair) + core
        self.sibling = 2 * pair + 1 - core
        self.beyond = 2 * (1 - pair) + 1 - core
        bit, low = self.own["bit"], self.own["low"]
        self.kinds = ((bit, low), (1 - bit, low), (bit, 1 - low), (1 - bit, 1 - low))
        pair, near, far = (
            [[functools.partial(stage, a, half) for half in range(2)] for a in range(2)]
            for stage in (self.from_pair, self.from_near, self.from_far)
        )
        self.stages = [self.begin, pair[0][0], pair[0][1], near[0][0], pair[1][0], near[0][1], pair[1][1]]
        self.stages += [far[0][0], far[1][0], near[1][0], far[0][1], far[1][1], near[1][1], self.end]

    def eighth(self, a, kind, half):
        rows = self.shards[a].shape[0] // 8
        bit, low = self.kinds[kind]
        return pl.ds(pl.multiple_of((2 * (bit + 2 * low) + half) * rows, rows), rows)

    def hop(self, a, kind, half):
        return self.hop_sem.at[0, a, kind, half], self.hop_sem.at[1, a, kind, half]

    def to_core(self, a, kind, half):
        return self.core_sem.at[0, a, kind, half], self.core_sem.at[1, a, kind, half]

    def whole(self, a):
        return self.whole_sem.at[0, a], self.whole_sem.at[1, a]

    def load(self, a):
        return pltpu.make_async_copy(self.shards[a], self.stage[a], self.load_sem.at[a])

    def in_place(self, a):
        return self.made is not None and a == self.count - 1

    def store(self, a):
        return pltpu.make_async_copy(self.stage[a], self.outs[a].at[self.mine], self.load_sem.at[a])

    def begin(self):
        greet(self.own, ("core", "pair", "bit", "low"))
        for a in range(self.count):
            if self.in_place(a):
                self.made()
            for kind in (0, 3)[: a + 1]:
                for half in range(2):
                    self.link.send(functools.partial(self.to_pair, a, kind, half))
        for a in range(self.count):
            if not self.in_place(a):
                self.load(a).start()
            self.link.send(functools.partial(self.own_to_core, a))

    def to_pair(self, a, kind, half):
        rows = self.eighth(a, kind, half)
        return self.shards[a].at[rows], self.outs[a].at[self.mine, rows], self.hop(a, kind, half), "pair"

    def own_to_core(self, a):
        return self.shards[a], self.outs[a].at[self.mine], self.whole(a), "core"

    def came(self, a, kind, half):
        return self.outs[a].at[self.theirs, self.eighth(a, kind, half)]

    def onward(self, a, kind, half, new_kind, dim):
        ref = self.came(a, kind, half)
        return ref, ref, self.to_core(a, kind, half) if dim == "core" else self.hop(a, new_kind, half), dim

    def pass_on(self, a, kind, half, new_kind, dim):
        self.link.send(functools.partial(self.onward, a, kind, half, new_kind, dim))

    def arrive(self, a, kind, half, dim):
        self.link.receive(self.came(a, kind, half), self.hop(a, kind, half), dim)
        self.pass_on(a, kind, half, kind, "core")

    def from_pair(self, a, half):
        self.arrive(a, 0, half, "pair")
        self.pass_on(a, 0, half, 1, "bit")
        self.pass_on(a, 0, half, 2, "low")
        if half == 1:
            if not self.in_place(a):
                self.load(a).wait()
            self.store(a).start()

    def from_near(self, a, half):
        self.arrive(a, 1, half, "bit")
        if a == 0 and half == 0:
            self.pass_on(a, 1, 0, 3, "low")
        self.arrive(a, 2, half, "low")
        if a == 0 and half == 1:
            self.pass_on(a, 2, 1, 3, "bit")

    def from_far(self, a, half):
        self.arrive(a, 3, half, "pair" if a == 1 else ("low", "bit")[half])

    def end(self):
        for a in range(self.count):
            self.link.receive(self.outs[a].at[self.sibling], self.whole(a), "core")
            for kind in range(4):
                for half in range(2):
                    ref = self.outs[a].at[self.beyond, self.eighth(a, kind, half)]
                    self.link.receive(ref, self.to_core(a, kind, half), "core")
            self.store(a).wait()
        self.link.finish()

    @staticmethod
    def scratch(shapes):
        count = len(shapes)
        dma = pltpu.SemaphoreType.DMA
        staged = [pltpu.VMEM(shape, jnp.bfloat16) for shape in shapes]
        return staged + [dma((count,)), dma((2, count, 4, 2)), dma((2, count, 4, 2)), dma((2, count))]


def gather_kernel(
    width, in_ref, dtproj_ref, alog_ref, xproj_ref, taps_ref, bias_ref, step_ref, skip_ref, gain_ref, inner_out, packed_out, *scratch
):
    packed = scratch[1]

    def pack():
        low = packed.dtype
        rank, states, columns = dtproj_ref.shape[0], alog_ref.shape[0], xproj_ref.shape[1]
        eye = (
            lax.broadcasted_iota(jnp.int32, (columns, columns), 0) == lane_index((columns, columns))
        ).astype(low)
        at = rank + states + columns
        owned = packed.shape[1]
        wide = jnp.float32
        packed[:rank, :] = dtproj_ref[...]
        packed[rank : rank + states, :] = alog_ref[...]
        packed[rank + states : at, :] = transposed_product(eye, xproj_ref[...]).astype(low)
        row = lax.broadcasted_iota(jnp.int32, (16, owned), 0)
        rows = jnp.concatenate([taps_ref[...].astype(wide), jnp.zeros((16 - TAPS, owned), wide)], axis=0)
        for place, ref in ((BIAS_ROW, bias_ref), (STEP_ROW, step_ref), (SKIP_ROW, skip_ref), (GAIN_ROW, gain_ref)):
            values = ref[...].astype(wide).reshape(1, ref.shape[0])
            if ref.shape[0] < owned:
                values = jnp.concatenate([values, jnp.zeros((1, owned - ref.shape[0]), wide)], axis=1)
            rows = jnp.where(row == place, values, rows)
        packed[at : at + 16, :] = rows.astype(low)
        packed[at + 16 :, :] = jnp.zeros((packed.shape[0] - at - 16, owned), low)

    gather = Gather((in_ref.at[:, pl.ds(0, width)], packed), (inner_out, packed_out), scratch, made=pack)
    for stage in gather.stages:
        stage()


def gathered_shape(shape):
    return jax.ShapeDtypeStruct((4,) + shape, jnp.bfloat16)


def gather_weights(in_w, dtproj_w, a_log, xproj_w, conv_w, vectors, collective_id):
    anywhere, vmem = pl.BlockSpec(memory_space=pl.ANY), pl.BlockSpec(memory_space=pltpu.VMEM)
    used = dtproj_w.shape[0] + a_log.shape[0] + xproj_w.shape[1] + TAPS + len(vectors)
    shapes = [(in_w.shape[0], in_w.shape[1] // 2), (used + -used % LANES, conv_w.shape[1])]
    return pl.pallas_call(
        functools.partial(gather_kernel, shapes[0][1]),
        out_shape=[gathered_shape(shape) for shape in shapes],
        in_specs=[anywhere] + [vmem] * (4 + len(vectors)),
        out_specs=[anywhere, anywhere],
        scratch_shapes=Gather.scratch(shapes),
        compiler_params=pltpu.CompilerParams(
            collective_id=collective_id, has_side_effects=True, vmem_limit_bytes=60 << 20
        ),
        name="gather_weights",
    )(in_w, dtproj_w, a_log, xproj_w, conv_w, *vectors)


def run_stages(stages, at_steps):
    for step in sorted(set(at_steps)):

        @pl.when(pl.program_id(0) == step)
        def _():
            for stage, at in zip(stages, at_steps):
                if at == step:
                    stage()


DIMS = ("pair", "high", "low", "bit")
MIXED = (
    ("pair", "bit", "low", "high"),
    ("bit", "low", "pair", "high"),
    ("low", "pair", "bit", "high"),
    ("pair", "low", "bit", "high"),
)
PAIR_FIRST = (("pair", "bit", "low", "high"), ("pair", "low", "bit", "high"))
LOW_FIRST, BIT_FIRST = ("high", "low", "bit"), ("high", "bit", "low")
EARLY_ORDERS = (MIXED[:2], MIXED[2:])
TAIL_ORDERS = (None, None, PAIR_FIRST * 2, PAIR_FIRST[:1], PAIR_FIRST[:1])
TAIL_SPREADS = ((LOW_FIRST,), (BIT_FIRST,), (LOW_FIRST, BIT_FIRST, LOW_FIRST, BIT_FIRST), (LOW_FIRST,), (LOW_FIRST,))
EVERY = slice(None)


def each_block(free, body):
    if not free:
        body(())
        return

    def step(i, carried):
        body(tuple(lax.rem(i // 2 ** (free - 1 - n), 2) for n in range(free)))
        return carried

    lax.fori_loop(0, 2**free, step, 0)


def part_columns(columns, parts, k):
    return pl.ds(k * (columns // parts), columns // parts)


def region(chosen, dims, columns):
    return tuple(chosen.get(d, EVERY) for d in dims) + (EVERY, columns)


class Halving:
    def __init__(self, link, orders, local, scratch, given=None):
        self.link, self.own, self.orders, self.local, self.given = link, link.own, orders, local, given
        self.cores, *self.arrived, self.load_sem, self.core_sem, self.half_sem = scratch
        self.parts = len(orders)

    def columns(self, k):
        return part_columns(self.local.shape[-1], self.parts, k)

    def lead(self, core):
        return () if self.given is not None else (core,)

    def of_pair(self, y, k):
        return region({"pair": y}, DIMS, self.columns(k))

    def loading(self, k, y):
        at = self.of_pair(y, k)
        kept = (2 * y + self.own["core"],) + at[1:]
        return pltpu.make_async_copy(self.given.at[kept], self.local.at[at], self.load_sem.at[k, y])

    def giving(self, k, y):
        at = self.of_pair(y, k)
        other = 1 - self.own["core"]
        if self.given is not None:
            src = self.given.at[(2 * y + other,) + at[1:]]
        else:
            src = self.local.at[(other,) + at]
        return src, self.cores.at[at], (self.core_sem.at[0, k, y], self.core_sem.at[1, k, y]), "core"

    def give(self, k):
        for y in range(2):
            self.link.send(functools.partial(self.giving, k, y))
            if self.given is not None:
                self.loading(k, y).start()

    def join(self, k):
        for y in range(2):
            if self.given is not None:
                self.loading(k, y).wait()
            sems = (self.core_sem.at[0, k, y], self.core_sem.at[1, k, y])
            self.link.receive(self.cores.at[self.of_pair(y, k)], sems, "core")

        def add(index):
            at = index + (EVERY, self.columns(k))
            kept = self.lead(self.own["core"]) + at
            self.local[kept] = self.local[kept] + self.cores[at]

        each_block(4, add)
        self.halve(k, 0)

    def half(self, k, step):
        dim = self.orders[k][step]
        chosen = {d: self.own[d] for d in self.orders[k][:step]}
        chosen[dim] = 1 - self.own[dim]
        at = self.lead(self.own["core"]) + region(chosen, DIMS, self.columns(k))
        sems = (self.half_sem.at[0, k, step], self.half_sem.at[1, k, step])
        return self.local.at[at], self.arrived[step].at[k], sems, dim

    def halve(self, k, step):
        self.link.send(functools.partial(self.half, k, step))

    def halved(self, k, step, done=None):
        sems = (self.half_sem.at[0, k, step], self.half_sem.at[1, k, step])
        self.link.receive(self.arrived[step].at[k], sems, self.orders[k][step])
        chosen = {d: self.own[d] for d in self.orders[k][: step + 1]}
        free = [d for d in DIMS if d not in chosen]

        def add(index):
            at = tuple(chosen[d] if d in chosen else index[free.index(d)] for d in DIMS)
            kept = self.lead(self.own["core"]) + at + (EVERY, self.columns(k))
            total = self.local[kept] + self.arrived[step][(k,) + index + (EVERY, EVERY)]
            if step < 3:
                self.local[kept] = total
            else:
                done(k, total)

        each_block(len(free), add)
        if step < 3:
            self.halve(k, step + 1)

    @staticmethod
    def scratch(shape, parts):
        rows, columns = shape
        dma = pltpu.SemaphoreType.DMA
        low = jnp.bfloat16
        shapes = [pltpu.VMEM((2, 2, 2, 2, rows, columns), low)]
        shapes += [pltpu.VMEM((parts,) + (2,) * (3 - step) + (rows, columns // parts), low) for step in range(4)]
        return shapes + [dma((parts, 2)), dma((2, parts, 2)), dma((2, parts, 4))]


class Spreading:
    def __init__(self, link, orders, full, sems):
        self.link, self.own, self.orders, self.full, self.sems = link, link.own, orders, full, sems
        self.parts = len(orders)

    def columns(self, k):
        return part_columns(self.full.shape[-1], self.parts, k)

    def put(self, k, value):
        at = tuple(self.own[d] for d in DIMS[1:]) + (EVERY, self.columns(k))
        self.full[at] = value
        self.pass_on(k, 0)

    def held(self, k, step):
        chosen = {d: self.own[d] for d in self.orders[k][step:]}
        here = self.full.at[region(chosen, DIMS[1:], self.columns(k))]
        return here, here, (self.sems.at[0, k, step], self.sems.at[1, k, step]), self.orders[k][step]

    def pass_on(self, k, step):
        self.link.send(functools.partial(self.held, k, step))

    def take(self, k, step):
        dim = self.orders[k][step]
        chosen = {d: self.own[d] for d in self.orders[k][step:]}
        chosen[dim] = 1 - self.own[dim]
        there = self.full.at[region(chosen, DIMS[1:], self.columns(k))]
        self.link.receive(there, (self.sems.at[0, k, step], self.sems.at[1, k, step]), dim)
        if step < 2:
            self.pass_on(k, step + 1)

    @staticmethod
    def scratch(shape, parts):
        return [pltpu.VMEM((2, 2, 2) + shape, jnp.bfloat16), pltpu.SemaphoreType.DMA((2, parts, 3))]


def run_events(events, last):
    events = sorted(events, key=lambda event: event[0])
    for step in range(last + 1):
        actions = [action for time, action in events if min(int(time), last) == step]
        if actions:

            @pl.when(pl.program_id(0) == step)
            def _():
                for action in actions:
                    action()


def block_rows(values, row, rows):
    return values[row : row + 1, :]


def lane_index(shape):
    return lax.broadcasted_iota(jnp.int32, shape, 1)


def dot(left, right):
    return jnp.dot(left, right, preferred_element_type=jnp.float32)


def smooth(values):
    share = jax.nn.sigmoid(values)
    return values * share, share


TAPS = 4
BIAS_ROW, STEP_ROW, SKIP_ROW, GAIN_ROW = 4, 5, 6, 7


def row_masks(lens_ref, start_ref, length):
    shape = (length, LANES)
    position = lax.broadcasted_iota(jnp.int32, shape, 0)
    cluster = jnp.zeros(shape, jnp.int32)
    begin = 0
    for slot in range(lens_ref.shape[1]):
        size = lens_ref[0, slot]
        flag = jnp.where((start_ref[0, slot] > 0) & (size > 0), 1, 0)
        cluster = cluster + jnp.where(position >= begin, flag, 0)
        begin = begin + size
    lane = lane_index(shape)
    masks = jnp.where((lane == 0) & (position < begin), 1.0, 0.0)
    for offset in range(1, TAPS):
        same = (lane == offset) & (position >= offset) & (cluster == pltpu.roll(cluster, offset, 0))
        masks = jnp.where(same, 1.0, masks)
    return masks


def front_kernel(
    lens_ref, start_ref, tokens_ref, gain_ref, w_ref, rows_ref, xproj_ref, inner_ref, pre_ref, u_ref, dbc_ref, xn_ref, xnt_ref, mask_ref
):
    @pl.when(pl.program_id(0) == 0)
    def _():
        mask_ref[...] = row_masks(lens_ref, start_ref, mask_ref.shape[0])
        x = tokens_ref[...].astype(jnp.float32)
        inv = lax.rsqrt(jnp.mean(x * x, axis=1, keepdims=True) + EPSILON)
        xn = (x * inv * gain_ref[...]).astype(jnp.bfloat16)
        xn_ref[...] = xn
        xnt_ref[...] = xn.T
        dbc_ref[...] = jnp.zeros_like(dbc_ref)

    inner = dot(xn_ref[...], w_ref[...])
    rows = rows_ref[...]
    pre = block_rows(rows, BIAS_ROW, 1) + block_rows(rows, TAPS - 1, 1) * inner
    for offset in range(1, TAPS):
        shifted = pltpu.roll(inner, offset, 0) * mask_ref[:, offset : offset + 1]
        pre = pre + block_rows(rows, TAPS - 1 - offset, 1) * shifted
    u = smooth(pre)[0].astype(jnp.bfloat16)
    inner_ref[...] = inner.astype(inner_ref.dtype)
    pre_ref[...] = pre
    u_ref[...] = u
    dbc_ref[...] += transposed_product(u, xproj_ref[...])


def whole_spec(shape):
    return pl.BlockSpec(shape, lambda i: (0,) * len(shape))


def columns_spec(rows, block):
    return pl.BlockSpec((rows, block), lambda i: (0, i))


def rows_spec(block, columns):
    return pl.BlockSpec((block, columns), lambda i: (i, 0))


def front(lens, starts, tokens, gain, inner_w, by_channel, xproj_t, block=512):
    length, features = tokens.shape
    width = inner_w.shape[1]
    low, wide = jnp.bfloat16, jnp.float32
    return pl.pallas_call(
        front_kernel,
        grid=(width // block,),
        in_specs=[
            pl.BlockSpec(memory_space=pltpu.SMEM),
            pl.BlockSpec(memory_space=pltpu.SMEM),
            whole_spec(tokens.shape),
            whole_spec(gain.shape),
            columns_spec(features, block),
            columns_spec(by_channel.shape[0], block),
            columns_spec(LANES, block),
        ],
        out_specs=[
            columns_spec(length, block),
            columns_spec(length, block),
            columns_spec(length, block),
            whole_spec((length, LANES)),
            whole_spec((length, features)),
            whole_spec((features, length)),
            whole_spec((length, LANES)),
        ],
        out_shape=[
            jax.ShapeDtypeStruct((length, width), low),
            jax.ShapeDtypeStruct((length, width), wide),
            jax.ShapeDtypeStruct((length, width), low),
            jax.ShapeDtypeStruct((length, LANES), wide),
            jax.ShapeDtypeStruct((length, features), low),
            jax.ShapeDtypeStruct((features, length), low),
            jax.ShapeDtypeStruct((length, LANES), wide),
        ],
        compiler_params=pltpu.CompilerParams(vmem_limit_bytes=60 << 20),
        name="front",
    )(lens, starts, tokens, gain, inner_w, by_channel, xproj_t)


def spread_states(dbc, first, states):
    rows = QLEN * states
    repeated = jnp.broadcast_to(dbc[:, None, :], (QLEN, states, LANES)).reshape(rows, LANES)
    state = lax.broadcasted_iota(jnp.int32, (rows, LANES), 0) % states
    own = jnp.where(lane_index((rows, LANES)) == first + state, repeated, 0.0)
    return jnp.broadcast_to(jnp.sum(own, axis=1, keepdims=True), (rows, LANES))


def diagonal_states(dbc, first, states):
    rows = QLEN * states
    pick = (
        lax.broadcasted_iota(jnp.int32, (LANES, rows), 0) == first + lane_index((LANES, rows)) % states
    ).astype(jnp.bfloat16)
    tiled = dot(dbc.astype(jnp.bfloat16), pick)
    own = lane_index((QLEN, rows)) // states == lax.broadcasted_iota(jnp.int32, (QLEN, rows), 0)
    return jnp.where(own, tiled, 0.0).astype(jnp.bfloat16)


def step_rank(dbc, rank):
    return jnp.where(lane_index(dbc.shape) < rank, dbc, 0.0).astype(jnp.bfloat16)


def twice(values):
    return jnp.concatenate([values] * (WIDE // LANES), axis=1)


def forward_kernel(rank, group, count, u_ref, dbc_ref, mask_ref, rows_ref, dtproj_ref, rate_ref, *refs):
    shards, (y_ref, h_ref, dt_ref), outs = refs[:count], refs[count : count + 3], refs[count + 3 : 2 * count + 3]
    (state, long_s, feed_s, b_s, cblk_s), scratch = refs[2 * count + 3 : 2 * count + 8], refs[2 * count + 8 :]
    blocks, _, width = long_s.shape
    states = rate_ref.shape[0]
    span = QLEN * states
    in_ref, out_ref = shards
    gather = Gather((in_ref.at[:, pl.ds(width, width)], out_ref), outs, scratch)
    run_stages(gather.stages[:-1], FORWARD_STEPS)

    @pl.when(pl.program_id(0) == 0)
    def _():
        state[...] = jnp.zeros_like(state)

    rank_rows = step_rank(dbc_ref[...], rank)
    keep = mask_ref[:, 1:2] > 0
    for c in range(0, width, WIDE):
        s = slice(c, c + WIDE)
        dt = jax.nn.softplus(dot(rank_rows, dtproj_ref[:, s]) + rows_ref[STEP_ROW : STEP_ROW + 1, s])
        dt_ref[:, s] = dt
        long = jnp.where(keep, dt, NEVER)
        feed = dt * u_ref[:, s].astype(jnp.float32)
        for j in range(blocks):
            long_s[j, :, s] = long[j * QLEN : (j + 1) * QLEN]
            feed_s[j, :, s] = feed[j * QLEN : (j + 1) * QLEN]
    for j in range(blocks):
        dbc = dbc_ref[j * QLEN : (j + 1) * QLEN, :]
        b_s[j * span : (j + 1) * span, :] = spread_states(dbc, rank, states)
        cblk_s[j * QLEN : (j + 1) * QLEN, :] = diagonal_states(dbc, rank + states, states)

    def block(j, carried):
        r0 = pl.multiple_of(j * QLEN, QLEN)
        h0 = pl.multiple_of(j * span, span)
        for c0 in range(0, width, group * WIDE):
            columns = [slice(c, c + WIDE) for c in range(c0, c0 + group * WIDE, WIDE)]
            held = [state[:, s] for s in columns]
            rates = [rate_ref[:, s] for s in columns]
            for t in range(QLEN):
                b_t = twice(b_s[pl.ds(h0 + t * states, states), :])
                for k, s in enumerate(columns):
                    decay = jnp.exp2(long_s[j, t : t + 1, s] * rates[k])
                    held[k] = decay * held[k] + b_t * feed_s[j, t : t + 1, s]
                    h_ref[pl.ds(h0 + t * states, states), s] = held[k].astype(h_ref.dtype)
            for k, s in enumerate(columns):
                state[:, s] = held[k]
            s = slice(c0, c0 + group * WIDE)
            y_ref[pl.ds(r0, QLEN), s] = dot(cblk_s[pl.ds(r0, QLEN), :], h_ref[pl.ds(h0, span), s])
        return carried

    lax.fori_loop(0, blocks, block, 0)
    run_stages(gather.stages[-1:], (pl.num_programs(0) - 1,))


def scan_forward(rank, u, dbc, masks, by_channel, dtproj, rate2, shards, collective_id, blocks=2, group=2):
    count = len(shards)
    shapes = [(shards[0].shape[0], shards[0].shape[1] // 2), shards[1].shape]
    anywhere = [pl.BlockSpec(memory_space=pl.ANY)] * count
    tokens, width = u.shape
    states = rate2.shape[0]
    rows = blocks * QLEN
    y, h, dt, *gathered = pl.pallas_call(
        functools.partial(forward_kernel, rank, group, count),
        grid=(tokens // rows,),
        in_specs=[
            rows_spec(rows, width),
            rows_spec(rows, LANES),
            rows_spec(rows, masks.shape[1]),
            whole_spec(by_channel.shape),
            whole_spec(dtproj.shape),
            whole_spec(rate2.shape),
            *anywhere,
        ],
        out_specs=[rows_spec(rows, width), rows_spec(rows * states, width), rows_spec(rows, width), *anywhere],
        out_shape=[
            jax.ShapeDtypeStruct((tokens, width), jnp.float32),
            jax.ShapeDtypeStruct((tokens * states, width), jnp.bfloat16),
            jax.ShapeDtypeStruct((tokens, width), jnp.float32),
            *(gathered_shape(shape) for shape in shapes),
        ],
        scratch_shapes=[
            pltpu.VMEM((states, width), jnp.float32),
            pltpu.VMEM((blocks, QLEN, width), jnp.float32),
            pltpu.VMEM((blocks, QLEN, width), jnp.float32),
            pltpu.VMEM((rows * states, LANES), jnp.float32),
            pltpu.VMEM((rows, QLEN * states), jnp.bfloat16),
            *Gather.scratch(shapes),
        ],
        compiler_params=pltpu.CompilerParams(
            collective_id=collective_id, has_side_effects=True, vmem_limit_bytes=60 << 20
        ),
        name="scan_forward",
    )(u, dbc, masks, by_channel, dtproj, rate2, *shards)
    return y, h, dt, gathered


def middle_kernel(
    xn_ref, xnt_ref, gate_ref, y_ref, u_ref, rows_ref, out_ref, cot_ref, tokens_ref, mask_ref,
    mixed_ref, dy_ref, dgate_ref, outgrad_ref, gategrad_ref, skip_ref, dxn_ref, branch, dbranch
):
    live = mask_ref[:, 0:1]

    @pl.when(pl.program_id(0) == 0)
    def _():
        branch[...] = jnp.zeros_like(branch)
        dxn_ref[...] = jnp.zeros_like(dxn_ref)
        dbranch[...] = (live * cot_ref[...].astype(jnp.float32)).astype(jnp.bfloat16)

    gate = dot(xn_ref[...], gate_ref[...])
    opened, share = smooth(gate)
    u = u_ref[...].astype(jnp.float32)
    y = y_ref[...] + rows_ref[SKIP_ROW : SKIP_ROW + 1, :] * u
    gated = (y * opened).astype(jnp.bfloat16)
    d_branch = dbranch[...]
    branch[...] += dot(gated, out_ref[...])
    outgrad_ref[...] = rows_product(gated, d_branch).astype(outgrad_ref.dtype)
    d_gated = transposed_product(d_branch, out_ref[...])
    d_y = d_gated * opened
    dy_ref[...] = d_y
    skip_ref[...] = jnp.sum(d_y * u, axis=0, keepdims=True)
    d_gate = (d_gated * y * share * (1.0 + gate * (1.0 - share))).astype(jnp.bfloat16)
    dgate_ref[...] = d_gate
    gategrad_ref[...] = dot(xnt_ref[...], d_gate).astype(gategrad_ref.dtype)
    dxn_ref[...] += transposed_product(d_gate, gate_ref[...])

    @pl.when(pl.program_id(0) == pl.num_programs(0) - 1)
    def _():
        mixed_ref[...] = (tokens_ref[...].astype(jnp.float32) + live * branch[...]).astype(mixed_ref.dtype)


def middle(xn, xnt, gate_w, y, u, by_channel, out_w, cotangent, tokens, masks, block=512):
    length, features = tokens.shape
    width = gate_w.shape[1]
    low, wide = jnp.bfloat16, jnp.float32
    channels = columns_spec(length, block)
    return pl.pallas_call(
        middle_kernel,
        grid=(width // block,),
        in_specs=[
            whole_spec(xn.shape),
            whole_spec(xnt.shape),
            columns_spec(features, block),
            channels,
            channels,
            columns_spec(by_channel.shape[0], block),
            rows_spec(block, features),
            whole_spec(tokens.shape),
            whole_spec(tokens.shape),
            whole_spec(masks.shape),
        ],
        out_specs=[
            whole_spec(tokens.shape),
            channels,
            channels,
            rows_spec(block, features),
            columns_spec(features, block),
            columns_spec(1, block),
            whole_spec(tokens.shape),
        ],
        out_shape=[
            jax.ShapeDtypeStruct(tokens.shape, low),
            jax.ShapeDtypeStruct((length, width), wide),
            jax.ShapeDtypeStruct((length, width), low),
            jax.ShapeDtypeStruct((width, features), low),
            jax.ShapeDtypeStruct((features, width), low),
            jax.ShapeDtypeStruct((1, width), wide),
            jax.ShapeDtypeStruct(tokens.shape, wide),
        ],
        scratch_shapes=[pltpu.VMEM(tokens.shape, wide), pltpu.VMEM(tokens.shape, low)],
        compiler_params=pltpu.CompilerParams(vmem_limit_bytes=60 << 20),
        name="middle",
    )(xn, xnt, gate_w, y, u, by_channel, out_w, cotangent, tokens, masks)


def backward_kernel(rank, count, steps, u_ref, dt_ref, dy_ref, dbc_ref, mask_ref, h_ref, before_ref, rows_ref, dtproj_ref, rate2_ref, rate_ref, *refs):
    grads, (du_ref, ddbc_ref, ldt_ref, dtproj_grad, bias_grad) = refs[:count], refs[count : count + 5]
    sums, refs = refs[count + 5 : 2 * count + 5], refs[2 * count + 5 :]
    message, long_s, feed_s, c_s, bblk_s, g_s, lrate_s, db_s, dc_s, before_s, e_s, lsum_s, small_s = refs[:13]
    blocks, _, width = dt_ref.shape
    states = rate_ref.shape[0]
    span = QLEN * states
    low, wide = jnp.bfloat16, jnp.float32
    link = Link(own_bits())
    per = (len(refs) - 13) // count
    halvings = []
    for a in range(count):
        local, *scratch = refs[13 + a * per : 13 + (a + 1) * per]
        halvings.append(Halving(link, EARLY_ORDERS[a], local, scratch, given=grads[a]))

    def keep_sum(out, parts, k, total):
        out[:, part_columns(out.shape[1], parts, k)] = total

    events = [(0, lambda: greet(link.own, ("core", "pair", "bit", "low", "high")))]
    for halving, out, part_times in zip(halvings, sums, BACKWARD_TIMES):
        done = functools.partial(keep_sum, out, halving.parts)
        for k, (give, join, *times) in enumerate(part_times):
            events += [(give, functools.partial(halving.give, k)), (join, functools.partial(halving.join, k))]
            events += [(time, functools.partial(halving.halved, k, step, done)) for step, time in enumerate(times)]
    final = steps - 1
    run_events([event for event in events if event[0] <= final], final)

    @pl.when(pl.program_id(0) == 0)
    def _():
        message[...] = jnp.zeros_like(message)
        ldt_ref[...] = jnp.zeros_like(ldt_ref)
        dtproj_grad[...] = jnp.zeros_like(dtproj_grad)
        bias_grad[...] = jnp.zeros_like(bias_grad)

    for j in range(blocks):
        own = slice(j * QLEN, (j + 1) * QLEN)
        keep = mask_ref[own, 1:2] > 0
        for c in range(0, width, WIDE):
            s = slice(c, c + WIDE)
            dt = dt_ref[j, :, s]
            long_s[j, :, s] = jnp.where(keep, dt, NEVER)
            feed_s[j, :, s] = dt * u_ref[own, s].astype(wide)
        dbc = dbc_ref[own, :]
        c_s[j * span : (j + 1) * span, :] = spread_states(dbc, rank + states, states)
        bblk_s[own, :] = diagonal_states(dbc, rank, states)
    by_token = (
        lane_index((QLEN, span)) // states == lax.broadcasted_iota(jnp.int32, (QLEN, span), 0)
    ).astype(low)
    state_of = lax.broadcasted_iota(jnp.int32, (span, LANES), 0) % states
    at_b = lane_index((span, LANES)) == rank + state_of
    at_c = lane_index((span, LANES)) == rank + states + state_of

    def block(step, carried):
        j = blocks - 1 - step
        r0 = pl.multiple_of(j * QLEN, QLEN)
        h0 = pl.multiple_of(j * span, span)

        @pl.when(j == 0)
        def _():
            before_s[...] = before_ref[...]

        @pl.when(j > 0)
        def _():
            before_s[...] = h_ref[pl.ds(pl.multiple_of(jnp.maximum(h0 - states, 0), states), states), :]

        db_s[...] = jnp.zeros_like(db_s)
        dc_s[...] = jnp.zeros_like(dc_s)
        for c in range(0, width, WIDE):
            s = slice(c, c + WIDE)
            held, rate2, rate, total = message[:, s], rate2_ref[:, s], rate_ref[:, s], ldt_ref[:, s]
            pending = None
            now = h_ref[pl.ds(h0 + (QLEN - 1) * states, states), s]
            for t in reversed(range(QLEN)):
                at = slice(t * states, (t + 1) * states)
                d_y = jnp.broadcast_to(dy_ref[j, t : t + 1, s], (states, WIDE))
                g = twice(c_s[pl.ds(h0 + t * states, states), :]) * d_y + held
                g_low = g.astype(low)
                g_s[at, s] = g_low
                dt = jnp.broadcast_to(long_s[j, t : t + 1, s], (states, WIDE))
                held = jnp.exp2(dt * rate2) * g
                before = before_s[:, s] if t == 0 else h_ref[pl.ds(h0 + (t - 1) * states, states), s]
                l = held.astype(low) * before
                lrate_s[at, s] = l * rate
                ldt = l * dt.astype(low)
                if pending is None:
                    pending = ldt
                else:
                    total = total + (pending + ldt).astype(wide)
                    pending = None
                feed = jnp.broadcast_to(feed_s[j, t : t + 1, s], (states, WIDE))
                for sums, product in ((db_s, g_low * feed.astype(low)), (dc_s, now * d_y.astype(low))):
                    sums[at, :] += (product[:, :LANES] + product[:, LANES:]).astype(wide)
                now = before
            message[:, s] = held
            ldt_ref[:, s] = total
            e_s[pl.ds(r0, QLEN), s] = dot(bblk_s[pl.ds(r0, QLEN), :], g_s[:, s])
            lsum_s[pl.ds(r0, QLEN), s] = dot(by_token, lrate_s[:, s])
        d_b = jnp.sum(db_s[...], axis=1, keepdims=True)
        d_c = jnp.sum(dc_s[...], axis=1, keepdims=True)
        placed = jnp.where(at_b, d_b, jnp.where(at_c, d_c, 0.0)).astype(low)
        small_s[pl.ds(r0, QLEN), :] = dot(by_token, placed)
        return carried

    lax.fori_loop(0, blocks, block, 0)
    rank_rows = step_rank(dbc_ref[...], rank)
    d_rank = jnp.zeros(rank_rows.shape, wide)
    tokens = blocks * QLEN
    for c in range(0, width, WIDE):
        s = slice(c, c + WIDE)
        dt = dt_ref[:, :, s].reshape(tokens, WIDE)
        d_y = dy_ref[:, :, s].reshape(tokens, WIDE)
        e = e_s[:, s]
        share = jnp.where(dt < 0.01, dt * (1.0 - dt * (0.5 - dt * (1.0 / 6.0))), 1.0 - jnp.exp(-dt))
        d_dt = e * u_ref[:, s].astype(wide) + lsum_s[:, s]
        d_step = (d_dt * share).astype(low)
        bias_grad[:, s] += jnp.sum(d_step.astype(wide), axis=0, keepdims=True)
        dtproj_grad[:, s] += rows_product(rank_rows, d_step)
        d_rank += transposed_product(d_step, dtproj_ref[:, s])
        du_ref[:, s] = d_y * rows_ref[SKIP_ROW : SKIP_ROW + 1, s] + e * dt
    ddbc_ref[...] = (jnp.where(lane_index(d_rank.shape) < rank, d_rank, 0.0) + small_s[...]).astype(low)
    run_events([event for event in events if event[0] > final] + [(steps, link.finish)], final)


def scan_backward(rank, u, dt, d_y, dbc, masks, h, by_channel, dtproj, rate2, rate, grads, collective_id, blocks=2):
    count = len(grads)
    anywhere = [pl.BlockSpec(memory_space=pl.ANY)] * count
    tokens, width = u.shape
    states = rate2.shape[0]
    rows = blocks * QLEN
    steps = tokens // rows
    low, wide = jnp.bfloat16, jnp.float32
    back = lambda i: (steps - 1 - i, 0)
    flat = lambda columns: pl.BlockSpec((rows, columns), back)
    cubes = pl.BlockSpec((blocks, QLEN, width), lambda i: (steps - 1 - i, 0, 0))
    in_blocks = lambda v: v.reshape(tokens // QLEN, QLEN, width)
    du, ddbc, ldt, dtproj_grad, bias_grad, *sums = pl.pallas_call(
        functools.partial(backward_kernel, rank, count, steps),
        grid=(steps,),
        in_specs=[
            flat(width),
            cubes,
            cubes,
            flat(LANES),
            flat(masks.shape[1]),
            pl.BlockSpec((rows * states, width), back),
            pl.BlockSpec((states, width), lambda i: (jnp.maximum((steps - 1 - i) * rows - 1, 0), 0)),
            whole_spec(by_channel.shape),
            whole_spec(dtproj.shape),
            whole_spec(rate2.shape),
            whole_spec(rate.shape),
            *anywhere,
        ],
        out_specs=[
            flat(width),
            flat(LANES),
            whole_spec(rate2.shape),
            whole_spec(dtproj.shape),
            whole_spec((1, width)),
            *(whole_spec(g.shape[4:]) for g in grads),
        ],
        out_shape=[
            jax.ShapeDtypeStruct((tokens, width), wide),
            jax.ShapeDtypeStruct((tokens, LANES), low),
            jax.ShapeDtypeStruct(rate2.shape, wide),
            jax.ShapeDtypeStruct(dtproj.shape, wide),
            jax.ShapeDtypeStruct((1, width), wide),
            *(jax.ShapeDtypeStruct(g.shape[4:], g.dtype) for g in grads),
        ],
        scratch_shapes=[
            pltpu.VMEM((states, width), wide),
            pltpu.VMEM((blocks, QLEN, width), wide),
            pltpu.VMEM((blocks, QLEN, width), wide),
            pltpu.VMEM((rows * states, LANES), wide),
            pltpu.VMEM((rows, QLEN * states), low),
            pltpu.VMEM((QLEN * states, width), low),
            pltpu.VMEM((QLEN * states, width), low),
            pltpu.VMEM((QLEN * states, LANES), wide),
            pltpu.VMEM((QLEN * states, LANES), wide),
            pltpu.VMEM((states, width), low),
            pltpu.VMEM((rows, width), wide),
            pltpu.VMEM((rows, width), wide),
            pltpu.VMEM((rows, LANES), wide),
            *(
                shape
                for g, orders in zip(grads, EARLY_ORDERS)
                for shape in (pltpu.VMEM((2, 2, 2, 2) + g.shape[4:], low), *Halving.scratch(g.shape[4:], len(orders)))
            ),
        ],
        compiler_params=pltpu.CompilerParams(
            collective_id=collective_id, has_side_effects=True, vmem_limit_bytes=60 << 20
        ),
        name="scan_backward",
    )(u, in_blocks(dt), in_blocks(d_y), dbc, masks, h, h, by_channel, dtproj, rate2, rate, *grads)
    return du, ddbc, ldt, dtproj_grad, bias_grad, sums


def tail_kernel(
    steps, rank, count, du_ref, ddbc_ref, xproj_ref, u_ref, inner_ref, pre_ref, rows_ref, mask_ref, xnt_ref, w_ref, dgate_ref, tokens_ref, cot_ref, gain_ref,
    dtproj_ref, alog_ref, bias_ref, skip_ref, *refs
):
    wide, low = jnp.float32, jnp.bfloat16
    pieces, tokengrad_ref, outs = refs[:count], refs[count], refs[count + 1 : 2 * count + 4]
    refs = refs[2 * count + 4 :]
    w_s, x_s, cot_s, dxn, dinner_s, xproj_s, row_s, inner_s, small_s, gain_s, load_sem, out_sem = refs[:12]
    link = Link(own_bits())
    halving_refs, spreading_refs = refs[12 : 12 + 24], refs[12 + 24 :]
    spreadings = [Spreading(link, orders, *spreading_refs[2 * a : 2 * a + 2]) for a, orders in enumerate(TAIL_SPREADS)]
    inner_sum = Halving(link, TAIL_ORDERS[2], inner_s, halving_refs[:8])
    small_sum = Halving(link, TAIL_ORDERS[3], small_s, halving_refs[8:16])
    gain_sum = Halving(link, TAIL_ORDERS[4], gain_s, halving_refs[16:])
    block = du_ref.shape[1]
    here = pl.program_id(0)
    columns = pl.ds(pl.multiple_of(here * block, block), block)
    final = steps - 1

    loads = [(w_ref, w_s), (tokens_ref, x_s), (cot_ref, cot_s), (dgate_ref, dxn)]
    loads = [functools.partial(pltpu.make_async_copy, src, dst, load_sem.at[i]) for i, (src, dst) in enumerate(loads)]

    def start():
        for load in loads:
            load().start()
        greet(link.own, ("core", "pair", "bit", "low", "high"))
        for piece, spreading in zip(pieces, spreadings):
            for k in range(spreading.parts):
                spreading.put(k, piece[:, spreading.columns(k)])

    def add_up(events, halving, spreading, part_times):
        for k, times in enumerate(part_times):
            give, join, *halves = times[:6]
            events += [(give, functools.partial(halving.give, k)), (join, functools.partial(halving.join, k))]
            events += [
                (time, functools.partial(halving.halved, k, step, spreading.put)) for step, time in enumerate(halves)
            ]
            events += [(time, functools.partial(spreading.take, k, step)) for step, time in enumerate(times[6:])]

    events = []
    for spreading, times in zip(spreadings, SPREAD_TIMES):
        events += [(time, functools.partial(spreading.take, 0, step)) for step, time in enumerate(times)]
    add_up(events, inner_sum, spreadings[count], INNER_TIMES)
    add_up(events, small_sum, spreadings[count + 1], SMALL_TIMES)
    add_up(events, gain_sum, spreadings[count + 2], GAIN_TIMES)

    def through_inner(chunk):
        if chunk == 0:
            for load in loads:
                load().wait()
        size = dinner_s.shape[1] // len(DXN_TIMES)
        own = slice(chunk * size, (chunk + 1) * size)
        dxn[...] += transposed_product(dinner_s[:, own], w_s[:, own])

    def through_norm():
        x = x_s[...].astype(wide)
        inv = lax.rsqrt(jnp.mean(x * x, axis=1, keepdims=True) + EPSILON)
        x_hat = x * inv
        gain_grad = jnp.sum(dxn[...] * x_hat, axis=0, keepdims=True)
        d_hat = dxn[...] * gain_ref[...]
        level = jnp.mean(d_hat * x_hat, axis=1, keepdims=True)
        tokengrad_ref[...] = cot_s[...].astype(wide) + inv * (d_hat - x_hat * level)
        size = gain_grad.shape[1] // 4
        rows, lanes = gain_s.shape[5:]
        gain_s[...] = jnp.zeros_like(gain_s)
        for shard in range(4):
            parts = [gain_grad[:, c : c + lanes] for c in range(shard * size, (shard + 1) * size, lanes)]
            block = jnp.concatenate(parts + [jnp.zeros((rows - len(parts), lanes), wide)], axis=0)
            gain_s[shard % 2, shard // 2, 0, 0, 0] = block.astype(low)

    events += [(time, functools.partial(through_inner, chunk)) for chunk, time in enumerate(DXN_TIMES)]
    events.append((NORM_TIME, through_norm))
    run_events([(0, start)], final)

    rows = rows_ref[...]
    pre = pre_ref[...]
    share = jax.nn.sigmoid(pre)
    d_u = du_ref[...] + dot(ddbc_ref[...], xproj_ref[...])
    d_pre = d_u * share * (1.0 + pre * (1.0 - share))
    inner = inner_ref[...].astype(wide)
    d_inner = block_rows(rows, TAPS - 1, 1) * d_pre
    sums = [None] * 8
    sums[TAPS - 1] = jnp.sum(d_pre * inner, axis=0, keepdims=True)
    sums[BIAS_ROW] = jnp.sum(d_pre, axis=0, keepdims=True)
    for offset in range(1, TAPS):
        same = d_pre * mask_ref[:, offset : offset + 1]
        back = pltpu.roll(same, same.shape[0] - offset, 0)
        sums[TAPS - 1 - offset] = jnp.sum(back * inner, axis=0, keepdims=True)
        d_inner = d_inner + block_rows(rows, TAPS - 1 - offset, 1) * back
    nothing = jnp.zeros_like(sums[0])
    row_s[:, columns] = jnp.concatenate([nothing if v is None else v for v in sums], axis=0)
    xproj_s[:, columns] = rows_product(ddbc_ref[...], u_ref[...])
    d_inner = d_inner.astype(low)
    inner_grad = dot(xnt_ref[...], d_inner).astype(low)
    size = inner_grad.shape[0] // 4
    for shard in range(4):
        own_rows = inner_grad[shard * size : (shard + 1) * size]
        inner_s[shard % 2, shard // 2, :, :, :, :, columns] = own_rows.reshape(2, 2, 2, size // 8, block)
    dinner_s[:, columns] = d_inner

    @pl.when(here == final)
    def _():
        owned = xproj_s.shape[1] // 4
        states = alog_ref.shape[0]
        row = lax.broadcasted_iota(jnp.int32, (8, owned), 0)
        for shard in range(4):
            own = slice(shard * owned, (shard + 1) * owned)
            rows = row_s[:, own]
            for at, extra in ((STEP_ROW, bias_ref[:, own]), (SKIP_ROW, skip_ref[:, own])):
                rows = jnp.where(row == at, extra, rows)
            stacked = [dtproj_ref[:rank, own], alog_ref[:, own], xproj_s[: rank + 2 * states, own], rows]
            height = 8 * small_s.shape[5]
            stacked.append(jnp.zeros((height - sum(v.shape[0] for v in stacked), owned), wide))
            stacked = jnp.concatenate(stacked, axis=0).astype(low)
            small_s[shard % 2, shard // 2] = stacked.reshape(2, 2, 2, height // 8, owned)

    run_events(events, final)

    @pl.when(here == final)
    def _():
        stores = [pltpu.make_async_copy(s.full, o, out_sem.at[i]) for i, (s, o) in enumerate(zip(spreadings, outs))]
        for copy in stores:
            copy.start()
        for copy in stores:
            copy.wait()
        link.finish()


def tail(
    rank, du, ddbc, xproj_t, u, inner, pre, by_channel, masks, xnt, inner_w, dxn_gate, tokens, cotangent, gain,
    dtproj_grad, alog_grad, bias_grad, skip_grad, pieces, collective_id, block=256,
):
    length, features = tokens.shape
    width = inner_w.shape[1]
    count = len(pieces)
    steps = width // block
    inner_shape = (features // 32, width)
    used = 2 * rank + 3 * alog_grad.shape[0] + 8
    small_shape = ((used + -used % LANES) // 8, width // 4)
    gain_shape = (16, LANES)
    shapes = [*(p.shape for p in pieces), inner_shape, small_shape, gain_shape]
    low, wide = jnp.bfloat16, jnp.float32
    channels = columns_spec(length, block)
    token_grad, *sums = pl.pallas_call(
        functools.partial(tail_kernel, steps, rank, count),
        grid=(steps,),
        in_specs=[
            channels,
            whole_spec(ddbc.shape),
            columns_spec(LANES, block),
            channels,
            channels,
            channels,
            columns_spec(by_channel.shape[0], block),
            whole_spec(masks.shape),
            whole_spec(xnt.shape),
            *[pl.BlockSpec(memory_space=pl.ANY)] * 4,
            whole_spec(gain.shape),
            whole_spec(dtproj_grad.shape),
            whole_spec(alog_grad.shape),
            whole_spec(bias_grad.shape),
            whole_spec(skip_grad.shape),
            *(whole_spec(p.shape) for p in pieces),
        ],
        out_specs=[whole_spec(tokens.shape), *[pl.BlockSpec(memory_space=pl.ANY)] * (count + 3)],
        out_shape=[
            jax.ShapeDtypeStruct(tokens.shape, wide),
            *(jax.ShapeDtypeStruct((2, 2, 2) + shape, low) for shape in shapes),
        ],
        scratch_shapes=[
            pltpu.VMEM(inner_w.shape, low),
            pltpu.VMEM(tokens.shape, low),
            pltpu.VMEM(tokens.shape, low),
            pltpu.VMEM(tokens.shape, wide),
            pltpu.VMEM((length, width), low),
            pltpu.VMEM((LANES, width), wide),
            pltpu.VMEM((8, width), wide),
            pltpu.VMEM((2, 2, 2, 2, 2) + inner_shape, low),
            pltpu.VMEM((2, 2, 2, 2, 2) + small_shape, low),
            pltpu.VMEM((2, 2, 2, 2, 2) + gain_shape, low),
            pltpu.SemaphoreType.DMA((4,)),
            pltpu.SemaphoreType.DMA((count + 3,)),
            *Halving.scratch(inner_shape, len(TAIL_ORDERS[2])),
            *Halving.scratch(small_shape, len(TAIL_ORDERS[3])),
            *Halving.scratch(gain_shape, len(TAIL_ORDERS[4])),
            *(v for shape, orders in zip(shapes, TAIL_SPREADS) for v in Spreading.scratch(shape, len(orders))),
        ],
        compiler_params=pltpu.CompilerParams(
            collective_id=collective_id, has_side_effects=True, vmem_limit_bytes=60 << 20
        ),
        name="tail",
    )(
        du, ddbc, xproj_t, u, inner, pre, by_channel, masks, xnt, inner_w, dxn_gate, tokens, cotangent, gain,
        dtproj_grad, alog_grad, bias_grad, skip_grad, *pieces,
    )
    return token_grad, sums


def finish_kernel(
    rank, states, gate_ref, out_ref, inner_ref, small_ref, gain_ref,
    in_grad, out_grad, dtproj_grad, alog_grad, xproj_grad, conv_grad, convb_grad, dtb_grad, skip_grad, gain_grad
):
    wide = jnp.float32
    width = inner_ref.shape[1]
    in_grad[:, :width] = inner_ref[...].astype(wide)
    in_grad[:, width:] = gate_ref[...].astype(wide)
    out_grad[...] = out_ref[...].astype(wide)

    @pl.when(pl.program_id(0) == 0)
    def _():
        small = small_ref[...].astype(wide)
        used = 2 * rank + 3 * states
        dtproj_grad[...] = small[:rank]
        alog_grad[...] = small[rank : rank + states]
        xproj_grad[...] = small[rank + states : rank + states + LANES].T[:, : rank + 2 * states]
        rows = small[used : used + 8]
        conv_grad[...] = rows[:TAPS]
        for ref, row in ((convb_grad, BIAS_ROW), (dtb_grad, STEP_ROW), (skip_grad, SKIP_ROW)):
            ref[...] = rows[row : row + 1]
        for part in range(gain_grad.shape[1] // LANES):
            gain_grad[:, part * LANES : (part + 1) * LANES] = gain_ref[part : part + 1, :].astype(wide)


def finish(rank, states, gate, out, inner, small, gain, features, steps=4):
    wide = jnp.float32
    owned = small.shape[1]
    width = inner.shape[1]
    small_shapes = [(rank, owned), (states, owned), (owned, rank + 2 * states), (TAPS, owned)]
    small_shapes += [(1, owned)] * 3 + [(1, features)]
    in_shape, out_shape = (inner.shape[0], 2 * width), out.shape
    return pl.pallas_call(
        functools.partial(finish_kernel, rank, states),
        grid=(steps,),
        in_specs=[
            rows_spec(gate.shape[0] // steps, width),
            rows_spec(out.shape[0] // steps, out.shape[1]),
            rows_spec(inner.shape[0] // steps, width),
            whole_spec(small.shape),
            whole_spec(gain.shape),
        ],
        out_specs=[
            rows_spec(in_shape[0] // steps, in_shape[1]),
            rows_spec(out_shape[0] // steps, out_shape[1]),
            *(whole_spec(shape) for shape in small_shapes),
        ],
        out_shape=[jax.ShapeDtypeStruct(shape, wide) for shape in (in_shape, out_shape, *small_shapes)],
        compiler_params=pltpu.CompilerParams(vmem_limit_bytes=60 << 20),
        name="finish",
    )(gate, out, inner, small, gain)


def add_groups(sums):
    groups = lax.axis_size("dp") // GROUP
    if groups == 1:
        return sums
    alike = [[g * GROUP + i for g in range(groups)] for i in range(GROUP)]
    return lax.psum(sums, "dp", axis_index_groups=alike)


def body(
    tokens,
    cotangent,
    prot_lens,
    clus_start,
    norm_gain,
    in_w,
    conv_w,
    conv_b,
    xproj_w,
    dtproj_w,
    dt_bias,
    a_log,
    d_skip,
    out_w,
):
    features = norm_gain.shape[0]
    width = in_w.shape[1] // 2
    rank, owned = dtproj_w.shape
    states = a_log.shape[0]
    used = 2 * rank + 3 * states + 8
    inner_w, packed = gather_weights(in_w, dtproj_w, a_log, xproj_w, conv_w, (conv_b, dt_bias, d_skip, norm_gain), 1)
    inner_w = inner_w.reshape(-1, width)
    gain = packed[:, used - 1, :features].reshape(1, -1).astype(jnp.float32)
    packed = jnp.swapaxes(packed, 0, 1).reshape(packed.shape[1], -1)
    dtproj = packed[:LANES]
    decay_rate = -jnp.exp(packed[rank : rank + states].astype(jnp.float32))
    rate2 = decay_rate * LOG2E
    xproj_t = packed[rank + states : rank + states + LANES]
    by_channel = packed[used - 8 : used].astype(jnp.float32)
    inner, pre, u, dbc, xn, xnt, masks = front(prot_lens, clus_start, tokens, gain, inner_w, by_channel, xproj_t)
    y, h, dt, (gate_w, out_full) = scan_forward(
        rank, u, dbc, masks, by_channel, dtproj, rate2, (in_w, out_w), 2
    )
    gate_w = gate_w.reshape(-1, width)
    out_full = out_full.reshape(-1, out_full.shape[2])
    mixed, d_y, _, out_local, gate_local, skip_local, dxn_gate = middle(
        xn, xnt, gate_w, y, u, by_channel, out_full, cotangent, tokens, masks
    )
    in_pieces = lambda v: v.reshape((4, 2, 2, 2, v.shape[0] // 32, v.shape[1]))
    du, ddbc, ldt, dtproj_local, dtb_local, early_pieces = scan_backward(
        rank,
        u,
        dt,
        d_y,
        dbc,
        masks,
        h,
        by_channel,
        dtproj,
        rate2,
        decay_rate.astype(jnp.bfloat16),
        [in_pieces(gate_local), in_pieces(out_local)],
        3,
    )
    token_grad, sums = tail(
        rank,
        du,
        ddbc,
        xproj_t,
        u,
        inner,
        pre,
        by_channel,
        masks,
        xnt,
        inner_w,
        dxn_gate,
        tokens,
        cotangent,
        gain,
        dtproj_local,
        ldt * decay_rate,
        dtb_local,
        skip_local,
        early_pieces,
        4,
    )
    sums = [v.reshape(-1, v.shape[-1]) for v in sums]
    grads = add_groups(finish(rank, states, *sums, features))
    in_grad, out_grad, dtproj_grad, alog_grad, xproj_grad, conv_grad, convb_grad, dtb_grad, skip_grad, gain_grad = grads
    return (
        mixed,
        token_grad,
        gain_grad[0],
        in_grad,
        conv_grad,
        convb_grad[0],
        xproj_grad,
        dtproj_grad,
        dtb_grad[0],
        alog_grad,
        skip_grad[0],
        out_grad,
    )


def solution(mesh):
    in_specs = (
        P(("dp", "fsdp"), None),
        P(("dp", "fsdp"), None),
        P(("dp", "fsdp"), None),
        P(("dp", "fsdp"), None),
        P("fsdp"),
        P("fsdp", None),
        P(None, "fsdp"),
        P("fsdp"),
        P("fsdp", None),
        P(None, "fsdp"),
        P("fsdp"),
        P(None, "fsdp"),
        P("fsdp"),
        P("fsdp", None),
    )
    out_specs = (
        P(("dp", "fsdp"), None),
        P(("dp", "fsdp"), None),
        P("fsdp"),
        P("fsdp", None),
        P(None, "fsdp"),
        P("fsdp"),
        P("fsdp", None),
        P(None, "fsdp"),
        P("fsdp"),
        P(None, "fsdp"),
        P("fsdp"),
        P("fsdp", None),
    )
    return jax.shard_map(body, mesh=mesh, in_specs=in_specs, out_specs=out_specs, check_vma=False)
```

```python
import functools

import jax
import jax.numpy as jnp
from jax import lax
from jax.experimental import pallas as pl
from jax.experimental.pallas import tpu as pltpu
from jax.sharding import PartitionSpec as P

QLEN = 16
LANES = 128
WIDE = 256
SPREAD_TIMES = ((4.02, 7.06, 13.1), (6.02, 12.02, 13.16))
INNER_TIMES = (
    (1, 3.02, 7.04, 12.04, 13.2, 13.32, 13.44, 13.52, 13.62),
    (3, 4.04, 10.04, 13.02, 13.12, 13.28, 13.42, 13.48, 13.6),
    (5, 7.02, 13.06, 13.22, 13.34, 13.46, 13.58, 13.7, 13.78),
    (7, 9.02, 13.08, 13.24, 13.36, 13.5, 13.64, 13.72, 13.8),
)
SMALL_TIMES = ((7, 10.02, 13.14, 13.26, 13.38, 13.54, 13.66, 13.74, 13.82),)
GAIN_TIMES = ((12.01, 13.04, 13.18, 13.3, 13.4, 13.56, 13.68, 13.76, 13.84),)
DXN_TIMES = (8, 9.5, 10.5, 11.5)
NORM_TIME = 12
NEVER = 1e30
LOG2E = 1.4426950408889634
FORWARD_STEPS = (0, 4, 6, 7, 7, 9, 9, 11, 11, 13, 13, 13, 14)
BACKWARD_TIMES = (
    ((0, 2.1, 6.1, 9.1, 11.1, 13.1), (0, 3.1, 7.1, 10.1, 12.1, 14.1)),
    ((0, 4.1, 8.1, 11.2, 13.2, 15.1), (0, 5.1, 9.2, 12.2, 14.2, 16.1)),
)


EPSILON = 1e-05


def rows_product(left, right):
    return lax.dot_general(
        left, right, (((0,), (0,)), ((), ())), preferred_element_type=jnp.float32
    )


def transposed_product(left, weight):
    return lax.dot_general(
        left, weight, (((1,), (1,)), ((), ())), preferred_element_type=jnp.float32
    )


MESH = pl.DeviceIdType.MESH
GROUP = 8


def own_bits():
    d, f = lax.axis_index("dp"), lax.axis_index("fsdp")
    inside = lax.rem(d, GROUP)
    return {
        "pair": f // 2,
        "core": lax.rem(f, 2),
        "high": inside // 4,
        "low": lax.rem(inside // 2, 2),
        "bit": lax.rem(inside, 2),
    }


def across(own, dim):
    d, f = lax.axis_index("dp"), lax.axis_index("fsdp")
    step = {"pair": 2, "core": 1, "high": 4, "low": 2, "bit": 1}[dim]
    flip = step * (1 - 2 * own[dim])
    return (d, f + flip) if dim in ("pair", "core") else (d + flip, f)


def greet(own, dims):
    barrier = pltpu.get_barrier_semaphore()
    for dim in dims:
        pl.semaphore_signal(barrier, inc=1, device_id=across(own, dim), device_id_type=MESH)
    pl.semaphore_wait(barrier, len(dims))


class Link:
    def __init__(self, own):
        self.own = own
        self.sent = []

    def copy(self, src, dst, sems, dim):
        return pltpu.make_async_remote_copy(
            src_ref=src,
            dst_ref=dst,
            send_sem=sems[0],
            recv_sem=sems[1],
            device_id=across(self.own, dim),
            device_id_type=MESH,
        )

    def send(self, described):
        self.copy(*described()).start()
        self.sent.append(described)

    def receive(self, ref, sems, dim):
        self.copy(ref, ref, sems, dim).wait_recv()

    def finish(self):
        for described in self.sent:
            self.copy(*described()).wait_send()


class Gather:
    def __init__(self, shards, outs, scratch, made=None):
        self.shards, self.outs, self.made = shards, outs, made
        self.count = len(shards)
        self.stage = scratch[: self.count]
        self.load_sem, self.core_sem, self.hop_sem, self.whole_sem = scratch[self.count :]
        self.own = own_bits()
        self.link = Link(self.own)
        pair, core = self.own["pair"], self.own["core"]
        self.mine = 2 * pair + core
        self.theirs = 2 * (1 - pair) + core
        self.sibling = 2 * pair + 1 - core
        self.beyond = 2 * (1 - pair) + 1 - core
        bit, low = self.own["bit"], self.own["low"]
        self.kinds = ((bit, low), (1 - bit, low), (bit, 1 - low), (1 - bit, 1 - low))
        pair, near, far = (
            [[functools.partial(stage, a, half) for half in range(2)] for a in range(2)]
            for stage in (self.from_pair, self.from_near, self.from_far)
        )
        self.stages = [self.begin, pair[0][0], pair[0][1], near[0][0], pair[1][0], near[0][1], pair[1][1]]
        self.stages += [far[0][0], far[1][0], near[1][0], far[0][1], far[1][1], near[1][1], self.end]

    def eighth(self, a, kind, half):
        rows = self.shards[a].shape[0] // 8
        bit, low = self.kinds[kind]
        return pl.ds(pl.multiple_of((2 * (bit + 2 * low) + half) * rows, rows), rows)

    def hop(self, a, kind, half):
        return self.hop_sem.at[0, a, kind, half], self.hop_sem.at[1, a, kind, half]

    def to_core(self, a, kind, half):
        return self.core_sem.at[0, a, kind, half], self.core_sem.at[1, a, kind, half]

    def whole(self, a):
        return self.whole_sem.at[0, a], self.whole_sem.at[1, a]

    def load(self, a):
        return pltpu.make_async_copy(self.shards[a], self.stage[a], self.load_sem.at[a])

    def in_place(self, a):
        return self.made is not None and a == self.count - 1

    def store(self, a):
        return pltpu.make_async_copy(self.stage[a], self.outs[a].at[self.mine], self.load_sem.at[a])

    def begin(self):
        greet(self.own, ("core", "pair", "bit", "low"))
        for a in range(self.count):
            if self.in_place(a):
                self.made()
            for kind in (0, 3)[: a + 1]:
                for half in range(2):
                    self.link.send(functools.partial(self.to_pair, a, kind, half))
        for a in range(self.count):
            if not self.in_place(a):
                self.load(a).start()
            self.link.send(functools.partial(self.own_to_core, a))

    def to_pair(self, a, kind, half):
        rows = self.eighth(a, kind, half)
        return self.shards[a].at[rows], self.outs[a].at[self.mine, rows], self.hop(a, kind, half), "pair"

    def own_to_core(self, a):
        return self.shards[a], self.outs[a].at[self.mine], self.whole(a), "core"

    def came(self, a, kind, half):
        return self.outs[a].at[self.theirs, self.eighth(a, kind, half)]

    def onward(self, a, kind, half, new_kind, dim):
        ref = self.came(a, kind, half)
        return ref, ref, self.to_core(a, kind, half) if dim == "core" else self.hop(a, new_kind, half), dim

    def pass_on(self, a, kind, half, new_kind, dim):
        self.link.send(functools.partial(self.onward, a, kind, half, new_kind, dim))

    def arrive(self, a, kind, half, dim):
        self.link.receive(self.came(a, kind, half), self.hop(a, kind, half), dim)
        self.pass_on(a, kind, half, kind, "core")

    def from_pair(self, a, half):
        self.arrive(a, 0, half, "pair")
        self.pass_on(a, 0, half, 1, "bit")
        self.pass_on(a, 0, half, 2, "low")
        if half == 1:
            if not self.in_place(a):
                self.load(a).wait()
            self.store(a).start()

    def from_near(self, a, half):
        self.arrive(a, 1, half, "bit")
        if a == 0 and half == 0:
            self.pass_on(a, 1, 0, 3, "low")
        self.arrive(a, 2, half, "low")
        if a == 0 and half == 1:
            self.pass_on(a, 2, 1, 3, "bit")

    def from_far(self, a, half):
        self.arrive(a, 3, half, "pair" if a == 1 else ("low", "bit")[half])

    def end(self):
        for a in range(self.count):
            self.link.receive(self.outs[a].at[self.sibling], self.whole(a), "core")
            for kind in range(4):
                for half in range(2):
                    ref = self.outs[a].at[self.beyond, self.eighth(a, kind, half)]
                    self.link.receive(ref, self.to_core(a, kind, half), "core")
            self.store(a).wait()
        self.link.finish()

    @staticmethod
    def scratch(shapes):
        count = len(shapes)
        dma = pltpu.SemaphoreType.DMA
        staged = [pltpu.VMEM(shape, jnp.bfloat16) for shape in shapes]
        return staged + [dma((count,)), dma((2, count, 4, 2)), dma((2, count, 4, 2)), dma((2, count))]


def gather_kernel(
    width, in_ref, dtproj_ref, alog_ref, xproj_ref, taps_ref, bias_ref, step_ref, skip_ref, gain_ref, inner_out, packed_out, *scratch
):
    packed = scratch[1]

    def pack():
        low = packed.dtype
        rank, states, columns = dtproj_ref.shape[0], alog_ref.shape[0], xproj_ref.shape[1]
        eye = (
            lax.broadcasted_iota(jnp.int32, (columns, columns), 0) == lane_index((columns, columns))
        ).astype(low)
        at = rank + states + columns
        owned = packed.shape[1]
        wide = jnp.float32
        packed[:rank, :] = dtproj_ref[...]
        packed[rank : rank + states, :] = alog_ref[...]
        packed[rank + states : at, :] = transposed_product(eye, xproj_ref[...]).astype(low)
        row = lax.broadcasted_iota(jnp.int32, (16, owned), 0)
        rows = jnp.concatenate([taps_ref[...].astype(wide), jnp.zeros((16 - TAPS, owned), wide)], axis=0)
        for place, ref in ((BIAS_ROW, bias_ref), (STEP_ROW, step_ref), (SKIP_ROW, skip_ref), (GAIN_ROW, gain_ref)):
            values = ref[...].astype(wide).reshape(1, ref.shape[0])
            if ref.shape[0] < owned:
                values = jnp.concatenate([values, jnp.zeros((1, owned - ref.shape[0]), wide)], axis=1)
            rows = jnp.where(row == place, values, rows)
        packed[at : at + 16, :] = rows.astype(low)
        packed[at + 16 :, :] = jnp.zeros((packed.shape[0] - at - 16, owned), low)

    gather = Gather((in_ref.at[:, pl.ds(0, width)], packed), (inner_out, packed_out), scratch, made=pack)
    for stage in gather.stages:
        stage()


def gathered_shape(shape):
    return jax.ShapeDtypeStruct((4,) + shape, jnp.bfloat16)


def gather_weights(in_w, dtproj_w, a_log, xproj_w, conv_w, vectors, collective_id):
    anywhere, vmem = pl.BlockSpec(memory_space=pl.ANY), pl.BlockSpec(memory_space=pltpu.VMEM)
    used = dtproj_w.shape[0] + a_log.shape[0] + xproj_w.shape[1] + TAPS + len(vectors)
    shapes = [(in_w.shape[0], in_w.shape[1] // 2), (used + -used % LANES, conv_w.shape[1])]
    return pl.pallas_call(
        functools.partial(gather_kernel, shapes[0][1]),
        out_shape=[gathered_shape(shape) for shape in shapes],
        in_specs=[anywhere] + [vmem] * (4 + len(vectors)),
        out_specs=[anywhere, anywhere],
        scratch_shapes=Gather.scratch(shapes),
        compiler_params=pltpu.CompilerParams(
            collective_id=collective_id, has_side_effects=True, vmem_limit_bytes=60 << 20
        ),
        name="gather_weights",
    )(in_w, dtproj_w, a_log, xproj_w, conv_w, *vectors)


def run_stages(stages, at_steps):
    for step in sorted(set(at_steps)):

        @pl.when(pl.program_id(0) == step)
        def _():
            for stage, at in zip(stages, at_steps):
                if at == step:
                    stage()


DIMS = ("pair", "high", "low", "bit")
MIXED = (
    ("pair", "bit", "low", "high"),
    ("bit", "low", "pair", "high"),
    ("low", "pair", "bit", "high"),
    ("pair", "low", "bit", "high"),
)
PAIR_FIRST = (("pair", "bit", "low", "high"), ("pair", "low", "bit", "high"))
LOW_FIRST, BIT_FIRST = ("high", "low", "bit"), ("high", "bit", "low")
EARLY_ORDERS = (MIXED[:2], MIXED[2:])
TAIL_ORDERS = (None, None, PAIR_FIRST * 2, PAIR_FIRST[:1], PAIR_FIRST[:1])
TAIL_SPREADS = ((LOW_FIRST,), (BIT_FIRST,), (LOW_FIRST, BIT_FIRST, LOW_FIRST, BIT_FIRST), (LOW_FIRST,), (LOW_FIRST,))
EVERY = slice(None)


def each_block(free, body):
    if not free:
        body(())
        return

    def step(i, carried):
        body(tuple(lax.rem(i // 2 ** (free - 1 - n), 2) for n in range(free)))
        return carried

    lax.fori_loop(0, 2**free, step, 0)


def part_columns(columns, parts, k):
    return pl.ds(k * (columns // parts), columns // parts)


def region(chosen, dims, columns):
    return tuple(chosen.get(d, EVERY) for d in dims) + (EVERY, columns)


class Halving:
    def __init__(self, link, orders, local, scratch, given=None):
        self.link, self.own, self.orders, self.local, self.given = link, link.own, orders, local, given
        self.cores, *self.arrived, self.load_sem, self.core_sem, self.half_sem = scratch
        self.parts = len(orders)

    def columns(self, k):
        return part_columns(self.local.shape[-1], self.parts, k)

    def lead(self, core):
        return () if self.given is not None else (core,)

    def of_pair(self, y, k):
        return region({"pair": y}, DIMS, self.columns(k))

    def loading(self, k, y):
        at = self.of_pair(y, k)
        kept = (2 * y + self.own["core"],) + at[1:]
        return pltpu.make_async_copy(self.given.at[kept], self.local.at[at], self.load_sem.at[k, y])

    def giving(self, k, y):
        at = self.of_pair(y, k)
        other = 1 - self.own["core"]
        if self.given is not None:
            src = self.given.at[(2 * y + other,) + at[1:]]
        else:
            src = self.local.at[(other,) + at]
        return src, self.cores.at[at], (self.core_sem.at[0, k, y], self.core_sem.at[1, k, y]), "core"

    def give(self, k):
        for y in range(2):
            self.link.send(functools.partial(self.giving, k, y))
            if self.given is not None:
                self.loading(k, y).start()

    def join(self, k):
        for y in range(2):
            if self.given is not None:
                self.loading(k, y).wait()
            sems = (self.core_sem.at[0, k, y], self.core_sem.at[1, k, y])
            self.link.receive(self.cores.at[self.of_pair(y, k)], sems, "core")

        def add(index):
            at = index + (EVERY, self.columns(k))
            kept = self.lead(self.own["core"]) + at
            self.local[kept] = self.local[kept] + self.cores[at]

        each_block(4, add)
        self.halve(k, 0)

    def half(self, k, step):
        dim = self.orders[k][step]
        chosen = {d: self.own[d] for d in self.orders[k][:step]}
        chosen[dim] = 1 - self.own[dim]
        at = self.lead(self.own["core"]) + region(chosen, DIMS, self.columns(k))
        sems = (self.half_sem.at[0, k, step], self.half_sem.at[1, k, step])
        return self.local.at[at], self.arrived[step].at[k], sems, dim

    def halve(self, k, step):
        self.link.send(functools.partial(self.half, k, step))

    def halved(self, k, step, done=None):
        sems = (self.half_sem.at[0, k, step], self.half_sem.at[1, k, step])
        self.link.receive(self.arrived[step].at[k], sems, self.orders[k][step])
        chosen = {d: self.own[d] for d in self.orders[k][: step + 1]}
        free = [d for d in DIMS if d not in chosen]

        def add(index):
            at = tuple(chosen[d] if d in chosen else index[free.index(d)] for d in DIMS)
            kept = self.lead(self.own["core"]) + at + (EVERY, self.columns(k))
            total = self.local[kept] + self.arrived[step][(k,) + index + (EVERY, EVERY)]
            if step < 3:
                self.local[kept] = total
            else:
                done(k, total)

        each_block(len(free), add)
        if step < 3:
            self.halve(k, step + 1)

    @staticmethod
    def scratch(shape, parts):
        rows, columns = shape
        dma = pltpu.SemaphoreType.DMA
        low = jnp.bfloat16
        shapes = [pltpu.VMEM((2, 2, 2, 2, rows, columns), low)]
        shapes += [pltpu.VMEM((parts,) + (2,) * (3 - step) + (rows, columns // parts), low) for step in range(4)]
        return shapes + [dma((parts, 2)), dma((2, parts, 2)), dma((2, parts, 4))]


class Spreading:
    def __init__(self, link, orders, full, sems):
        self.link, self.own, self.orders, self.full, self.sems = link, link.own, orders, full, sems
        self.parts = len(orders)

    def columns(self, k):
        return part_columns(self.full.shape[-1], self.parts, k)

    def put(self, k, value):
        at = tuple(self.own[d] for d in DIMS[1:]) + (EVERY, self.columns(k))
        self.full[at] = value
        self.pass_on(k, 0)

    def held(self, k, step):
        chosen = {d: self.own[d] for d in self.orders[k][step:]}
        here = self.full.at[region(chosen, DIMS[1:], self.columns(k))]
        return here, here, (self.sems.at[0, k, step], self.sems.at[1, k, step]), self.orders[k][step]

    def pass_on(self, k, step):
        self.link.send(functools.partial(self.held, k, step))

    def take(self, k, step):
        dim = self.orders[k][step]
        chosen = {d: self.own[d] for d in self.orders[k][step:]}
        chosen[dim] = 1 - self.own[dim]
        there = self.full.at[region(chosen, DIMS[1:], self.columns(k))]
        self.link.receive(there, (self.sems.at[0, k, step], self.sems.at[1, k, step]), dim)
        if step < 2:
            self.pass_on(k, step + 1)

    @staticmethod
    def scratch(shape, parts):
        return [pltpu.VMEM((2, 2, 2) + shape, jnp.bfloat16), pltpu.SemaphoreType.DMA((2, parts, 3))]


def run_events(events, last):
    events = sorted(events, key=lambda event: event[0])
    for step in range(last + 1):
        actions = [action for time, action in events if min(int(time), last) == step]
        if actions:

            @pl.when(pl.program_id(0) == step)
            def _():
                for action in actions:
                    action()


def block_rows(values, row, rows):
    return values[row : row + 1, :]


def lane_index(shape):
    return lax.broadcasted_iota(jnp.int32, shape, 1)


def dot(left, right):
    return jnp.dot(left, right, preferred_element_type=jnp.float32)


def smooth(values):
    share = jax.nn.sigmoid(values)
    return values * share, share


TAPS = 4
BIAS_ROW, STEP_ROW, SKIP_ROW, GAIN_ROW = 4, 5, 6, 7


def row_masks(lens_ref, start_ref, length):
    shape = (length, LANES)
    position = lax.broadcasted_iota(jnp.int32, shape, 0)
    cluster = jnp.zeros(shape, jnp.int32)
    begin = 0
    for slot in range(lens_ref.shape[1]):
        size = lens_ref[0, slot]
        flag = jnp.where((start_ref[0, slot] > 0) & (size > 0), 1, 0)
        cluster = cluster + jnp.where(position >= begin, flag, 0)
        begin = begin + size
    lane = lane_index(shape)
    masks = jnp.where((lane == 0) & (position < begin), 1.0, 0.0)
    for offset in range(1, TAPS):
        same = (lane == offset) & (position >= offset) & (cluster == pltpu.roll(cluster, offset, 0))
        masks = jnp.where(same, 1.0, masks)
    return masks


def front_kernel(
    lens_ref, start_ref, tokens_ref, gain_ref, w_ref, rows_ref, xproj_ref, inner_ref, pre_ref, u_ref, dbc_ref, xn_ref, xnt_ref, mask_ref
):
    @pl.when(pl.program_id(0) == 0)
    def _():
        mask_ref[...] = row_masks(lens_ref, start_ref, mask_ref.shape[0])
        x = tokens_ref[...].astype(jnp.float32)
        inv = lax.rsqrt(jnp.mean(x * x, axis=1, keepdims=True) + EPSILON)
        xn = (x * inv * gain_ref[...]).astype(jnp.bfloat16)
        xn_ref[...] = xn
        xnt_ref[...] = xn.T
        dbc_ref[...] = jnp.zeros_like(dbc_ref)

    inner = dot(xn_ref[...], w_ref[...])
    rows = rows_ref[...]
    pre = block_rows(rows, BIAS_ROW, 1) + block_rows(rows, TAPS - 1, 1) * inner
    for offset in range(1, TAPS):
        shifted = pltpu.roll(inner, offset, 0) * mask_ref[:, offset : offset + 1]
        pre = pre + block_rows(rows, TAPS - 1 - offset, 1) * shifted
    u = smooth(pre)[0].astype(jnp.bfloat16)
    inner_ref[...] = inner.astype(inner_ref.dtype)
    pre_ref[...] = pre
    u_ref[...] = u
    dbc_ref[...] += transposed_product(u, xproj_ref[...])


def whole_spec(shape):
    return pl.BlockSpec(shape, lambda i: (0,) * len(shape))


def columns_spec(rows, block):
    return pl.BlockSpec((rows, block), lambda i: (0, i))


def rows_spec(block, columns):
    return pl.BlockSpec((block, columns), lambda i: (i, 0))


def front(lens, starts, tokens, gain, inner_w, by_channel, xproj_t, block=512):
    length, features = tokens.shape
    width = inner_w.shape[1]
    low, wide = jnp.bfloat16, jnp.float32
    return pl.pallas_call(
        front_kernel,
        grid=(width // block,),
        in_specs=[
            pl.BlockSpec(memory_space=pltpu.SMEM),
            pl.BlockSpec(memory_space=pltpu.SMEM),
            whole_spec(tokens.shape),
            whole_spec(gain.shape),
            columns_spec(features, block),
            columns_spec(by_channel.shape[0], block),
            columns_spec(LANES, block),
        ],
        out_specs=[
            columns_spec(length, block),
            columns_spec(length, block),
            columns_spec(length, block),
            whole_spec((length, LANES)),
            whole_spec((length, features)),
            whole_spec((features, length)),
            whole_spec((length, LANES)),
        ],
        out_shape=[
            jax.ShapeDtypeStruct((length, width), low),
            jax.ShapeDtypeStruct((length, width), wide),
            jax.ShapeDtypeStruct((length, width), low),
            jax.ShapeDtypeStruct((length, LANES), wide),
            jax.ShapeDtypeStruct((length, features), low),
            jax.ShapeDtypeStruct((features, length), low),
            jax.ShapeDtypeStruct((length, LANES), wide),
        ],
        compiler_params=pltpu.CompilerParams(vmem_limit_bytes=60 << 20),
        name="front",
    )(lens, starts, tokens, gain, inner_w, by_channel, xproj_t)


def spread_states(dbc, first, states):
    rows = QLEN * states
    repeated = jnp.broadcast_to(dbc[:, None, :], (QLEN, states, LANES)).reshape(rows, LANES)
    state = lax.broadcasted_iota(jnp.int32, (rows, LANES), 0) % states
    own = jnp.where(lane_index((rows, LANES)) == first + state, repeated, 0.0)
    return jnp.broadcast_to(jnp.sum(own, axis=1, keepdims=True), (rows, LANES))


def diagonal_states(dbc, first, states):
    rows = QLEN * states
    pick = (
        lax.broadcasted_iota(jnp.int32, (LANES, rows), 0) == first + lane_index((LANES, rows)) % states
    ).astype(jnp.bfloat16)
    tiled = dot(dbc.astype(jnp.bfloat16), pick)
    own = lane_index((QLEN, rows)) // states == lax.broadcasted_iota(jnp.int32, (QLEN, rows), 0)
    return jnp.where(own, tiled, 0.0).astype(jnp.bfloat16)


def step_rank(dbc, rank):
    return jnp.where(lane_index(dbc.shape) < rank, dbc, 0.0).astype(jnp.bfloat16)


def twice(values):
    return jnp.concatenate([values] * (WIDE // LANES), axis=1)


def forward_kernel(rank, group, count, u_ref, dbc_ref, mask_ref, rows_ref, dtproj_ref, rate_ref, *refs):
    shards, (y_ref, h_ref, dt_ref), outs = refs[:count], refs[count : count + 3], refs[count + 3 : 2 * count + 3]
    (state, long_s, feed_s, b_s, cblk_s), scratch = refs[2 * count + 3 : 2 * count + 8], refs[2 * count + 8 :]
    blocks, _, width = long_s.shape
    states = rate_ref.shape[0]
    span = QLEN * states
    in_ref, out_ref = shards
    gather = Gather((in_ref.at[:, pl.ds(width, width)], out_ref), outs, scratch)
    run_stages(gather.stages[:-1], FORWARD_STEPS)

    @pl.when(pl.program_id(0) == 0)
    def _():
        state[...] = jnp.zeros_like(state)

    rank_rows = step_rank(dbc_ref[...], rank)
    keep = mask_ref[:, 1:2] > 0
    for c in range(0, width, WIDE):
        s = slice(c, c + WIDE)
        dt = jax.nn.softplus(dot(rank_rows, dtproj_ref[:, s]) + rows_ref[STEP_ROW : STEP_ROW + 1, s])
        dt_ref[:, s] = dt
        long = jnp.where(keep, dt, NEVER)
        feed = dt * u_ref[:, s].astype(jnp.float32)
        for j in range(blocks):
            long_s[j, :, s] = long[j * QLEN : (j + 1) * QLEN]
            feed_s[j, :, s] = feed[j * QLEN : (j + 1) * QLEN]
    for j in range(blocks):
        dbc = dbc_ref[j * QLEN : (j + 1) * QLEN, :]
        b_s[j * span : (j + 1) * span, :] = spread_states(dbc, rank, states)
        cblk_s[j * QLEN : (j + 1) * QLEN, :] = diagonal_states(dbc, rank + states, states)

    def block(j, carried):
        r0 = pl.multiple_of(j * QLEN, QLEN)
        h0 = pl.multiple_of(j * span, span)
        for c0 in range(0, width, group * WIDE):
            columns = [slice(c, c + WIDE) for c in range(c0, c0 + group * WIDE, WIDE)]
            held = [state[:, s] for s in columns]
            rates = [rate_ref[:, s] for s in columns]
            for t in range(QLEN):
                b_t = twice(b_s[pl.ds(h0 + t * states, states), :])
                for k, s in enumerate(columns):
                    decay = jnp.exp2(long_s[j, t : t + 1, s] * rates[k])
                    held[k] = decay * held[k] + b_t * feed_s[j, t : t + 1, s]
                    h_ref[pl.ds(h0 + t * states, states), s] = held[k].astype(h_ref.dtype)
            for k, s in enumerate(columns):
                state[:, s] = held[k]
            s = slice(c0, c0 + group * WIDE)
            y_ref[pl.ds(r0, QLEN), s] = dot(cblk_s[pl.ds(r0, QLEN), :], h_ref[pl.ds(h0, span), s])
        return carried

    lax.fori_loop(0, blocks, block, 0)
    run_stages(gather.stages[-1:], (pl.num_programs(0) - 1,))


def scan_forward(rank, u, dbc, masks, by_channel, dtproj, rate2, shards, collective_id, blocks=2, group=2):
    count = len(shards)
    shapes = [(shards[0].shape[0], shards[0].shape[1] // 2), shards[1].shape]
    anywhere = [pl.BlockSpec(memory_space=pl.ANY)] * count
    tokens, width = u.shape
    states = rate2.shape[0]
    rows = blocks * QLEN
    y, h, dt, *gathered = pl.pallas_call(
        functools.partial(forward_kernel, rank, group, count),
        grid=(tokens // rows,),
        in_specs=[
            rows_spec(rows, width),
            rows_spec(rows, LANES),
            rows_spec(rows, masks.shape[1]),
            whole_spec(by_channel.shape),
            whole_spec(dtproj.shape),
            whole_spec(rate2.shape),
            *anywhere,
        ],
        out_specs=[rows_spec(rows, width), rows_spec(rows * states, width), rows_spec(rows, width), *anywhere],
        out_shape=[
            jax.ShapeDtypeStruct((tokens, width), jnp.float32),
            jax.ShapeDtypeStruct((tokens * states, width), jnp.bfloat16),
            jax.ShapeDtypeStruct((tokens, width), jnp.float32),
            *(gathered_shape(shape) for shape in shapes),
        ],
        scratch_shapes=[
            pltpu.VMEM((states, width), jnp.float32),
            pltpu.VMEM((blocks, QLEN, width), jnp.float32),
            pltpu.VMEM((blocks, QLEN, width), jnp.float32),
            pltpu.VMEM((rows * states, LANES), jnp.float32),
            pltpu.VMEM((rows, QLEN * states), jnp.bfloat16),
            *Gather.scratch(shapes),
        ],
        compiler_params=pltpu.CompilerParams(
            collective_id=collective_id, has_side_effects=True, vmem_limit_bytes=60 << 20
        ),
        name="scan_forward",
    )(u, dbc, masks, by_channel, dtproj, rate2, *shards)
    return y, h, dt, gathered


def middle_kernel(
    xn_ref, xnt_ref, gate_ref, y_ref, u_ref, rows_ref, out_ref, cot_ref, tokens_ref, mask_ref,
    mixed_ref, dy_ref, dgate_ref, outgrad_ref, gategrad_ref, skip_ref, dxn_ref, branch, dbranch
):
    live = mask_ref[:, 0:1]

    @pl.when(pl.program_id(0) == 0)
    def _():
        branch[...] = jnp.zeros_like(branch)
        dxn_ref[...] = jnp.zeros_like(dxn_ref)
        dbranch[...] = (live * cot_ref[...].astype(jnp.float32)).astype(jnp.bfloat16)

    gate = dot(xn_ref[...], gate_ref[...])
    opened, share = smooth(gate)
    u = u_ref[...].astype(jnp.float32)
    y = y_ref[...] + rows_ref[SKIP_ROW : SKIP_ROW + 1, :] * u
    gated = (y * opened).astype(jnp.bfloat16)
    d_branch = dbranch[...]
    branch[...] += dot(gated, out_ref[...])
    outgrad_ref[...] = rows_product(gated, d_branch).astype(outgrad_ref.dtype)
    d_gated = transposed_product(d_branch, out_ref[...])
    d_y = d_gated * opened
    dy_ref[...] = d_y
    skip_ref[...] = jnp.sum(d_y * u, axis=0, keepdims=True)
    d_gate = (d_gated * y * share * (1.0 + gate * (1.0 - share))).astype(jnp.bfloat16)
    dgate_ref[...] = d_gate
    gategrad_ref[...] = dot(xnt_ref[...], d_gate).astype(gategrad_ref.dtype)
    dxn_ref[...] += transposed_product(d_gate, gate_ref[...])

    @pl.when(pl.program_id(0) == pl.num_programs(0) - 1)
    def _():
        mixed_ref[...] = (tokens_ref[...].astype(jnp.float32) + live * branch[...]).astype(mixed_ref.dtype)


def middle(xn, xnt, gate_w, y, u, by_channel, out_w, cotangent, tokens, masks, block=512):
    length, features = tokens.shape
    width = gate_w.shape[1]
    low, wide = jnp.bfloat16, jnp.float32
    channels = columns_spec(length, block)
    return pl.pallas_call(
        middle_kernel,
        grid=(width // block,),
        in_specs=[
            whole_spec(xn.shape),
            whole_spec(xnt.shape),
            columns_spec(features, block),
            channels,
            channels,
            columns_spec(by_channel.shape[0], block),
            rows_spec(block, features),
            whole_spec(tokens.shape),
            whole_spec(tokens.shape),
            whole_spec(masks.shape),
        ],
        out_specs=[
            whole_spec(tokens.shape),
            channels,
            channels,
            rows_spec(block, features),
            columns_spec(features, block),
            columns_spec(1, block),
            whole_spec(tokens.shape),
        ],
        out_shape=[
            jax.ShapeDtypeStruct(tokens.shape, low),
            jax.ShapeDtypeStruct((length, width), wide),
            jax.ShapeDtypeStruct((length, width), low),
            jax.ShapeDtypeStruct((width, features), low),
            jax.ShapeDtypeStruct((features, width), low),
            jax.ShapeDtypeStruct((1, width), wide),
            jax.ShapeDtypeStruct(tokens.shape, wide),
        ],
        scratch_shapes=[pltpu.VMEM(tokens.shape, wide), pltpu.VMEM(tokens.shape, low)],
        compiler_params=pltpu.CompilerParams(vmem_limit_bytes=60 << 20),
        name="middle",
    )(xn, xnt, gate_w, y, u, by_channel, out_w, cotangent, tokens, masks)


def backward_kernel(rank, count, steps, u_ref, dt_ref, dy_ref, dbc_ref, mask_ref, h_ref, before_ref, rows_ref, dtproj_ref, rate2_ref, rate_ref, *refs):
    grads, (du_ref, ddbc_ref, ldt_ref, dtproj_grad, bias_grad) = refs[:count], refs[count : count + 5]
    sums, refs = refs[count + 5 : 2 * count + 5], refs[2 * count + 5 :]
    message, long_s, feed_s, c_s, bblk_s, g_s, lrate_s, db_s, dc_s, before_s, e_s, lsum_s, small_s = refs[:13]
    blocks, _, width = dt_ref.shape
    states = rate_ref.shape[0]
    span = QLEN * states
    low, wide = jnp.bfloat16, jnp.float32
    link = Link(own_bits())
    per = (len(refs) - 13) // count
    halvings = []
    for a in range(count):
        local, *scratch = refs[13 + a * per : 13 + (a + 1) * per]
        halvings.append(Halving(link, EARLY_ORDERS[a], local, scratch, given=grads[a]))

    def keep_sum(out, parts, k, total):
        out[:, part_columns(out.shape[1], parts, k)] = total

    events = [(0, lambda: greet(link.own, ("core", "pair", "bit", "low", "high")))]
    for halving, out, part_times in zip(halvings, sums, BACKWARD_TIMES):
        done = functools.partial(keep_sum, out, halving.parts)
        for k, (give, join, *times) in enumerate(part_times):
            events += [(give, functools.partial(halving.give, k)), (join, functools.partial(halving.join, k))]
            events += [(time, functools.partial(halving.halved, k, step, done)) for step, time in enumerate(times)]
    final = steps - 1
    run_events([event for event in events if event[0] <= final], final)

    @pl.when(pl.program_id(0) == 0)
    def _():
        message[...] = jnp.zeros_like(message)
        ldt_ref[...] = jnp.zeros_like(ldt_ref)
        dtproj_grad[...] = jnp.zeros_like(dtproj_grad)
        bias_grad[...] = jnp.zeros_like(bias_grad)

    for j in range(blocks):
        own = slice(j * QLEN, (j + 1) * QLEN)
        keep = mask_ref[own, 1:2] > 0
        for c in range(0, width, WIDE):
            s = slice(c, c + WIDE)
            dt = dt_ref[j, :, s]
            long_s[j, :, s] = jnp.where(keep, dt, NEVER)
            feed_s[j, :, s] = dt * u_ref[own, s].astype(wide)
        dbc = dbc_ref[own, :]
        c_s[j * span : (j + 1) * span, :] = spread_states(dbc, rank + states, states)
        bblk_s[own, :] = diagonal_states(dbc, rank, states)
    by_token = (
        lane_index((QLEN, span)) // states == lax.broadcasted_iota(jnp.int32, (QLEN, span), 0)
    ).astype(low)
    state_of = lax.broadcasted_iota(jnp.int32, (span, LANES), 0) % states
    at_b = lane_index((span, LANES)) == rank + state_of
    at_c = lane_index((span, LANES)) == rank + states + state_of

    def block(step, carried):
        j = blocks - 1 - step
        r0 = pl.multiple_of(j * QLEN, QLEN)
        h0 = pl.multiple_of(j * span, span)

        @pl.when(j == 0)
        def _():
            before_s[...] = before_ref[...]

        @pl.when(j > 0)
        def _():
            before_s[...] = h_ref[pl.ds(pl.multiple_of(jnp.maximum(h0 - states, 0), states), states), :]

        db_s[...] = jnp.zeros_like(db_s)
        dc_s[...] = jnp.zeros_like(dc_s)
        for c in range(0, width, WIDE):
            s = slice(c, c + WIDE)
            held, rate2, rate, total = message[:, s], rate2_ref[:, s], rate_ref[:, s], ldt_ref[:, s]
            pending = None
            now = h_ref[pl.ds(h0 + (QLEN - 1) * states, states), s]
            for t in reversed(range(QLEN)):
                at = slice(t * states, (t + 1) * states)
                d_y = jnp.broadcast_to(dy_ref[j, t : t + 1, s], (states, WIDE))
                g = twice(c_s[pl.ds(h0 + t * states, states), :]) * d_y + held
                g_low = g.astype(low)
                g_s[at, s] = g_low
                dt = jnp.broadcast_to(long_s[j, t : t + 1, s], (states, WIDE))
                held = jnp.exp2(dt * rate2) * g
                before = before_s[:, s] if t == 0 else h_ref[pl.ds(h0 + (t - 1) * states, states), s]
                l = held.astype(low) * before
                lrate_s[at, s] = l * rate
                ldt = l * dt.astype(low)
                if pending is None:
                    pending = ldt
                else:
                    total = total + (pending + ldt).astype(wide)
                    pending = None
                feed = jnp.broadcast_to(feed_s[j, t : t + 1, s], (states, WIDE))
                for sums, product in ((db_s, g_low * feed.astype(low)), (dc_s, now * d_y.astype(low))):
                    sums[at, :] += (product[:, :LANES] + product[:, LANES:]).astype(wide)
                now = before
            message[:, s] = held
            ldt_ref[:, s] = total
            e_s[pl.ds(r0, QLEN), s] = dot(bblk_s[pl.ds(r0, QLEN), :], g_s[:, s])
            lsum_s[pl.ds(r0, QLEN), s] = dot(by_token, lrate_s[:, s])
        d_b = jnp.sum(db_s[...], axis=1, keepdims=True)
        d_c = jnp.sum(dc_s[...], axis=1, keepdims=True)
        placed = jnp.where(at_b, d_b, jnp.where(at_c, d_c, 0.0)).astype(low)
        small_s[pl.ds(r0, QLEN), :] = dot(by_token, placed)
        return carried

    lax.fori_loop(0, blocks, block, 0)
    rank_rows = step_rank(dbc_ref[...], rank)
    d_rank = jnp.zeros(rank_rows.shape, wide)
    tokens = blocks * QLEN
    for c in range(0, width, WIDE):
        s = slice(c, c + WIDE)
        dt = dt_ref[:, :, s].reshape(tokens, WIDE)
        d_y = dy_ref[:, :, s].reshape(tokens, WIDE)
        e = e_s[:, s]
        share = jnp.where(dt < 0.01, dt * (1.0 - dt * (0.5 - dt * (1.0 / 6.0))), 1.0 - jnp.exp(-dt))
        d_dt = e * u_ref[:, s].astype(wide) + lsum_s[:, s]
        d_step = (d_dt * share).astype(low)
        bias_grad[:, s] += jnp.sum(d_step.astype(wide), axis=0, keepdims=True)
        dtproj_grad[:, s] += rows_product(rank_rows, d_step)
        d_rank += transposed_product(d_step, dtproj_ref[:, s])
        du_ref[:, s] = d_y * rows_ref[SKIP_ROW : SKIP_ROW + 1, s] + e * dt
    ddbc_ref[...] = (jnp.where(lane_index(d_rank.shape) < rank, d_rank, 0.0) + small_s[...]).astype(low)
    run_events([event for event in events if event[0] > final] + [(steps, link.finish)], final)


def scan_backward(rank, u, dt, d_y, dbc, masks, h, by_channel, dtproj, rate2, rate, grads, collective_id, blocks=2):
    count = len(grads)
    anywhere = [pl.BlockSpec(memory_space=pl.ANY)] * count
    tokens, width = u.shape
    states = rate2.shape[0]
    rows = blocks * QLEN
    steps = tokens // rows
    low, wide = jnp.bfloat16, jnp.float32
    back = lambda i: (steps - 1 - i, 0)
    flat = lambda columns: pl.BlockSpec((rows, columns), back)
    cubes = pl.BlockSpec((blocks, QLEN, width), lambda i: (steps - 1 - i, 0, 0))
    in_blocks = lambda v: v.reshape(tokens // QLEN, QLEN, width)
    du, ddbc, ldt, dtproj_grad, bias_grad, *sums = pl.pallas_call(
        functools.partial(backward_kernel, rank, count, steps),
        grid=(steps,),
        in_specs=[
            flat(width),
            cubes,
            cubes,
            flat(LANES),
            flat(masks.shape[1]),
            pl.BlockSpec((rows * states, width), back),
            pl.BlockSpec((states, width), lambda i: (jnp.maximum((steps - 1 - i) * rows - 1, 0), 0)),
            whole_spec(by_channel.shape),
            whole_spec(dtproj.shape),
            whole_spec(rate2.shape),
            whole_spec(rate.shape),
            *anywhere,
        ],
        out_specs=[
            flat(width),
            flat(LANES),
            whole_spec(rate2.shape),
            whole_spec(dtproj.shape),
            whole_spec((1, width)),
            *(whole_spec(g.shape[4:]) for g in grads),
        ],
        out_shape=[
            jax.ShapeDtypeStruct((tokens, width), wide),
            jax.ShapeDtypeStruct((tokens, LANES), low),
            jax.ShapeDtypeStruct(rate2.shape, wide),
            jax.ShapeDtypeStruct(dtproj.shape, wide),
            jax.ShapeDtypeStruct((1, width), wide),
            *(jax.ShapeDtypeStruct(g.shape[4:], g.dtype) for g in grads),
        ],
        scratch_shapes=[
            pltpu.VMEM((states, width), wide),
            pltpu.VMEM((blocks, QLEN, width), wide),
            pltpu.VMEM((blocks, QLEN, width), wide),
            pltpu.VMEM((rows * states, LANES), wide),
            pltpu.VMEM((rows, QLEN * states), low),
            pltpu.VMEM((QLEN * states, width), low),
            pltpu.VMEM((QLEN * states, width), low),
            pltpu.VMEM((QLEN * states, LANES), wide),
            pltpu.VMEM((QLEN * states, LANES), wide),
            pltpu.VMEM((states, width), low),
            pltpu.VMEM((rows, width), wide),
            pltpu.VMEM((rows, width), wide),
            pltpu.VMEM((rows, LANES), wide),
            *(
                shape
                for g, orders in zip(grads, EARLY_ORDERS)
                for shape in (pltpu.VMEM((2, 2, 2, 2) + g.shape[4:], low), *Halving.scratch(g.shape[4:], len(orders)))
            ),
        ],
        compiler_params=pltpu.CompilerParams(
            collective_id=collective_id, has_side_effects=True, vmem_limit_bytes=60 << 20
        ),
        name="scan_backward",
    )(u, in_blocks(dt), in_blocks(d_y), dbc, masks, h, h, by_channel, dtproj, rate2, rate, *grads)
    return du, ddbc, ldt, dtproj_grad, bias_grad, sums


def tail_kernel(
    steps, rank, count, du_ref, ddbc_ref, xproj_ref, u_ref, inner_ref, pre_ref, rows_ref, mask_ref, xnt_ref, w_ref, dgate_ref, tokens_ref, cot_ref, gain_ref,
    dtproj_ref, alog_ref, bias_ref, skip_ref, *refs
):
    wide, low = jnp.float32, jnp.bfloat16
    pieces, tokengrad_ref, outs = refs[:count], refs[count], refs[count + 1 : 2 * count + 4]
    refs = refs[2 * count + 4 :]
    w_s, x_s, cot_s, dxn, dinner_s, xproj_s, row_s, inner_s, small_s, gain_s, load_sem, out_sem = refs[:12]
    link = Link(own_bits())
    halving_refs, spreading_refs = refs[12 : 12 + 24], refs[12 + 24 :]
    spreadings = [Spreading(link, orders, *spreading_refs[2 * a : 2 * a + 2]) for a, orders in enumerate(TAIL_SPREADS)]
    inner_sum = Halving(link, TAIL_ORDERS[2], inner_s, halving_refs[:8])
    small_sum = Halving(link, TAIL_ORDERS[3], small_s, halving_refs[8:16])
    gain_sum = Halving(link, TAIL_ORDERS[4], gain_s, halving_refs[16:])
    block = du_ref.shape[1]
    here = pl.program_id(0)
    columns = pl.ds(pl.multiple_of(here * block, block), block)
    final = steps - 1

    loads = [(w_ref, w_s), (tokens_ref, x_s), (cot_ref, cot_s), (dgate_ref, dxn)]
    loads = [functools.partial(pltpu.make_async_copy, src, dst, load_sem.at[i]) for i, (src, dst) in enumerate(loads)]

    def store(i):
        src, dst = (dxn, tokengrad_ref) if i == len(outs) else (spreadings[i].full, outs[i])
        return pltpu.make_async_copy(src, dst, out_sem.at[i])

    def start():
        for load in loads:
            load().start()
        greet(link.own, ("core", "pair", "bit", "low", "high"))
        for piece, spreading in zip(pieces, spreadings):
            for k in range(spreading.parts):
                spreading.put(k, piece[:, spreading.columns(k)])

    def add_up(events, halving, spreading, part_times):
        for k, times in enumerate(part_times):
            give, join, *halves = times[:6]
            events += [(give, functools.partial(halving.give, k)), (join, functools.partial(halving.join, k))]
            events += [
                (time, functools.partial(halving.halved, k, step, spreading.put)) for step, time in enumerate(halves)
            ]
            events += [(time, functools.partial(spreading.take, k, step)) for step, time in enumerate(times[6:])]

    events = []
    for spreading, times in zip(spreadings, SPREAD_TIMES):
        events += [(time, functools.partial(spreading.take, 0, step)) for step, time in enumerate(times)]
    add_up(events, inner_sum, spreadings[count], INNER_TIMES)
    add_up(events, small_sum, spreadings[count + 1], SMALL_TIMES)
    add_up(events, gain_sum, spreadings[count + 2], GAIN_TIMES)

    def through_inner(chunk):
        if chunk == 0:
            for load in loads:
                load().wait()
        size = dinner_s.shape[1] // len(DXN_TIMES)
        own = slice(chunk * size, (chunk + 1) * size)
        dxn[...] += transposed_product(dinner_s[:, own], w_s[:, own])

    def through_norm():
        x = x_s[...].astype(wide)
        inv = lax.rsqrt(jnp.mean(x * x, axis=1, keepdims=True) + EPSILON)
        x_hat = x * inv
        gain_grad = jnp.sum(dxn[...] * x_hat, axis=0, keepdims=True)
        d_hat = dxn[...] * gain_ref[...]
        level = jnp.mean(d_hat * x_hat, axis=1, keepdims=True)
        dxn[...] = cot_s[...].astype(wide) + inv * (d_hat - x_hat * level)
        store(len(outs)).start()
        size = gain_grad.shape[1] // 4
        rows, lanes = gain_s.shape[5:]
        gain_s[...] = jnp.zeros_like(gain_s)
        for shard in range(4):
            parts = [gain_grad[:, c : c + lanes] for c in range(shard * size, (shard + 1) * size, lanes)]
            block = jnp.concatenate(parts + [jnp.zeros((rows - len(parts), lanes), wide)], axis=0)
            gain_s[shard % 2, shard // 2, 0, 0, 0] = block.astype(low)

    taken = [[times] for times in SPREAD_TIMES] + [INNER_TIMES, SMALL_TIMES, GAIN_TIMES]
    for i, part_times in enumerate(taken):
        last = max(times[-1] for times in part_times) + 0.001
        events.append((last, functools.partial(lambda i: store(i).start(), i)))
    events += [(time, functools.partial(through_inner, chunk)) for chunk, time in enumerate(DXN_TIMES)]
    events.append((NORM_TIME, through_norm))
    run_events([(0, start)], final)

    rows = rows_ref[...]
    pre = pre_ref[...]
    share = jax.nn.sigmoid(pre)
    d_u = du_ref[...] + dot(ddbc_ref[...], xproj_ref[...])
    d_pre = d_u * share * (1.0 + pre * (1.0 - share))
    inner = inner_ref[...].astype(wide)
    d_inner = block_rows(rows, TAPS - 1, 1) * d_pre
    sums = [None] * 8
    sums[TAPS - 1] = jnp.sum(d_pre * inner, axis=0, keepdims=True)
    sums[BIAS_ROW] = jnp.sum(d_pre, axis=0, keepdims=True)
    for offset in range(1, TAPS):
        same = d_pre * mask_ref[:, offset : offset + 1]
        back = pltpu.roll(same, same.shape[0] - offset, 0)
        sums[TAPS - 1 - offset] = jnp.sum(back * inner, axis=0, keepdims=True)
        d_inner = d_inner + block_rows(rows, TAPS - 1 - offset, 1) * back
    nothing = jnp.zeros_like(sums[0])
    row_s[:, columns] = jnp.concatenate([nothing if v is None else v for v in sums], axis=0)
    xproj_s[:, columns] = rows_product(ddbc_ref[...], u_ref[...])
    d_inner = d_inner.astype(low)
    inner_grad = dot(xnt_ref[...], d_inner).astype(low)
    size = inner_grad.shape[0] // 4
    for shard in range(4):
        own_rows = inner_grad[shard * size : (shard + 1) * size]
        inner_s[shard % 2, shard // 2, :, :, :, :, columns] = own_rows.reshape(2, 2, 2, size // 8, block)
    dinner_s[:, columns] = d_inner

    @pl.when(here == final)
    def _():
        owned = xproj_s.shape[1] // 4
        states = alog_ref.shape[0]
        row = lax.broadcasted_iota(jnp.int32, (8, owned), 0)
        for shard in range(4):
            own = slice(shard * owned, (shard + 1) * owned)
            rows = row_s[:, own]
            for at, extra in ((STEP_ROW, bias_ref[:, own]), (SKIP_ROW, skip_ref[:, own])):
                rows = jnp.where(row == at, extra, rows)
            stacked = [dtproj_ref[:rank, own], alog_ref[:, own], xproj_s[: rank + 2 * states, own], rows]
            height = 8 * small_s.shape[5]
            stacked.append(jnp.zeros((height - sum(v.shape[0] for v in stacked), owned), wide))
            stacked = jnp.concatenate(stacked, axis=0).astype(low)
            small_s[shard % 2, shard // 2] = stacked.reshape(2, 2, 2, height // 8, owned)

    run_events(events, final)

    @pl.when(here == final)
    def _():
        for i in range(len(outs) + 1):
            store(i).wait()
        link.finish()


def tail(
    rank, du, ddbc, xproj_t, u, inner, pre, by_channel, masks, xnt, inner_w, dxn_gate, tokens, cotangent, gain,
    dtproj_grad, alog_grad, bias_grad, skip_grad, pieces, collective_id, block=256,
):
    length, features = tokens.shape
    width = inner_w.shape[1]
    count = len(pieces)
    steps = width // block
    inner_shape = (features // 32, width)
    used = 2 * rank + 3 * alog_grad.shape[0] + 8
    small_shape = ((used + -used % LANES) // 8, width // 4)
    gain_shape = (16, LANES)
    shapes = [*(p.shape for p in pieces), inner_shape, small_shape, gain_shape]
    low, wide = jnp.bfloat16, jnp.float32
    channels = columns_spec(length, block)
    token_grad, *sums = pl.pallas_call(
        functools.partial(tail_kernel, steps, rank, count),
        grid=(steps,),
        in_specs=[
            channels,
            whole_spec(ddbc.shape),
            columns_spec(LANES, block),
            channels,
            channels,
            channels,
            columns_spec(by_channel.shape[0], block),
            whole_spec(masks.shape),
            whole_spec(xnt.shape),
            *[pl.BlockSpec(memory_space=pl.ANY)] * 4,
            whole_spec(gain.shape),
            whole_spec(dtproj_grad.shape),
            whole_spec(alog_grad.shape),
            whole_spec(bias_grad.shape),
            whole_spec(skip_grad.shape),
            *(whole_spec(p.shape) for p in pieces),
        ],
        out_specs=[pl.BlockSpec(memory_space=pl.ANY)] * (count + 4),
        out_shape=[
            jax.ShapeDtypeStruct(tokens.shape, wide),
            *(jax.ShapeDtypeStruct((2, 2, 2) + shape, low) for shape in shapes),
        ],
        scratch_shapes=[
            pltpu.VMEM(inner_w.shape, low),
            pltpu.VMEM(tokens.shape, low),
            pltpu.VMEM(tokens.shape, low),
            pltpu.VMEM(tokens.shape, wide),
            pltpu.VMEM((length, width), low),
            pltpu.VMEM((LANES, width), wide),
            pltpu.VMEM((8, width), wide),
            pltpu.VMEM((2, 2, 2, 2, 2) + inner_shape, low),
            pltpu.VMEM((2, 2, 2, 2, 2) + small_shape, low),
            pltpu.VMEM((2, 2, 2, 2, 2) + gain_shape, low),
            pltpu.SemaphoreType.DMA((4,)),
            pltpu.SemaphoreType.DMA((count + 4,)),
            *Halving.scratch(inner_shape, len(TAIL_ORDERS[2])),
            *Halving.scratch(small_shape, len(TAIL_ORDERS[3])),
            *Halving.scratch(gain_shape, len(TAIL_ORDERS[4])),
            *(v for shape, orders in zip(shapes, TAIL_SPREADS) for v in Spreading.scratch(shape, len(orders))),
        ],
        compiler_params=pltpu.CompilerParams(
            collective_id=collective_id, has_side_effects=True, vmem_limit_bytes=60 << 20
        ),
        name="tail",
    )(
        du, ddbc, xproj_t, u, inner, pre, by_channel, masks, xnt, inner_w, dxn_gate, tokens, cotangent, gain,
        dtproj_grad, alog_grad, bias_grad, skip_grad, *pieces,
    )
    return token_grad, sums


def finish_kernel(
    rank, states, gate_ref, out_ref, inner_ref, small_ref, gain_ref,
    in_grad, out_grad, dtproj_grad, alog_grad, xproj_grad, conv_grad, convb_grad, dtb_grad, skip_grad, gain_grad
):
    wide = jnp.float32
    width = inner_ref.shape[1]
    in_grad[:, :width] = inner_ref[...].astype(wide)
    in_grad[:, width:] = gate_ref[...].astype(wide)
    out_grad[...] = out_ref[...].astype(wide)

    @pl.when(pl.program_id(0) == 0)
    def _():
        small = small_ref[...].astype(wide)
        used = 2 * rank + 3 * states
        dtproj_grad[...] = small[:rank]
        alog_grad[...] = small[rank : rank + states]
        xproj_grad[...] = small[rank + states : rank + states + LANES].T[:, : rank + 2 * states]
        rows = small[used : used + 8]
        conv_grad[...] = rows[:TAPS]
        for ref, row in ((convb_grad, BIAS_ROW), (dtb_grad, STEP_ROW), (skip_grad, SKIP_ROW)):
            ref[...] = rows[row : row + 1]
        for part in range(gain_grad.shape[1] // LANES):
            gain_grad[:, part * LANES : (part + 1) * LANES] = gain_ref[part : part + 1, :].astype(wide)


def finish(rank, states, gate, out, inner, small, gain, features, steps=4):
    wide = jnp.float32
    owned = small.shape[1]
    width = inner.shape[1]
    small_shapes = [(rank, owned), (states, owned), (owned, rank + 2 * states), (TAPS, owned)]
    small_shapes += [(1, owned)] * 3 + [(1, features)]
    in_shape, out_shape = (inner.shape[0], 2 * width), out.shape
    return pl.pallas_call(
        functools.partial(finish_kernel, rank, states),
        grid=(steps,),
        in_specs=[
            rows_spec(gate.shape[0] // steps, width),
            rows_spec(out.shape[0] // steps, out.shape[1]),
            rows_spec(inner.shape[0] // steps, width),
            whole_spec(small.shape),
            whole_spec(gain.shape),
        ],
        out_specs=[
            rows_spec(in_shape[0] // steps, in_shape[1]),
            rows_spec(out_shape[0] // steps, out_shape[1]),
            *(whole_spec(shape) for shape in small_shapes),
        ],
        out_shape=[jax.ShapeDtypeStruct(shape, wide) for shape in (in_shape, out_shape, *small_shapes)],
        compiler_params=pltpu.CompilerParams(vmem_limit_bytes=60 << 20),
        name="finish",
    )(gate, out, inner, small, gain)


def add_groups(sums):
    groups = lax.axis_size("dp") // GROUP
    if groups == 1:
        return sums
    alike = [[g * GROUP + i for g in range(groups)] for i in range(GROUP)]
    return lax.psum(sums, "dp", axis_index_groups=alike)


def body(
    tokens,
    cotangent,
    prot_lens,
    clus_start,
    norm_gain,
    in_w,
    conv_w,
    conv_b,
    xproj_w,
    dtproj_w,
    dt_bias,
    a_log,
    d_skip,
    out_w,
):
    features = norm_gain.shape[0]
    width = in_w.shape[1] // 2
    rank, owned = dtproj_w.shape
    states = a_log.shape[0]
    used = 2 * rank + 3 * states + 8
    inner_w, packed = gather_weights(in_w, dtproj_w, a_log, xproj_w, conv_w, (conv_b, dt_bias, d_skip, norm_gain), 1)
    inner_w = inner_w.reshape(-1, width)
    gain = packed[:, used - 1, :features].reshape(1, -1).astype(jnp.float32)
    packed = jnp.swapaxes(packed, 0, 1).reshape(packed.shape[1], -1)
    dtproj = packed[:LANES]
    decay_rate = -jnp.exp(packed[rank : rank + states].astype(jnp.float32))
    rate2 = decay_rate * LOG2E
    xproj_t = packed[rank + states : rank + states + LANES]
    by_channel = packed[used - 8 : used].astype(jnp.float32)
    inner, pre, u, dbc, xn, xnt, masks = front(prot_lens, clus_start, tokens, gain, inner_w, by_channel, xproj_t)
    y, h, dt, (gate_w, out_full) = scan_forward(
        rank, u, dbc, masks, by_channel, dtproj, rate2, (in_w, out_w), 2
    )
    gate_w = gate_w.reshape(-1, width)
    out_full = out_full.reshape(-1, out_full.shape[2])
    mixed, d_y, _, out_local, gate_local, skip_local, dxn_gate = middle(
        xn, xnt, gate_w, y, u, by_channel, out_full, cotangent, tokens, masks
    )
    in_pieces = lambda v: v.reshape((4, 2, 2, 2, v.shape[0] // 32, v.shape[1]))
    du, ddbc, ldt, dtproj_local, dtb_local, early_pieces = scan_backward(
        rank,
        u,
        dt,
        d_y,
        dbc,
        masks,
        h,
        by_channel,
        dtproj,
        rate2,
        decay_rate.astype(jnp.bfloat16),
        [in_pieces(gate_local), in_pieces(out_local)],
        3,
    )
    token_grad, sums = tail(
        rank,
        du,
        ddbc,
        xproj_t,
        u,
        inner,
        pre,
        by_channel,
        masks,
        xnt,
        inner_w,
        dxn_gate,
        tokens,
        cotangent,
        gain,
        dtproj_local,
        ldt * decay_rate,
        dtb_local,
        skip_local,
        early_pieces,
        4,
    )
    sums = [v.reshape(-1, v.shape[-1]) for v in sums]
    grads = add_groups(finish(rank, states, *sums, features))
    in_grad, out_grad, dtproj_grad, alog_grad, xproj_grad, conv_grad, convb_grad, dtb_grad, skip_grad, gain_grad = grads
    return (
        mixed,
        token_grad,
        gain_grad[0],
        in_grad,
        conv_grad,
        convb_grad[0],
        xproj_grad,
        dtproj_grad,
        dtb_grad[0],
        alog_grad,
        skip_grad[0],
        out_grad,
    )


def solution(mesh):
    in_specs = (
        P(("dp", "fsdp"), None),
        P(("dp", "fsdp"), None),
        P(("dp", "fsdp"), None),
        P(("dp", "fsdp"), None),
        P("fsdp"),
        P("fsdp", None),
        P(None, "fsdp"),
        P("fsdp"),
        P("fsdp", None),
        P(None, "fsdp"),
        P("fsdp"),
        P(None, "fsdp"),
        P("fsdp"),
        P("fsdp", None),
    )
    out_specs = (
        P(("dp", "fsdp"), None),
        P(("dp", "fsdp"), None),
        P("fsdp"),
        P("fsdp", None),
        P(None, "fsdp"),
        P("fsdp"),
        P("fsdp", None),
        P(None, "fsdp"),
        P("fsdp"),
        P(None, "fsdp"),
        P("fsdp"),
        P("fsdp", None),
    )
    return jax.shard_map(body, mesh=mesh, in_specs=in_specs, out_specs=out_specs, check_vma=False)
```
